32 devices in a mesh: seq: 8 (over z, y), rows: 4 (over x, core).
Axes of the slice: x: 2, y: 2, z: 4, core: 2. Of those that a mesh axis runs over, the one named last changes fastest.
Arguments:
- tokens: bfloat16 [64, 1024, 512], P('rows', 'seq'), may hold values from -8 to 8
- cotangent: bfloat16 [64, 1024, 512], P('rows', 'seq'), may hold values from -6 to 6
- reset_pos: int32 [64, 8], P('rows'), may hold values from 0 to 1023, as said below
- norm1_gain: float32 [512], replicated, may hold values from 0.1 to 1.9
- w_in: bfloat16 [512, 3072], replicated, may hold values from -0.25 to 0.25
- forget_bias: float32 [1024], replicated, may hold values from 0.5 to 1.5
- input_bias: float32 [1024], replicated, may hold values from -14 to -3
- w_out: bfloat16 [1024, 512], replicated, may hold values from -0.75 to 0.75
- norm2_gain: float32 [512], replicated, may hold values from 0.1 to 1.9
- w_up: bfloat16 [512, 2048], replicated, may hold values from -0.25 to 0.25
- up_bias: float32 [2048], replicated, may hold values from -3 to 3
- w_down: bfloat16 [2048, 512], replicated, may hold values from -0.125 to 0.125
- down_bias: float32 [512], replicated, may hold values from -3 to 3
Outputs:
- mixed: bfloat16 [64, 1024, 512], P('rows', 'seq')
- grad_tokens: float32 [64, 1024, 512], P('rows', 'seq')
- grad_norm1_gain: float32 [512], replicated
- grad_w_in: float32 [512, 3072], replicated
- grad_forget_bias: float32 [1024], replicated
- grad_input_bias: float32 [1024], replicated
- grad_w_out: float32 [1024, 512], replicated
- grad_norm2_gain: float32 [512], replicated
- grad_w_up: float32 [512, 2048], replicated
- grad_up_bias: float32 [2048], replicated
- grad_w_down: float32 [2048, 512], replicated
- grad_down_bias: float32 [512], replicated
The draws below stay inside these ranges and needn't reach their ends.
Inputs may be any that keep to these rules, and one draw needn't show every extreme that they name: `reset_pos`: 0 marks no start. In each aligned block of 16 rows, one row, drawn from the seed, holds only zeros.
All inputs are finite; a program needn't handle non-finite values.
Results may differ from the reference program's by a relative error of at most 0.0062.
Values sent between devices are 32-bit elements; how exact they have to be, the bound alone decides.
A program may use at most 256 MiB of HBM per device.

```python
import math
import jax
import jax.numpy as jnp
from jax import lax

D = 512
H = 1024
FF = 2048
ROWS_DEV = 16
NRESET = 8
LEN = 1024
ROWS = 64


def draw_reset_pos(key, part):
    key = jax.random.fold_in(key, 7)
    first_key, second_key = jax.random.split(key, 2)
    positions = jax.random.randint(first_key, (ROWS, NRESET), 1, LEN)
    chosen = jax.random.randint(second_key, (ROWS // ROWS_DEV,), 0, ROWS_DEV)
    row_ids = jnp.arange(ROWS)
    whole_rows = chosen[row_ids // ROWS_DEV] == row_ids % ROWS_DEV
    positions = jnp.where(whole_rows[:, None], 0, positions)
    other_row = (chosen[0] + 1) % ROWS_DEV
    positions = positions.at[other_row, 0].set(LEN - 1)
    return positions.astype(jnp.int32)


def draw_tokens(key, part):
    key = jax.random.fold_in(key, 11)
    noise_key, level_key = jax.random.split(key, 2)
    places = jnp.arange(LEN, dtype=jnp.int32)
    segment = places * 8 // LEN
    noise = jnp.clip(jax.random.normal(noise_key, (ROWS, LEN, D), jnp.float32), -4.5, 4.5)
    levels = jnp.clip(0.7 * jax.random.normal(level_key, (ROWS, 8, D), jnp.float32), -2.8, 2.8)
    return (noise + levels[:, segment]).astype(jnp.bfloat16)


def draw_input_bias(key, part):
    key = jax.random.fold_in(key, 13)
    pick_key, rate_key, fast_key = jax.random.split(key, 3)
    share = 0.5
    rate_lo = 0.5
    rate_hi = 2.0
    slow = jax.random.uniform(pick_key, (H,), jnp.float32) < share
    log_rate = jax.random.uniform(rate_key, (H,), jnp.float32, jnp.log(rate_lo), jnp.log(rate_hi))
    slow_bias = log_rate - jnp.log(jnp.float32(LEN)) - 0.8
    fast_bias = jax.random.uniform(fast_key, (H,), jnp.float32, -5.0, -3.0)
    return jnp.where(slow, slow_bias, fast_bias).astype(jnp.float32)


def level_of(key, extent, shards, low, high):
    def one(dim, blocks):
        heights = jax.random.uniform(jax.random.fold_in(jax.random.fold_in(key, 6), dim), (blocks,), jnp.float32, low / len(shards), high / len(shards))
        return jnp.repeat(jnp.exp(heights), extent[dim] // blocks).reshape((-1,) + (1,) * (len(extent) - dim - 1))

    factor_of = one(*shards[0])
    for cut in shards[1:]:
        factor_of = factor_of * one(*cut)
    return factor_of


def centred(rng, extent, deviation, reach, shards=(), kind=jnp.bfloat16):
    values = deviation * jax.random.normal(rng, extent, jnp.float32)
    if shards:
        values = values * level_of(rng, extent, shards, -0.22, 0.18)
    return jnp.clip(values, -reach, reach).astype(kind)


def setup_inputs(seed: int = 0) -> dict:
    arg_keys = jax.random.split(jax.random.key(seed), 14)
    tokens = draw_tokens(jax.random.fold_in(arg_keys[13], 71), 0)
    cotangent = centred(arg_keys[1], (ROWS, LEN, D), 1.0, 6.0, ((0, 4), (1, 8)))
    reset_pos = draw_reset_pos(jax.random.fold_in(arg_keys[13], 71), 0)
    norm1_gain = jnp.clip(1.0 + 0.18 * jax.random.normal(arg_keys[3], (D,), jnp.float32), 0.1, 1.9)
    w_in = centred(arg_keys[4], (D, 3 * H), D ** -0.5, 0.25)
    forget_bias = jnp.clip(jax.random.uniform(arg_keys[5], (H,), jnp.float32, 0.5, 1.5), 0.5, 1.5)
    input_bias = draw_input_bias(jax.random.fold_in(arg_keys[13], 71), 0)
    w_out = centred(arg_keys[7], (H, D), 64 ** -0.5, 0.75)
    norm2_gain = jnp.clip(1.0 + 0.18 * jax.random.normal(arg_keys[8], (D,), jnp.float32), 0.1, 1.9)
    w_up = centred(arg_keys[9], (D, FF), D ** -0.5, 0.25)
    up_bias = centred(arg_keys[10], (FF,), 0.5, 3.0, (), jnp.float32)
    w_down = centred(arg_keys[11], (FF, D), FF ** -0.5, 0.125)
    down_bias = centred(arg_keys[12], (D,), 0.5, 3.0, (), jnp.float32)
    return {"tokens": tokens, "cotangent": cotangent, "reset_pos": reset_pos, "norm1_gain": norm1_gain, "w_in": w_in, "forget_bias": forget_bias, "input_bias": input_bias, "w_out": w_out, "norm2_gain": norm2_gain, "w_up": w_up, "up_bias": up_bias, "w_down": w_down, "down_bias": down_bias}


@jax.custom_vjp
def low(v):
    return lax.optimization_barrier(v.astype(jnp.bfloat16)).astype(jnp.float32)

@jax.custom_vjp
def low_back(v):
    return v

def low_keep(v):
    return (low(v), None)

def low_pass(kept, grad):
    return (grad,)

def back_keep(v):
    return (v, None)

def back_low(kept, grad):
    return (low(grad),)
low.defvjp(low_keep, low_pass)
low_back.defvjp(back_keep, back_low)

def root_norm(values, gain):
    return values * lax.rsqrt(lax.optimization_barrier(jnp.mean(values * values, axis=-1, keepdims=True)) + 1e-06) * gain

def gate_terms(part_forget, part_input, part_cand, bias_forget, bias_input):
    log_forget = -jax.nn.softplus(-(part_forget + bias_forget))
    log_input = -jax.nn.softplus(-(part_input + bias_input))
    log_total = jnp.logaddexp(log_forget, log_input)
    return (jnp.exp(log_forget - log_total), jnp.exp(log_input - log_total) * part_cand)

def matmul(left, right):
    return jnp.dot(left, right, precision=lax.Precision.HIGHEST, preferred_element_type=jnp.float32)

def advance(state, pair):
    decay_now, update_now = pair
    state = decay_now * state + update_now
    return (state, state)

def forward(values, starts, gain_one, weight_in, bias_forget, bias_input, weight_out, gain_two, weight_up, bias_up, weight_down, bias_down):
    hidden = weight_out.shape[0]
    normed = low(root_norm(values, gain_one))
    project = low_back(matmul(normed, weight_in))
    decay_raw, update = gate_terms(project[..., :hidden], project[..., hidden:2 * hidden], project[..., 2 * hidden:], bias_forget, bias_input)
    decay = decay_raw * (1.0 - starts)[..., None]
    first_state = jnp.zeros((values.shape[0], hidden), jnp.float32)
    unused, states = lax.scan(jax.checkpoint(advance), first_state, (jnp.moveaxis(decay, 1, 0), jnp.moveaxis(update, 1, 0)))
    states = jnp.moveaxis(states, 0, 1)
    middle = values + low_back(matmul(low(states), weight_out))
    normed_two = low(root_norm(middle, gain_two))
    up_pre = low_back(matmul(normed_two, weight_up)) + bias_up
    activated = low(jax.nn.gelu(up_pre))
    return middle + matmul(activated, weight_down) + bias_down

def reference(tokens, cotangent, reset_pos, norm1_gain, w_in, forget_bias, input_bias, w_out, norm2_gain, w_up, up_bias, w_down, down_bias):
    group = math.gcd(ROWS, max(1, 4096 // LEN))
    params = tuple((item.astype(jnp.float32) for item in (norm1_gain, w_in, forget_bias, input_bias, w_out, norm2_gain, w_up, up_bias, w_down, down_bias)))
    places = jnp.arange(LEN, dtype=jnp.int32)
    starts = jnp.any(reset_pos[:, :, None] == places[None, None, :], axis=1).astype(jnp.float32)
    values = tokens.astype(jnp.float32).reshape(ROWS // group, group, LEN, D)
    backs = cotangent.astype(jnp.float32).reshape(ROWS // group, group, LEN, D)
    starts = starts.reshape(ROWS // group, group, LEN)
    zeros = tuple((jnp.zeros_like(item) for item in params))

    def one_group(totals, items):
        value_rows, back_rows, start_rows = items

        def apply(inner, *weights):
            return forward(inner, start_rows, *weights)
        result, pull = jax.vjp(apply, value_rows, *params)
        grads = pull(back_rows)
        totals = tuple((left + right for left, right in zip(totals, grads[1:])))
        return (totals, (result.astype(jnp.bfloat16), grads[0]))
    totals, (results, grad_rows) = lax.scan(one_group, zeros, (values, backs, starts))
    return (results.reshape(ROWS, LEN, D), grad_rows.reshape(ROWS, LEN, D), totals[0], totals[1], totals[2], totals[3], totals[4], totals[5], totals[6], totals[7], totals[8], totals[9])
```

```python
import functools
import math

import jax
import jax.numpy as jnp
from jax import lax
from jax.experimental import pallas as pl
from jax.experimental.pallas import tpu as pltpu
from jax.sharding import PartitionSpec as P

MESH = pl.DeviceIdType.MESH
STAGES = 13
KINDS = 14


def place():
    seq = lax.axis_index("seq")
    rows = lax.axis_index("rows")
    return lax.div(rows, 2), lax.rem(seq, 2), lax.div(seq, 2), lax.rem(rows, 2)


def spot(x, y, z, core):
    return (z * 2 + y, x * 2 + core)


def greet(partners):
    barrier = pltpu.get_barrier_semaphore()
    x, y, z, core = place()
    for there in partners:
        pl.semaphore_signal(barrier, inc=1, device_id=there, device_id_type=MESH)

    @pl.when(z > 0)
    def _():
        pl.semaphore_signal(barrier, inc=1, device_id=spot(x, y, z - 1, core), device_id_type=MESH)

    @pl.when(z < 3)
    def _():
        pl.semaphore_signal(barrier, inc=1, device_id=spot(x, y, z + 1, core), device_id_type=MESH)

    pl.semaphore_wait(barrier, len(partners) + jnp.where(z > 0, 1, 0) + jnp.where(z < 3, 1, 0))


class Summing:
    def __init__(self, grads, slots, half_in, part_in, up_in, down_in, last_in, result, send, recv, local):
        self.grads, self.slots = grads, slots
        self.half_in, self.part_in, self.up_in, self.down_in, self.last_in = half_in, part_in, up_in, down_in, last_in
        self.result, self.send, self.recv, self.local = result, send, recv, local
        x, y, z, core = place()
        self.z = z
        first = core == 0
        self.sibling = spot(x, y, z, 1 - core)
        along_x, along_y = spot(1 - x, y, z, core), spot(x, 1 - y, z, core)
        self.near = tuple(jnp.where(first, a, b) for a, b in zip(along_x, along_y))
        self.far = tuple(jnp.where(first, b, a) for a, b in zip(along_x, along_y))
        self.above = spot(x, y, z + 1, core)
        self.below = spot(x, y, z - 1, core)
        near_bit = jnp.where(first, x, y)
        far_bit = jnp.where(first, y, x)
        self.half = core * 256
        self.other_half = (1 - core) * 256
        self.part = self.half + near_bit * 128
        self.other_part = self.half + (1 - near_bit) * 128
        self.far_bit = far_bit

    def copy(self, kind, unit, source, target, device):
        return pltpu.make_async_remote_copy(
            src_ref=source, dst_ref=target, send_sem=self.send.at[kind, unit], recv_sem=self.recv.at[kind, unit],
            device_id=device, device_id_type=MESH,
        )

    def rows(self, unit, start, count):
        return self.grads.at[lax.rem(unit, self.slots), pl.ds(pl.multiple_of(start, 8), count)]

    def done(self, unit, start, count):
        return self.result.at[unit, pl.ds(pl.multiple_of(start, 8), count)]

    def c_half(self, u):
        return self.copy(0, u, self.rows(u, self.other_half, 256), self.half_in.at[lax.rem(u, 2)], self.sibling)

    def c_part(self, u):
        return self.copy(1, u, self.rows(u, self.other_part, 128), self.part_in.at[lax.rem(u, 2)], self.near)

    def c_up(self, u, z):
        lo = 32 * (z + 1)
        return self.copy(2, u, self.rows(u, self.part + lo, 128 - lo), self.up_in.at[lax.rem(u, 4), pl.ds(lo - 32, 128 - lo)], self.above)

    def c_down(self, u, z):
        return self.copy(3, u, self.rows(u, self.part, 32 * z), self.down_in.at[lax.rem(u, 4), pl.ds(0, 32 * z)], self.below)

    def c_last(self, u):
        return self.copy(4, u, self.rows(u, self.part + 32 * self.z + 16 * (1 - self.far_bit), 16), self.last_in.at[u], self.far)

    def c_own(self, u):
        start = self.part + 32 * self.z + 16 * self.far_bit
        return pltpu.make_async_copy(self.rows(u, start, 16), self.done(u, start, 16), self.local.at[u])

    def c_far(self, u):
        start = self.part + 32 * self.z + 16 * self.far_bit
        return self.copy(5, u, self.rows(u, start, 16), self.done(u, start, 16), self.far)

    def c_rise(self, u, hop):
        piece = self.done(u, self.part + 32 * (self.z - hop), 32)
        return self.copy(6 + hop, u, piece, piece, self.above)

    def c_fall(self, u, hop):
        piece = self.done(u, self.part + 32 * (self.z + hop), 32)
        return self.copy(9 + hop, u, piece, piece, self.below)

    def c_near(self, u):
        piece = self.done(u, self.part, 128)
        return self.copy(12, u, piece, piece, self.near)

    def c_sibling(self, u):
        piece = self.done(u, self.half, 256)
        return self.copy(13, u, piece, piece, self.sibling)

    def add(self, u, start, count, ref):
        here = self.rows(u, start, count)
        here[...] = here[...] + ref[...]

    def stage(self, s, u):
        z = self.z
        if s == 0:
            self.c_half(u).start()
        elif s == 1:
            self.c_half(u).wait()
            self.add(u, self.half, 256, self.half_in.at[lax.rem(u, 2)])
            self.c_part(u).start()
        elif s == 2:
            self.c_part(u).wait()
            self.add(u, self.part, 128, self.part_in.at[lax.rem(u, 2)])
        if 2 <= s <= 5:
            for k in range(4):
                if s == 2 + k:
                    @pl.when(z == k)
                    def _():
                        if k > 0:
                            self.c_up(u, k - 1).wait_recv()
                            self.add(u, self.part + 32 * k, 128 - 32 * k, self.up_in.at[lax.rem(u, 4), pl.ds(32 * k - 32, 128 - 32 * k)])
                        if k < 3:
                            self.c_up(u, k).start()
                if s == 5 - k:
                    @pl.when(z == k)
                    def _():
                        if k < 3:
                            self.c_down(u, k + 1).wait_recv()
                            self.add(u, self.part, 32 * k + 32, self.down_in.at[lax.rem(u, 4), pl.ds(0, 32 * k + 32)])
                        if k > 0:
                            self.c_down(u, k).start()
        if s == 5:
            self.c_last(u).start()
        elif s == 6:
            for k in range(4):
                @pl.when(z == k)
                def _():
                    if k < 3:
                        self.c_up(u, k).wait_send()
                    if k > 0:
                        self.c_down(u, k).wait_send()
            self.c_last(u).wait()
            self.add(u, self.part + 32 * z + 16 * self.far_bit, 16, self.last_in.at[u])
            self.c_far(u).start()
            self.c_own(u).start()
        elif s == 7:
            self.c_far(u).wait()
            self.c_own(u).wait()
        if 7 <= s <= 10:
            hop = s - 7
            if hop > 0:
                @pl.when(z >= hop)
                def _():
                    self.c_rise_in(u, hop - 1).wait_recv()

                @pl.when(z + hop < 4)
                def _():
                    self.c_fall_in(u, hop - 1).wait_recv()
            if hop < 3:
                @pl.when((z >= hop) & (z < 3))
                def _():
                    self.c_rise(u, hop).start()

                @pl.when((z + hop < 4) & (z > 0))
                def _():
                    self.c_fall(u, hop).start()
        if s == 10:
            self.c_near(u).start()
        elif s == 11:
            for hop in range(3):
                @pl.when((z >= hop) & (z < 3))
                def _():
                    self.c_rise(u, hop).wait_send()

                @pl.when((z + hop < 4) & (z > 0))
                def _():
                    self.c_fall(u, hop).wait_send()
            self.c_near(u).wait_send()
            self.c_near_in(u).wait_recv()
            self.c_sibling(u).start()
        elif s == 12:
            self.c_sibling(u).wait_send()
            self.c_sibling_in(u).wait_recv()

    def c_rise_in(self, u, hop):
        piece = self.done(u, self.part + 32 * (self.z - 1 - hop), 32)
        return self.copy(6 + hop, u, piece, piece, self.below)

    def c_fall_in(self, u, hop):
        piece = self.done(u, self.part + 32 * (self.z + 1 + hop), 32)
        return self.copy(9 + hop, u, piece, piece, self.above)

    def c_near_in(self, u):
        piece = self.done(u, self.other_part, 128)
        return self.copy(12, u, piece, piece, self.near)

    def c_sibling_in(self, u):
        piece = self.done(u, self.other_half, 256)
        return self.copy(13, u, piece, piece, self.sibling)


def scratch(units, slots, width):
    f32 = jnp.float32
    return [
        pltpu.VMEM((slots, 512, width), f32),
        pltpu.VMEM((2, 256, width), f32),
        pltpu.VMEM((2, 128, width), f32),
        pltpu.VMEM((4, 96, width), f32),
        pltpu.VMEM((4, 96, width), f32),
        pltpu.VMEM((units, 16, width), f32),
        pltpu.SemaphoreType.DMA((KINDS, units)),
        pltpu.SemaphoreType.DMA((KINDS, units)),
        pltpu.SemaphoreType.DMA((units,)),
    ]


def sum_kernel(units, slots, packed, result, grads, half_in, part_in, up_in, down_in, last_in, send, recv, local, load):
    ring = Summing(grads, slots, half_in, part_in, up_in, down_in, last_in, result, send, recv, local)
    greet((ring.sibling, ring.near, ring.far))

    def bring(u):
        return pltpu.make_async_copy(packed.at[u], grads.at[lax.rem(u, slots)], load.at[lax.rem(u, 2)])

    bring(0).start()

    def tick(t, carry):
        @pl.when(t < units)
        def _():
            bring(t).wait()

        @pl.when(t + 1 < units)
        def _():
            bring(t + 1).start()
        for s in reversed(range(STAGES)):
            u = t - s

            @pl.when((u >= 0) & (u < units))
            def _():
                ring.stage(s, u)
        return carry

    lax.fori_loop(0, units + STAGES - 1, tick, 0)


def sum_all(packed, cid=0):
    units, rows, width = packed.shape
    slots = 10
    return pl.pallas_call(
        functools.partial(sum_kernel, units, slots),
        out_shape=jax.ShapeDtypeStruct(packed.shape, jnp.float32),
        in_specs=[pl.BlockSpec(memory_space=pl.ANY)],
        out_specs=pl.BlockSpec(memory_space=pl.ANY),
        scratch_shapes=scratch(units, slots, width) + [pltpu.SemaphoreType.DMA((2,))],
        compiler_params=pltpu.CompilerParams(collective_id=cid, has_side_effects=True, vmem_limit_bytes=56 * 2**20),
        name="sum_all",
    )(packed)


def carried_in(part, axis, combine, identity, reverse):
    count = lax.axis_size(axis)
    place = lax.axis_index(axis)
    ahead = count - 1 - place if reverse else place
    gathered = jax.tree.map(lambda a: lax.all_gather(a, axis), part)
    state = jax.tree.map(lambda a, e: jnp.zeros_like(a) + jnp.asarray(e, a.dtype), part, identity)

    def one(hop, state):
        source = count - 1 - hop if reverse else hop
        return combine(
            state, jax.tree.map(lambda a: lax.dynamic_index_in_dim(a, source, 0, False), gathered)
        )

    return lax.fori_loop(0, ahead, one, state)


def root_norm(values, gain):
    return values * lax.rsqrt(jnp.mean(values * values, axis=-1, keepdims=True) + 1e-06) * gain


def gate_terms(part_forget, part_input, part_cand, bias_forget, bias_input):
    log_forget = -jax.nn.softplus(-(part_forget + bias_forget))
    log_input = -jax.nn.softplus(-(part_input + bias_input))
    log_total = jnp.logaddexp(log_forget, log_input)
    return (jnp.exp(log_forget - log_total), jnp.exp(log_input - log_total) * part_cand)


def affine_join(earlier, later):
    return (earlier[0] * later[0], later[0] * earlier[1] + later[1])


def left_dot(left, right):
    return lax.dot_general(
        left, right, (((0,), (0,)), ((), ())), preferred_element_type=jnp.float32
    )


def right_dot(left, right):
    return lax.dot_general(
        left, right, (((1,), (1,)), ((), ())), preferred_element_type=jnp.float32
    )


def shift_gelu(values, shift):
    return jax.nn.gelu(values + shift)


def on_device(
    tokens,
    cotangent,
    reset_pos,
    norm1_gain,
    w_in,
    forget_bias,
    input_bias,
    w_out,
    norm2_gain,
    w_up,
    up_bias,
    w_down,
    down_bias,
):
    row_count, steps_dev, width = tokens.shape
    hidden = w_out.shape[0]
    total = row_count * steps_dev
    inner = math.gcd(steps_dev, max(1, steps_dev // 16))
    turns = steps_dev // inner
    inputs = tokens.reshape(total, width).astype(jnp.float32)
    places = lax.axis_index("seq") * steps_dev + jnp.arange(steps_dev, dtype=jnp.int32)
    starts = jnp.any(reset_pos[:, :, None] == places[None, None, :], axis=1)
    kept = jnp.where(starts, 0.0, 1.0).astype(jnp.float32)
    kept_time = jnp.transpose(kept)[:, :, None]
    w_forget = w_in[:, :hidden]
    w_input = w_in[:, hidden : 2 * hidden]
    w_cand = w_in[:, 2 * hidden :]
    normed, norm1_pull = jax.vjp(root_norm, inputs, norm1_gain)
    normed_low = normed.astype(jnp.bfloat16)
    part_forget = jnp.dot(normed_low, w_forget, preferred_element_type=jnp.float32)
    part_input = jnp.dot(normed_low, w_input, preferred_element_type=jnp.float32)
    part_cand = jnp.dot(normed_low, w_cand, preferred_element_type=jnp.float32)
    (decay_raw, update), gate_pull = jax.vjp(
        gate_terms, part_forget, part_input, part_cand, forget_bias, input_bias
    )
    decay_time = jnp.moveaxis(decay_raw.reshape(row_count, steps_dev, hidden), 1, 0) * kept_time
    update_time = jnp.moveaxis(update.reshape(row_count, steps_dev, hidden), 1, 0)
    decay_blocks = decay_time.reshape(turns, inner, row_count, hidden)
    update_blocks = update_time.reshape(turns, inner, row_count, hidden)
    ones_rows = jnp.ones((row_count, hidden), jnp.float32)
    zero_rows = jnp.zeros((row_count, hidden), jnp.float32)

    def summary_step(carry, pieces):
        product, running = carry
        decay_piece, update_piece = pieces
        for offset in range(inner):
            running = decay_piece[offset] * running + update_piece[offset]
            product = decay_piece[offset] * product
        return ((product, running), None)

    (local_product, local_end), unused = lax.scan(
        summary_step, (ones_rows, zero_rows), (decay_blocks, update_blocks)
    )
    carried = carried_in(
        (local_product, local_end), "seq", affine_join, (ones_rows, zero_rows), False
    )[1]

    def state_step(running, pieces):
        decay_piece, update_piece = pieces
        states_out = []
        before_out = []
        for offset in range(inner):
            before_out.append(running)
            running = decay_piece[offset] * running + update_piece[offset]
            states_out.append(running)
        return (running, (jnp.stack(states_out), jnp.stack(before_out)))

    unused_end, (state_blocks, before_blocks) = lax.scan(
        state_step, carried, (decay_blocks, update_blocks)
    )
    state_time = state_blocks.reshape(steps_dev, row_count, hidden)
    before_time = before_blocks.reshape(steps_dev, row_count, hidden)
    state_low = jnp.moveaxis(state_time.astype(jnp.bfloat16), 0, 1).reshape(total, hidden)
    middle = inputs + jnp.dot(state_low, w_out, preferred_element_type=jnp.float32)
    normed_two, norm2_pull = jax.vjp(root_norm, middle, norm2_gain)
    normed_two_low = normed_two.astype(jnp.bfloat16)
    up_pre = jnp.dot(normed_two_low, w_up, preferred_element_type=jnp.float32)
    activated, gelu_pull = jax.vjp(shift_gelu, up_pre, up_bias)
    activated_low = activated.astype(jnp.bfloat16)
    result = middle + jnp.dot(activated_low, w_down, preferred_element_type=jnp.float32) + down_bias
    mixed = result.astype(jnp.bfloat16).reshape(row_count, steps_dev, width)
    back_out = cotangent.reshape(total, width)
    grad_down = left_dot(activated_low, back_out)
    grad_down_bias = jnp.sum(back_out.astype(jnp.float32), axis=0)
    back_act = right_dot(back_out, w_down)
    back_up, grad_up_bias = gelu_pull(back_act)
    back_up_low = back_up.astype(jnp.bfloat16)
    grad_up = left_dot(normed_two_low, back_up_low)
    back_norm_two = right_dot(back_up_low, w_up)
    back_mid_norm, grad_norm2 = norm2_pull(back_norm_two)
    back_middle = back_out.astype(jnp.float32) + back_mid_norm
    back_mid_low = back_middle.astype(jnp.bfloat16)
    grad_out = left_dot(state_low, back_mid_low)
    back_state = right_dot(back_mid_low, w_out).reshape(row_count, steps_dev, hidden)
    back_state_blocks = jnp.moveaxis(back_state, 1, 0).reshape(turns, inner, row_count, hidden)

    def back_summary(carry, pieces):
        product, flowing = carry
        decay_piece, back_piece = pieces
        for offset in reversed(range(inner)):
            flowing = decay_piece[offset] * (back_piece[offset] + flowing)
            product = decay_piece[offset] * product
        return ((product, flowing), None)

    (back_product, back_end), unused = lax.scan(
        back_summary, (ones_rows, zero_rows), (decay_blocks, back_state_blocks), reverse=True
    )
    returned = carried_in(
        (back_product, back_end), "seq", affine_join, (ones_rows, zero_rows), True
    )[1]

    def back_step(flowing, pieces):
        decay_piece, back_piece = pieces
        totals_out = [None] * inner
        for offset in reversed(range(inner)):
            total_here = back_piece[offset] + flowing
            totals_out[offset] = total_here
            flowing = decay_piece[offset] * total_here
        return (flowing, jnp.stack(totals_out))

    unused_flow, total_blocks = lax.scan(
        back_step, returned, (decay_blocks, back_state_blocks), reverse=True
    )
    back_total_time = total_blocks.reshape(steps_dev, row_count, hidden)
    back_decay_time = back_total_time * before_time * kept_time
    back_decay = jnp.moveaxis(back_decay_time, 0, 1).reshape(total, hidden)
    back_total = jnp.moveaxis(back_total_time, 0, 1).reshape(total, hidden)
    back_forget, back_input, back_cand, grad_forget, grad_input = gate_pull(
        (back_decay, back_total)
    )
    forget_low = back_forget.astype(jnp.bfloat16)
    input_low = back_input.astype(jnp.bfloat16)
    cand_low = back_cand.astype(jnp.bfloat16)
    grad_in = jnp.concatenate(
        [
            left_dot(normed_low, forget_low),
            left_dot(normed_low, input_low),
            left_dot(normed_low, cand_low),
        ],
        axis=1,
    )
    back_norm_one = (
        right_dot(forget_low, w_forget)
        + right_dot(input_low, w_input)
        + right_dot(cand_low, w_cand)
    )
    back_in_norm, grad_norm1 = norm1_pull(back_norm_one)
    back_inputs = (back_middle + back_in_norm).reshape(row_count, steps_dev, width)
    if lax.axis_size("seq") == 8 and lax.axis_size("rows") == 4:
        pieces = [grad_in[:, 512 * i : 512 * i + 512] for i in range(6)]
        pieces += [grad_out[:512], grad_out[512:]]
        pieces += [grad_up[:, 512 * i : 512 * i + 512] for i in range(4)]
        pieces += [grad_down[512 * i : 512 * i + 512] for i in range(4)]
        summed = sum_all(jnp.stack(pieces))
        grad_in = jnp.concatenate([summed[i] for i in range(6)], axis=1)
        grad_out = summed[6:8].reshape(1024, 512)
        grad_up = jnp.concatenate([summed[8 + i] for i in range(4)], axis=1)
        grad_down = summed[12:16].reshape(2048, 512)
    else:
        grad_in, grad_out, grad_up, grad_down = lax.psum((grad_in, grad_out, grad_up, grad_down), ("seq", "rows"))
    grad_norm1, grad_forget, grad_input, grad_norm2, grad_up_bias, grad_down_bias = lax.psum(
        (grad_norm1, grad_forget, grad_input, grad_norm2, grad_up_bias, grad_down_bias), ("seq", "rows")
    )
    return (
        mixed,
        back_inputs,
        grad_norm1,
        grad_in,
        grad_forget,
        grad_input,
        grad_out,
        grad_norm2,
        grad_up,
        grad_up_bias,
        grad_down,
        grad_down_bias,
    )


def solution(mesh):
    return jax.shard_map(
        on_device,
        mesh=mesh,
        in_specs=(
            P("rows", "seq", None),
            P("rows", "seq", None),
            P("rows", None),
            P(),
            P(),
            P(),
            P(),
            P(),
            P(),
            P(),
            P(),
            P(),
            P(),
        ),
        out_specs=(
            P("rows", "seq", None),
            P("rows", "seq", None),
            P(),
            P(),
            P(),
            P(),
            P(),
            P(),
            P(),
            P(),
            P(),
            P(),
        ),
        check_vma=False,
    )
```

```python
import functools
import math
import jax
import jax.numpy as jnp
from jax import lax
from jax.experimental import pallas as pl
from jax.experimental.pallas import tpu as pltpu
from jax.sharding import PartitionSpec as P

MESH = pl.DeviceIdType.MESH
EPS = 1e-6
F32 = jnp.float32
BF16 = jnp.bfloat16
STAGES = 13
KINDS = 14


def place():
    seq = lax.axis_index("seq")
    rows = lax.axis_index("rows")
    return lax.div(rows, 2), lax.rem(seq, 2), lax.div(seq, 2), lax.rem(rows, 2)


def spot(x, y, z, core):
    return (z * 2 + y, x * 2 + core)


def dot(left, right):
    return jnp.dot(left, right, preferred_element_type=F32)


def dot_nt(left, right):
    return lax.dot_general(left, right, (((1,), (1,)), ((), ())), preferred_element_type=F32)


def dot_tn(left, right):
    return lax.dot_general(left, right, (((0,), (0,)), ((), ())), preferred_element_type=F32)


class Chain:
    def __init__(self, count, sign, sent, got, join, send, recv):
        self.count, self.sign = count, sign
        self.sent, self.got, self.join = sent, got, join
        self.send, self.recv = send, recv
        self.rounds = max(1, math.ceil(math.log2(count)))
        seq = lax.axis_index("seq")
        self.seq = seq
        self.place = seq if sign > 0 else count - 1 - seq

    def partners(self):
        for r in range(self.rounds):
            far = 2**r
            yield self.seq + self.sign * far, self.place + far < self.count
            yield self.seq - self.sign * far, self.place >= far

    def copy(self, part, r, other):
        return pltpu.make_async_remote_copy(
            src_ref=self.sent.at[part, r], dst_ref=self.got.at[part, r],
            send_sem=self.send.at[part, r], recv_sem=self.recv.at[part, r],
            device_id=(other, lax.axis_index("rows")), device_id_type=MESH,
        )

    def push(self, part, r):
        @pl.when(self.place + 2**r < self.count)
        def _():
            self.copy(part, r, self.seq + self.sign * 2**r).start()

    def start(self, part, product, end):
        self.sent[part, 0, 0] = product
        self.sent[part, 0, 1] = end
        self.join[part, 0] = jnp.ones_like(product)
        self.join[part, 1] = jnp.zeros_like(end)
        self.push(part, 0)

    def advance(self, part, r):
        last = r == self.rounds - 1

        @pl.when(self.place >= 2**r)
        def _():
            self.copy(part, r, self.seq - self.sign * 2**r).wait_recv()
            product, end = self.got[part, r, 0], self.got[part, r, 1]
            own = self.join[part, 0]
            self.join[part, 1] = self.join[part, 1] + own * end
            if not last:
                self.join[part, 0] = own * product
                here = self.sent[part, r, 0]
                self.sent[part, r + 1, 0] = here * product
                self.sent[part, r + 1, 1] = self.sent[part, r, 1] + here * end

        if not last:
            @pl.when(self.place < 2**r)
            def _():
                self.sent[part, r + 1] = self.sent[part, r]
            self.push(part, r + 1)

    def finish(self, part):
        for r in range(self.rounds):
            @pl.when(self.place + 2**r < self.count)
            def _():
                self.copy(part, r, self.seq + self.sign * 2**r).wait_send()


def greet_chain(chain):
    barrier = pltpu.get_barrier_semaphore()
    rows = lax.axis_index("rows")
    total = 0
    for other, there in chain.partners():
        @pl.when(there)
        def _():
            pl.semaphore_signal(barrier, inc=1, device_id=(other, rows), device_id_type=MESH)
        total = total + jnp.where(there, 1, 0)
    return barrier, total


def chain_scratch(parts, count, rows, width):
    rounds = max(1, math.ceil(math.log2(count)))
    return [
        pltpu.VMEM((parts, rounds, 2, rows, width), F32),
        pltpu.VMEM((parts, rounds, 2, rows, width), F32),
        pltpu.VMEM((parts, 2, rows, width), F32),
        pltpu.SemaphoreType.DMA((parts, rounds)),
        pltpu.SemaphoreType.DMA((parts, rounds)),
    ]


def front_kernel(
    count, rows, steps, chunk, block,
    tokens, cotangent, reset, gain, w_in, forget_bias, input_bias, w_out,
    x_out, cot_out, middle_out, state_out, decay_out, fade_out, rise_out, weight_out, lean_out,
    tok_v, cot_v, x_v, normed_v, w_v, w_out_v, keep_v, decay_v, update_v, cand_v, fade_v, rise_v, weight_v, lean_v, state_v, middle_v,
    sent, got, join, send, recv, sems, out_sems,
):
    total, width = x_v.shape
    hidden = w_out_v.shape[0]
    parts = hidden // chunk
    size = block * rows
    blocks = steps // block
    chain = Chain(count, 1, sent, got, join, send, recv)
    barrier, greeted = greet_chain(chain)
    loads = [pltpu.make_async_copy(tokens, tok_v, sems.at[0])]
    for j in range(parts):
        for k in range(3):
            loads.append(pltpu.make_async_copy(w_in.at[:, pl.ds(k * hidden + j * chunk, chunk)], w_v.at[j, :, pl.ds(k * chunk, chunk)], sems.at[1 + 3 * j + k]))
    loads.append(pltpu.make_async_copy(cotangent, cot_v, sems.at[1 + 3 * parts]))
    loads.append(pltpu.make_async_copy(w_out, w_out_v, sems.at[2 + 3 * parts]))
    for load in loads:
        load.start()
    loads[0].wait()

    first = lax.axis_index("seq") * steps
    marks = [jnp.broadcast_to(reset[:, k : k + 1], (rows, 128)) for k in range(reset.shape[1])]

    def mark(t, carry):
        hit = marks[0] == first + t
        for one in marks[1:]:
            hit = hit | (one == first + t)
        keep_v[pl.ds(pl.multiple_of(t * rows, rows), rows)] = jnp.where(hit, 0.0, 1.0)
        return carry

    lax.fori_loop(0, steps, mark, 0, unroll=4)
    gains = gain[...]

    def norm(b, carry):
        at = pl.ds(pl.multiple_of(b * size, size), size)
        x = tok_v[:, pl.ds(pl.multiple_of(b * block, block), block), :].astype(F32)
        x = jnp.swapaxes(x, 0, 1).reshape(size, width)
        x_v[at] = x.astype(BF16)
        scale = lax.rsqrt(jnp.mean(x * x, axis=-1, keepdims=True) + EPS)
        normed_v[at] = (x * scale * gains).astype(BF16)
        return carry

    lax.fori_loop(0, blocks, norm, 0)
    outs = [pltpu.make_async_copy(x_v, x_out, out_sems.at[0])]
    outs[0].start()

    def gates(j):
        lanes = pl.ds(j * chunk, chunk)
        shift_f, shift_i = -forget_bias[:, lanes], -input_bias[:, lanes]

        def one(b, carry):
            product, end = carry
            at = pl.ds(pl.multiple_of(b * size, size), size)
            project = dot(normed_v[at], w_v[j])
            neg_f = shift_f - project[:, :chunk]
            neg_i = shift_i - project[:, chunk : 2 * chunk]
            cand = project[:, 2 * chunk :]
            lower = jnp.maximum(jnp.minimum(neg_f, neg_i) - 20.0, 0.0)
            exp_f = jnp.exp(jnp.minimum(neg_f - lower, 80.0))
            exp_i = jnp.exp(jnp.minimum(neg_i - lower, 80.0))
            one_f, one_i = 1.0 + exp_f, 1.0 + exp_i
            share = 1.0 / (one_f + one_i)
            decay, weight = one_i * share, one_f * share
            fade_v[j % 2, at] = (decay * (exp_f * share)).astype(BF16)
            rise_v[j % 2, at] = (weight * (exp_i * share)).astype(BF16)
            weight_v[j % 2, at] = weight.astype(BF16)
            cand_v[at, lanes] = cand
            update = weight * cand
            update_v[at, lanes] = update
            keep = jnp.concatenate([keep_v[at]] * (chunk // 128), axis=1)
            decay = decay * keep
            decay_v[at, lanes] = decay
            for t in range(block):
                here = decay[t * rows : (t + 1) * rows]
                end = here * end + update[t * rows : (t + 1) * rows]
                product = here * product
            return product, end

        start = (jnp.ones((rows, chunk), F32), jnp.zeros((rows, chunk), F32))
        return lax.fori_loop(0, blocks, one, start)

    def scan(j):
        lanes = pl.ds(j * chunk, chunk)

        def one(b, state):
            at = pl.ds(pl.multiple_of(b * size, size), size)
            states = []
            for t in range(block):
                here = pl.ds(pl.multiple_of(b * size + t * rows, rows), rows)
                keep = jnp.concatenate([keep_v[here]] * (chunk // 128), axis=1)
                lean_v[j % 2, here] = (keep * state - cand_v[here, lanes]).astype(BF16)
                state = decay_v[here, lanes] * state + update_v[here, lanes]
                states.append(state.astype(BF16))
            low = jnp.concatenate(states, axis=0)
            state_v[at, lanes] = low
            add = dot(low, w_out_v[lanes])
            if j == 0:
                middle_v[at] = x_v[at].astype(F32) + add
            else:
                middle_v[at] = middle_v[at] + add
            return state

        lax.fori_loop(0, blocks, one, join[j, 1])

    def put(source, target, slot, wait=False):
        copy = pltpu.make_async_copy(source, target, out_sems.at[slot])
        if wait:
            copy.wait()
        else:
            copy.start()

    def gate_outs(j, wait=False):
        lanes = pl.ds(j * chunk, chunk)
        for k, (a, b) in enumerate(((fade_v, fade_out), (rise_v, rise_out), (weight_v, weight_out))):
            put(a.at[j % 2], b.at[:, lanes], 1 + 3 * j + k, wait)
        put(decay_v.at[:, lanes], decay_out.at[:, lanes], 1 + 3 * parts + j, wait)

    def scan_outs(j, wait=False):
        lanes = pl.ds(j * chunk, chunk)
        put(lean_v.at[j % 2], lean_out.at[:, lanes], 1 + 4 * parts + 2 * j, wait)
        put(state_v.at[:, lanes], state_out.at[:, lanes], 2 + 4 * parts + 2 * j, wait)

    ready = 0
    for j in range(parts):
        for k in range(3):
            loads[1 + 3 * j + k].wait()
        if j >= 2:
            gate_outs(j - 2, True)
        product, end = gates(j)
        gate_outs(j)
        if j == 0:
            pl.semaphore_wait(barrier, greeted)
        chain.start(j, product, end)
        for i in range(j - 1, -1, -1):
            if j - 1 - i < chain.rounds:
                chain.advance(i, j - 1 - i)
    for k in range(2):
        loads[1 + 3 * parts + k].wait()

    def turn(b, carry):
        at = pl.ds(pl.multiple_of(b * size, size), size)
        c = cot_v[:, pl.ds(pl.multiple_of(b * block, block), block), :].astype(F32)
        normed_v[at] = jnp.swapaxes(c, 0, 1).reshape(size, width).astype(BF16)
        return carry

    lax.fori_loop(0, blocks, turn, 0)
    put(normed_v, cot_out, 1 + 6 * parts)

    step = parts - 1
    while ready < parts:
        for i in range(parts - 1, -1, -1):
            if 0 <= step - 1 - i < chain.rounds and step >= parts:
                chain.advance(i, step - 1 - i)
        while ready < parts and ready + chain.rounds <= step:
            if ready >= 2:
                scan_outs(ready - 2, True)
            scan(ready)
            scan_outs(ready)
            ready += 1
        step += 1
    put(middle_v, middle_out, 2 + 6 * parts)
    for j in range(parts):
        if j >= parts - 2:
            gate_outs(j, True)
            scan_outs(j, True)
        chain.finish(j)
    outs[0].wait()
    put(normed_v, cot_out, 1 + 6 * parts, True)
    put(middle_v, middle_out, 2 + 6 * parts, True)


def front(tokens, cotangent, reset, gain, w_in, forget_bias, input_bias, w_out, cid=1):
    rows, steps, width = tokens.shape
    hidden = w_out.shape[0]
    total = rows * steps
    count = lax.axis_size("seq")
    chunk, block = 256, 16
    parts = hidden // chunk
    anywhere = pl.BlockSpec(memory_space=pl.ANY)
    vmem = pl.BlockSpec(memory_space=pltpu.VMEM)
    shape = jax.ShapeDtypeStruct
    return pl.pallas_call(
        functools.partial(front_kernel, count, rows, steps, chunk, block),
        out_shape=(
            shape((total, width), BF16), shape((total, width), BF16), shape((total, width), F32),
            shape((total, hidden), BF16), shape((total, hidden), F32), shape((total, hidden), BF16),
            shape((total, hidden), BF16), shape((total, hidden), BF16), shape((total, hidden), BF16),
        ),
        in_specs=[anywhere, anywhere, vmem, vmem, anywhere, vmem, vmem, anywhere],
        out_specs=(anywhere,) * 9,
        scratch_shapes=[
            pltpu.VMEM(tokens.shape, BF16), pltpu.VMEM(tokens.shape, BF16), pltpu.VMEM((total, width), BF16), pltpu.VMEM((total, width), BF16),
            pltpu.VMEM((parts, width, 3 * chunk), BF16), pltpu.VMEM(w_out.shape, BF16), pltpu.VMEM((total, 128), F32),
            pltpu.VMEM((total, hidden), F32), pltpu.VMEM((total, hidden), F32), pltpu.VMEM((total, hidden), F32),
            pltpu.VMEM((2, total, chunk), BF16), pltpu.VMEM((2, total, chunk), BF16), pltpu.VMEM((2, total, chunk), BF16),
            pltpu.VMEM((2, total, chunk), BF16), pltpu.VMEM((total, hidden), BF16), pltpu.VMEM((total, width), F32),
            *chain_scratch(parts, count, rows, chunk),
            pltpu.SemaphoreType.DMA((3 + 3 * parts,)), pltpu.SemaphoreType.DMA((3 + 6 * parts,)),
        ],
        compiler_params=pltpu.CompilerParams(collective_id=cid, has_side_effects=True, vmem_limit_bytes=62 * 2**20),
        cost_estimate=pl.CostEstimate(flops=2 * total * width * 4 * hidden, bytes_accessed=40 * 2**20, transcendentals=3 * total * hidden),
        name="front",
    )(tokens, cotangent, reset, gain.reshape(1, -1), w_in, forget_bias.reshape(1, -1), input_bias.reshape(1, -1), w_out)


class Summing:
    def __init__(self, span, grads, slots, half_in, part_in, up_in, down_in, last_in, result, send, recv, local):
        self.grads, self.slots = grads, slots
        self.half_in, self.part_in, self.up_in, self.down_in, self.last_in = half_in, part_in, up_in, down_in, last_in
        self.result, self.send, self.recv, self.local = result, send, recv, local
        x, y, z, core = place()
        self.z = z
        first = core == 0
        self.sibling = spot(x, y, z, 1 - core)
        along_x, along_y = spot(1 - x, y, z, core), spot(x, 1 - y, z, core)
        self.near = tuple(jnp.where(first, a, b) for a, b in zip(along_x, along_y))
        self.far = tuple(jnp.where(first, b, a) for a, b in zip(along_x, along_y))
        self.above = spot(x, y, z + 1, core)
        self.below = spot(x, y, z - 1, core)
        near_bit = jnp.where(first, x, y)
        far_bit = jnp.where(first, y, x)
        self.n_half, self.n_part, self.n_line, self.n_tip = span // 2, span // 4, span // 16, span // 32
        self.half = core * self.n_half
        self.other_half = (1 - core) * self.n_half
        self.part = self.half + near_bit * self.n_part
        self.other_part = self.half + (1 - near_bit) * self.n_part
        self.tip = self.part + self.n_line * z + self.n_tip * far_bit
        self.other_tip = self.part + self.n_line * z + self.n_tip * (1 - far_bit)

    def copy(self, kind, unit, source, target, device):
        return pltpu.make_async_remote_copy(
            src_ref=source, dst_ref=target, send_sem=self.send.at[kind, unit], recv_sem=self.recv.at[kind, unit],
            device_id=device, device_id_type=MESH,
        )

    def rows(self, unit, start, count):
        return self.grads.at[lax.rem(unit, self.slots), pl.ds(pl.multiple_of(start, 8), count)]

    def done(self, unit, start, count):
        return self.result.at[unit, pl.ds(pl.multiple_of(start, 8), count)]

    def c_half(self, u):
        return self.copy(0, u, self.rows(u, self.other_half, self.n_half), self.half_in.at[lax.rem(u, 2)], self.sibling)

    def c_part(self, u):
        return self.copy(1, u, self.rows(u, self.other_part, self.n_part), self.part_in.at[lax.rem(u, 2)], self.near)

    def c_up(self, u, z):
        low, rest = self.n_line * (z + 1), self.n_line * (3 - z)
        return self.copy(2, u, self.rows(u, self.part + low, rest), self.up_in.at[lax.rem(u, 4), pl.ds(low - self.n_line, rest)], self.above)

    def c_down(self, u, z):
        rest = self.n_line * z
        return self.copy(3, u, self.rows(u, self.part, rest), self.down_in.at[lax.rem(u, 4), pl.ds(0, rest)], self.below)

    def c_last(self, u):
        return self.copy(4, u, self.rows(u, self.other_tip, self.n_tip), self.last_in.at[u], self.far)

    def c_own(self, u):
        return pltpu.make_async_copy(self.rows(u, self.tip, self.n_tip), self.done(u, self.tip, self.n_tip), self.local.at[u])

    def c_far(self, u):
        return self.copy(5, u, self.rows(u, self.tip, self.n_tip), self.done(u, self.tip, self.n_tip), self.far)

    def c_rise(self, u, hop, back=0):
        piece = self.done(u, self.part + self.n_line * (self.z - hop - back), self.n_line)
        return self.copy(6 + hop, u, piece, piece, self.above)

    def c_fall(self, u, hop, back=0):
        piece = self.done(u, self.part + self.n_line * (self.z + hop + back), self.n_line)
        return self.copy(9 + hop, u, piece, piece, self.below)

    def c_near(self, u, start):
        piece = self.done(u, start, self.n_part)
        return self.copy(12, u, piece, piece, self.near)

    def c_sibling(self, u, start):
        piece = self.done(u, start, self.n_half)
        return self.copy(13, u, piece, piece, self.sibling)

    def add(self, u, start, count, ref):
        slot = lax.rem(u, self.slots)
        step = math.gcd(count, 32)

        def one(i, carry):
            here = pl.ds(pl.multiple_of(start + i * step, 8), step)
            there = pl.ds(pl.multiple_of(i * step, 8), step)
            self.grads[slot, here] = self.grads[slot, here] + ref[there]
            return carry

        if count == step:
            one(0, 0)
        else:
            lax.fori_loop(0, count // step, one, 0)

    def stage(self, s, u):
        z = self.z
        if s == 0:
            self.c_half(u).start()
        elif s == 1:
            self.c_half(u).wait()
            self.add(u, self.half, self.n_half, self.half_in.at[lax.rem(u, 2)])
            self.c_part(u).start()
        elif s == 2:
            self.c_part(u).wait()
            self.add(u, self.part, self.n_part, self.part_in.at[lax.rem(u, 2)])
        if 2 <= s <= 5:
            for k in range(4):
                if s == 2 + k:
                    @pl.when(z == k)
                    def _():
                        if k > 0:
                            self.c_up(u, k - 1).wait_recv()
                            low, rest = self.n_line * k, self.n_line * (4 - k)
                            self.add(u, self.part + low, rest, self.up_in.at[lax.rem(u, 4), pl.ds(low - self.n_line, rest)])
                        if k < 3:
                            self.c_up(u, k).start()
                if s == 5 - k:
                    @pl.when(z == k)
                    def _():
                        if k < 3:
                            self.c_down(u, k + 1).wait_recv()
                            rest = self.n_line * (k + 1)
                            self.add(u, self.part, rest, self.down_in.at[lax.rem(u, 4), pl.ds(0, rest)])
                        if k > 0:
                            self.c_down(u, k).start()
        if s == 5:
            self.c_last(u).start()
        elif s == 6:
            for k in range(4):
                @pl.when(z == k)
                def _():
                    if k < 3:
                        self.c_up(u, k).wait_send()
                    if k > 0:
                        self.c_down(u, k).wait_send()
            self.c_last(u).wait()
            self.add(u, self.tip, self.n_tip, self.last_in.at[u])
            self.c_far(u).start()
            self.c_own(u).start()
        elif s == 7:
            self.c_far(u).wait()
            self.c_own(u).wait()
        if 7 <= s <= 10:
            hop = s - 7
            if hop > 0:
                @pl.when(z >= hop)
                def _():
                    self.c_rise(u, hop - 1, 1).wait_recv()

                @pl.when(z + hop < 4)
                def _():
                    self.c_fall(u, hop - 1, 1).wait_recv()
            if hop < 3:
                @pl.when((z >= hop) & (z < 3))
                def _():
                    self.c_rise(u, hop).start()

                @pl.when((z + hop < 4) & (z > 0))
                def _():
                    self.c_fall(u, hop).start()
        if s == 10:
            self.c_near(u, self.part).start()
        elif s == 11:
            for hop in range(3):
                @pl.when((z >= hop) & (z < 3))
                def _():
                    self.c_rise(u, hop).wait_send()

                @pl.when((z + hop < 4) & (z > 0))
                def _():
                    self.c_fall(u, hop).wait_send()
            self.c_near(u, self.part).wait_send()
            self.c_near(u, self.other_part).wait_recv()
            self.c_sibling(u, self.half).start()
        elif s == 12:
            self.c_sibling(u, self.half).wait_send()
            self.c_sibling(u, self.other_half).wait_recv()


def sum_scratch(units, slots, span, width):
    return [
        pltpu.VMEM((slots, span, width), F32),
        pltpu.VMEM((2, span // 2, width), F32),
        pltpu.VMEM((2, span // 4, width), F32),
        pltpu.VMEM((4, 3 * span // 16, width), F32),
        pltpu.VMEM((4, 3 * span // 16, width), F32),
        pltpu.VMEM((units, span // 32, width), F32),
        pltpu.SemaphoreType.DMA((KINDS, units)),
        pltpu.SemaphoreType.DMA((KINDS, units)),
        pltpu.SemaphoreType.DMA((units,)),
    ]


def greet_ring(ring):
    barrier = pltpu.get_barrier_semaphore()
    for there in (ring.sibling, ring.near, ring.far):
        pl.semaphore_signal(barrier, inc=1, device_id=there, device_id_type=MESH)

    @pl.when(ring.z > 0)
    def _():
        pl.semaphore_signal(barrier, inc=1, device_id=ring.below, device_id_type=MESH)

    @pl.when(ring.z < 3)
    def _():
        pl.semaphore_signal(barrier, inc=1, device_id=ring.above, device_id_type=MESH)

    return 3 + jnp.where(ring.z > 0, 1, 0) + jnp.where(ring.z < 3, 1, 0)


GELU_A = math.sqrt(2.0 / math.pi)
GELU_B = GELU_A * 0.044715
UNIT = 512
SMALL_ROWS = 256


def back_kernel(
    ringed, count, rows, steps, units, slots, holes, block,
    x_in, cot_in, middle_in, state_in, decay_in, fade_in, rise_in, weight_in, lean_in,
    gain_one, gain_two, up_bias, down_bias, w_in, w_out, w_up, w_down,
    mixed_out, tokens_out, result, small_out,
    middle_v, second_v, mixed_v, flow_v, state_v, cot_v, x_v, low_v, turned_v, w_in_v, w_out_v, w_up_v, w_down_v,
    decay_s, fade_s, rise_s, weight_s, lean_s, mixed_s, tokens_s, sums_v,
    load_sems, stream_sems, stage_sems,
    sent, got, join, send, recv,
    *ring_refs,
):
    total, width = x_v.shape
    hidden = w_out_v.shape[0]
    inner = w_down_v.shape[0]
    size = block * rows
    blocks = steps // block
    wide = UNIT
    halves = hidden // wide
    big = 512
    chain = Chain(count, -1, sent, got, join, send, recv)
    barrier, greeted = greet_chain(chain)
    grads = ring_refs[0]
    if ringed:
        ring = Summing(UNIT, grads, slots, *ring_refs[1:6], result, *ring_refs[6:9])
        small = Summing(SMALL_ROWS, ring_refs[9], 1, *ring_refs[10:15], small_out, *ring_refs[15:18])
        greeted = greeted + greet_ring(ring)
        small_v = ring_refs[9].at[0]
    else:
        small_v = ring_refs[1].at[0]

    loads = [
        pltpu.make_async_copy(source, target, load_sems.at[k])
        for k, (source, target) in enumerate((
            (middle_in, middle_v), (w_up, w_up_v), (cot_in, cot_v), (w_down, w_down_v), (state_in, state_v),
            (w_out, w_out_v), (w_in, w_in_v), (x_in, x_v),
        ))
    ]
    for load in loads:
        load.start()

    def at_block(b, n=size):
        return pl.ds(pl.multiple_of(b * n, n), n)

    def stage_at(t, s):
        v = t - s
        if isinstance(v, int):
            u = v - sum(hole < v for hole in holes)
            if 0 <= v and v not in holes and u <= units:
                ring.stage(s, u) if u < units else small.stage(s, 0)
            return
        u, real = v, v >= 0
        for hole in holes:
            u = u - jnp.where(v > hole, 1, 0)
            real = real & (v != hole)

        @pl.when(real & (u < units))
        def _():
            ring.stage(s, u)

        @pl.when(real & (u == units))
        def _():
            small.stage(s, 0)

    def tick(t):
        if ringed:
            for s in reversed(range(STAGES)):
                stage_at(t, s)

    def put_units(first, number):
        if not ringed:
            for k in range(number):
                copy = pltpu.make_async_copy(grads.at[lax.rem(first + k, slots)], result.at[first + k], load_sems.at[0])
                copy.start()
                copy.wait()

    sums_v[...] = jnp.zeros_like(sums_v)
    small_v[...] = jnp.zeros_like(small_v)

    def put_small(row, value):
        for k in range(value.shape[1] // 128):
            small_v[pl.ds(row + k, 1)] = value[:, 128 * k : 128 * k + 128]

    loads[0].wait()
    gains = gain_two[...]
    bias = down_bias[...]

    def norm_two(b, carry):
        at = at_block(b)
        value = middle_v[at]
        scale = lax.rsqrt(jnp.mean(value * value, axis=-1, keepdims=True) + EPS)
        normed = value * scale * gains
        low_v[at] = normed.astype(BF16)
        turned_v[:, at] = jnp.swapaxes(normed, 0, 1).astype(BF16)
        mixed_v[at] = value + bias
        second_v[at] = jnp.zeros_like(value)
        return carry

    lax.fori_loop(0, blocks, norm_two, 0)
    for k in (1, 2, 3):
        loads[k].wait()
    pl.semaphore_wait(barrier, greeted)

    def feed(f, tok):
        at = at_block(tok, big)
        lanes = pl.ds(pl.multiple_of(f * UNIT, UNIT), UNIT)
        cot = cot_v[at]
        pre = dot(low_v[at], w_up_v[:, lanes]) + up_bias[:, lanes]
        back_act = dot_nt(cot, w_down_v[lanes])
        square = pre * pre
        gate = 0.5 * jnp.tanh(pre * (GELU_A + GELU_B * square)) + 0.5
        act = pre * gate
        slope = gate + act * (1.0 - gate) * (2.0 * GELU_A + 6.0 * GELU_B * square)
        back_up = back_act * slope
        sums_v[0:1, lanes] = sums_v[0:1, lanes] + jnp.sum(back_up, axis=0, keepdims=True)
        act, back_up = act.astype(BF16), back_up.astype(BF16)
        mixed_v[at] = mixed_v[at] + dot(act, w_down_v[lanes])
        second_v[at] = second_v[at] + dot_nt(back_up, w_up_v[:, lanes])
        slot = lax.rem(2 * f, slots)
        down = dot_tn(act, cot)
        up = dot(turned_v[:, at], back_up)

        @pl.when(tok == 0)
        def _():
            grads[slot] = down
            grads[slot + 1] = up

        @pl.when(tok > 0)
        def _():
            grads[slot] = grads[slot] + down
            grads[slot + 1] = grads[slot + 1] + up

    per = total // big
    turns = inner // UNIT

    def feed_one(f, carry):
        for half in range(2):
            def one(tok, inner_carry):
                feed(f, tok)
                return inner_carry

            lax.fori_loop(half * per // 2, (half + 1) * per // 2, one, 0)
            if half == 1:
                put_units(2 * f, 2)
            tick(2 * f - 1 + half)
        return carry

    lax.fori_loop(0, turns, feed_one, 0)

    def stage_copy(buffer, target, b):
        slot = lax.rem(b, 2)
        return pltpu.make_async_copy(buffer.at[slot], target.at[:, pl.ds(pl.multiple_of(b * block, block), block), :], stage_sems.at[slot])

    def finish_two(b, carry):
        norm_sum, cot_sum = carry
        at = at_block(b)

        @pl.when(b >= 2)
        def _():
            stage_copy(mixed_s, mixed_out, b - 2).wait()
        mixed = jnp.swapaxes(mixed_v[at].reshape(block, rows, width), 0, 1)
        mixed_s[lax.rem(b, 2)] = mixed.astype(BF16)
        stage_copy(mixed_s, mixed_out, b).start()
        value, grad, cot = middle_v[at], second_v[at], cot_v[at].astype(F32)
        scale = lax.rsqrt(jnp.mean(value * value, axis=-1, keepdims=True) + EPS)
        plain = value * scale
        norm_sum = norm_sum + jnp.sum((grad * plain).reshape(size // 8, 8, width), axis=0)
        cot_sum = cot_sum + jnp.sum(cot.reshape(size // 8, 8, width), axis=0)
        lean = grad * gains
        back = cot + scale * (lean - plain * jnp.mean(lean * plain, axis=-1, keepdims=True))
        second_v[at] = back
        low_v[at] = back.astype(BF16)
        return norm_sum, cot_sum

    zero = jnp.zeros((8, width), F32)
    norm_sum, cot_sum = lax.fori_loop(0, blocks, finish_two, (zero, zero))
    for b in (blocks - 2, blocks - 1):
        stage_copy(mixed_s, mixed_out, b).wait()
    put_small(20, jnp.sum(norm_sum, axis=0, keepdims=True))
    put_small(24, sums_v[0:1])
    put_small(40, jnp.sum(cot_sum, axis=0, keepdims=True))
    tick(2 * turns - 1)

    loads[4].wait()
    loads[5].wait()

    def stream(buffer, source, j, b, k):
        slot = lax.rem(b, 2)
        lanes = pl.ds(j * wide, wide)
        return pltpu.make_async_copy(source.at[at_block(b), lanes], buffer.at[slot], stream_sems.at[k, slot])

    flows = [mixed_v, flow_v]

    def first_pass(j):
        stream(decay_s, decay_in, j, blocks - 1, 0).start()

        def one(i, carry):
            product, flow = carry
            b = blocks - 1 - i
            at = at_block(b)

            @pl.when(b > 0)
            def _():
                stream(decay_s, decay_in, j, b - 1, 0).start()
            back = dot_nt(low_v[at], w_out_v[pl.ds(j * wide, wide)])
            flows[j][at] = back
            stream(decay_s, decay_in, j, b, 0).wait()
            slot = lax.rem(b, 2)
            for t in reversed(range(block)):
                here = slice(t * rows, (t + 1) * rows)
                decay = decay_s[slot, here]
                flow = decay * (back[here] + flow)
                product = decay * product
            return product, flow

        product, flow = lax.fori_loop(0, blocks, one, (jnp.ones((rows, wide), F32), jnp.zeros((rows, wide), F32)))
        chain.start(j, product, flow)

    def grad_out(j):
        slot = (2 * turns + j) % slots

        def one(tok, carry):
            at = at_block(tok, big)
            part = dot_tn(state_v[at, pl.ds(j * UNIT, UNIT)], low_v[at])

            @pl.when(tok == 0)
            def _():
                grads[slot] = part

            @pl.when(tok > 0)
            def _():
                grads[slot] = grads[slot] + part
            return carry

        lax.fori_loop(0, per, one, 0)
        put_units(2 * turns + j, 1)

    now = 2 * turns
    for j in range(halves):
        first_pass(j)
        grad_out(j)
        for i in range(j):
            if j - 1 - i < chain.rounds:
                chain.advance(i, j - 1 - i)
        tick(now)
        now += 1

    loads[7].wait()
    gains_one = gain_one[...]

    def norm_one(b, carry):
        at = at_block(b)
        value = x_v[at].astype(F32)
        scale = lax.rsqrt(jnp.mean(value * value, axis=-1, keepdims=True) + EPS)
        turned_v[:, at] = jnp.swapaxes(value * scale * gains_one, 0, 1).astype(BF16)
        middle_v[at] = jnp.zeros_like(value)
        return carry

    streams = ((decay_s, decay_in), (fade_s, fade_in), (rise_s, rise_in), (weight_s, weight_in), (lean_s, lean_in))
    backs = [lambda at: (state_v, (at, slice(0, UNIT))), lambda at: (state_v, (at, slice(UNIT, 2 * UNIT))), lambda at: (cot_v, (at, slice(None)))]

    def second_pass(j):
        for k, (buffer, source) in enumerate(streams):
            stream(buffer, source, j, blocks - 1, k).start()

        def one(i, carry):
            flow, sum_f, sum_i = carry
            b = blocks - 1 - i
            at = at_block(b)
            slot = lax.rem(b, 2)

            @pl.when(b > 0)
            def _():
                for k, (buffer, source) in enumerate(streams):
                    stream(buffer, source, j, b - 1, k).start()
            for k, (buffer, source) in enumerate(streams):
                stream(buffer, source, j, b, k).wait()
            parts = []
            for t in reversed(range(block)):
                here = slice(t * rows, (t + 1) * rows)
                there = pl.ds(pl.multiple_of(b * size + t * rows, rows), rows)
                reach = flows[j][there] + flow
                flow = decay_s[slot, here] * reach
                lean = reach * lean_s[slot, here].astype(F32)
                grad_f = fade_s[slot, here].astype(F32) * lean
                grad_i = -(rise_s[slot, here].astype(F32) * lean)
                sum_f, sum_i = sum_f + grad_f, sum_i + grad_i
                state_v[there, 0:UNIT] = grad_f.astype(BF16)
                state_v[there, UNIT : 2 * UNIT] = grad_i.astype(BF16)
                cot_v[there] = (weight_s[slot, here].astype(F32) * reach).astype(BF16)
            return flow, sum_f, sum_i

        none = jnp.zeros((rows, wide), F32)
        unused, sum_f, sum_i = lax.fori_loop(0, blocks, one, (join[j, 1], none, none))
        put_small(4 + 4 * j, jnp.sum(sum_f, axis=0, keepdims=True))
        put_small(12 + 4 * j, jnp.sum(sum_i, axis=0, keepdims=True))

    def project(j, k, base):
        slot = (base + k) % slots

        def one(tok, carry):
            at = at_block(tok, big)
            ref, index = backs[k](at)
            piece = ref[index]
            part = dot(turned_v[:, at], piece)
            columns = pl.ds(k * hidden + j * wide, wide)
            middle_v[at] = middle_v[at] + dot_nt(piece, w_in_v[:, columns])

            @pl.when(tok == 0)
            def _():
                grads[slot] = part

            @pl.when(tok > 0)
            def _():
                grads[slot] = grads[slot] + part
            return carry

        lax.fori_loop(0, per, one, 0)
        put_units(base + k, 1)

    base = 2 * turns + halves
    lax.fori_loop(0, blocks, norm_one, 0)
    for step in range(halves, halves + chain.rounds):
        for i in range(halves):
            if 0 <= step - 1 - i < chain.rounds:
                chain.advance(i, step - 1 - i)
    tick(now)
    now += 1
    loads[6].wait()
    for j in range(halves):
        second_pass(j)
        tick(now)
        now += 1
        for k in range(3):
            project(j, k, base + 3 * j)
            if k < 2 or j == 0:
                tick(now)
                now += 1

    def finish_one(b, norm_sum):
        at = at_block(b)

        @pl.when(b >= 2)
        def _():
            stage_copy(tokens_s, tokens_out, b - 2).wait()
        value, grad = x_v[at].astype(F32), middle_v[at]
        scale = lax.rsqrt(jnp.mean(value * value, axis=-1, keepdims=True) + EPS)
        plain = value * scale
        norm_sum = norm_sum + jnp.sum((grad * plain).reshape(size // 8, 8, width), axis=0)
        lean = grad * gains_one
        back = second_v[at] + scale * (lean - plain * jnp.mean(lean * plain, axis=-1, keepdims=True))
        tokens_s[lax.rem(b, 2)] = jnp.swapaxes(back.reshape(block, rows, width), 0, 1)
        stage_copy(tokens_s, tokens_out, b).start()
        return norm_sum

    norm_sum = lax.fori_loop(0, blocks, finish_one, jnp.zeros((8, width), F32))
    put_small(0, jnp.sum(norm_sum, axis=0, keepdims=True))
    if ringed:
        def drain(t, carry):
            tick(t)
            return carry

        lax.fori_loop(now, units + len(holes) + STAGES, drain, 0)
    else:
        copy = pltpu.make_async_copy(small_v, small_out.at[0], load_sems.at[0])
        copy.start()
        copy.wait()
    for b in (blocks - 2, blocks - 1):
        stage_copy(tokens_s, tokens_out, b).wait()
    for j in range(halves):
        chain.finish(j)


def back(ringed, shape_in, x, cot, middle, state, decay, fade, rise, weight, lean, gain_one, gain_two, up_bias, down_bias, w_in, w_out, w_up, w_down, cid=2):
    rows, steps, width = shape_in
    total = rows * steps
    hidden = w_out.shape[0]
    inner = w_down.shape[0]
    count = lax.axis_size("seq")
    block = 16
    size = block * rows
    wide = UNIT
    halves = hidden // wide
    units = 2 * (inner // UNIT) + halves + 3 * halves
    slots = 10
    first = 2 * (inner // UNIT) + halves
    holes = (first, first + 1, first + 5)
    anywhere = pl.BlockSpec(memory_space=pl.ANY)
    vmem = pl.BlockSpec(memory_space=pltpu.VMEM)
    shape = jax.ShapeDtypeStruct
    if ringed:
        more = sum_scratch(units, slots, UNIT, width) + sum_scratch(1, 1, SMALL_ROWS, 128)
    else:
        more = [pltpu.VMEM((slots, UNIT, width), F32), pltpu.VMEM((1, SMALL_ROWS, 128), F32)]
    return pl.pallas_call(
        functools.partial(back_kernel, ringed, count, rows, steps, units, slots, holes, block),
        out_shape=(
            shape(shape_in, BF16), shape(shape_in, F32), shape((units, UNIT, width), F32), shape((1, SMALL_ROWS, 128), F32),
        ),
        in_specs=[anywhere] * 9 + [vmem] * 4 + [anywhere] * 4,
        out_specs=(anywhere,) * 4,
        scratch_shapes=[
            pltpu.VMEM((total, width), F32), pltpu.VMEM((total, width), F32), pltpu.VMEM((total, width), F32), pltpu.VMEM((total, width), F32),
            pltpu.VMEM((total, hidden), BF16), pltpu.VMEM((total, width), BF16), pltpu.VMEM((total, width), BF16), pltpu.VMEM((total, width), BF16),
            pltpu.VMEM((width, total), BF16),
            pltpu.VMEM(w_in.shape, BF16), pltpu.VMEM(w_out.shape, BF16), pltpu.VMEM(w_up.shape, BF16), pltpu.VMEM(w_down.shape, BF16),
            pltpu.VMEM((2, size, wide), F32), pltpu.VMEM((2, size, wide), BF16), pltpu.VMEM((2, size, wide), BF16),
            pltpu.VMEM((2, size, wide), BF16), pltpu.VMEM((2, size, wide), BF16),
            pltpu.VMEM((2, rows, block, width), BF16), pltpu.VMEM((2, rows, block, width), F32), pltpu.VMEM((8, inner), F32),
            pltpu.SemaphoreType.DMA((8,)), pltpu.SemaphoreType.DMA((5, 2)), pltpu.SemaphoreType.DMA((2,)),
            *chain_scratch(halves, count, rows, wide),
            *more,
        ],
        compiler_params=pltpu.CompilerParams(collective_id=cid, has_side_effects=True, vmem_limit_bytes=63 * 2**20),
        cost_estimate=pl.CostEstimate(flops=2 * total * width * (8 * hidden + 6 * inner), bytes_accessed=80 * 2**20, transcendentals=total * inner),
        name="back",
    )(x, cot, middle, state, decay, fade, rise, weight, lean, gain_one.reshape(1, -1), gain_two.reshape(1, -1), up_bias.reshape(1, -1), down_bias.reshape(1, -1), w_in, w_out, w_up, w_down)


def on_device(tokens, cotangent, reset_pos, norm1_gain, w_in, forget_bias, input_bias, w_out, norm2_gain, w_up, up_bias, w_down, down_bias):
    ringed = lax.axis_size("seq") == 8 and lax.axis_size("rows") == 4
    width = tokens.shape[-1]
    hidden, inner = w_out.shape[0], w_down.shape[0]
    kept = front(tokens, cotangent, reset_pos, norm1_gain, w_in, forget_bias, input_bias, w_out)
    mixed, grad_tokens, units, small = back(
        ringed, tokens.shape, *kept, norm1_gain, norm2_gain, up_bias, down_bias, w_in, w_out, w_up, w_down
    )
    if not ringed:
        units, small = lax.psum((units, small), ("seq", "rows"))
    feeds = inner // UNIT
    halves = hidden // UNIT
    grad_down = jnp.concatenate([units[2 * f] for f in range(feeds)], axis=0)
    grad_up = jnp.concatenate([units[2 * f + 1] for f in range(feeds)], axis=1)
    grad_out = units[2 * feeds : 2 * feeds + halves].reshape(hidden, width)
    base = 2 * feeds + halves
    grad_in = jnp.concatenate([units[base + 3 * j + k] for k in range(3) for j in range(halves)], axis=1)
    flat = small[0]

    def rows_of(first, length):
        return flat[first : first + length // 128].reshape(length)

    return (
        mixed, grad_tokens, rows_of(0, width), grad_in, rows_of(4, hidden), rows_of(12, hidden), grad_out,
        rows_of(20, width), grad_up, rows_of(24, inner), grad_down, rows_of(40, width),
    )


def solution(mesh):
    return jax.shard_map(
        on_device,
        mesh=mesh,
        in_specs=(
            P("rows", "seq", None),
            P("rows", "seq", None),
            P("rows", None),
            P(),
            P(),
            P(),
            P(),
            P(),
            P(),
            P(),
            P(),
            P(),
            P(),
        ),
        out_specs=(
            P("rows", "seq", None),
            P("rows", "seq", None),
            P(),
            P(),
            P(),
            P(),
            P(),
            P(),
            P(),
            P(),
            P(),
            P(),
        ),
        check_vma=False,
    )
```

```python
import functools
import math
import jax
import jax.numpy as jnp
from jax import lax
from jax.experimental import pallas as pl
from jax.experimental.pallas import tpu as pltpu
from jax.sharding import PartitionSpec as P

MESH = pl.DeviceIdType.MESH
EPS = 1e-6
F32 = jnp.float32
BF16 = jnp.bfloat16
STAGES = 13
KINDS = 10
SPAN = 512
UNIT = 256
WIDE = 512
SLOTS = 12
SMALL_ROWS = 48
DOUBLINGS = 5
SLOW = (0, 1, 3, 6, 8, 10, 11, 12, 14, 16, 19, 21, 22)
FAST = (0, 1, 3, 5, 7, 8, 9, 10, 11, 13, 15, 17, 18)


def place():
    seq = lax.axis_index("seq")
    rows = lax.axis_index("rows")
    return lax.div(rows, 2), lax.rem(seq, 2), lax.div(seq, 2), lax.rem(rows, 2)


def spot(x, y, z, core):
    return (z * 2 + y, x * 2 + core)


def dot(left, right):
    return jnp.dot(left, right, preferred_element_type=F32)


def dot_nt(left, right):
    return lax.dot_general(left, right, (((1,), (1,)), ((), ())), preferred_element_type=F32)


def dot_tn(left, right):
    return lax.dot_general(left, right, (((0,), (0,)), ((), ())), preferred_element_type=F32)


class Chain:
    def __init__(self, count, sign, sent, got, join, send, recv):
        self.count, self.sign = count, sign
        self.sent, self.got, self.join = sent, got, join
        self.send, self.recv = send, recv
        self.rounds = max(1, math.ceil(math.log2(count)))
        seq = lax.axis_index("seq")
        self.seq = seq
        self.place = seq if sign > 0 else count - 1 - seq

    def partners(self):
        for r in range(self.rounds):
            far = 2**r
            yield self.seq + self.sign * far, self.place + far < self.count
            yield self.seq - self.sign * far, self.place >= far

    def copy(self, part, r, other):
        return pltpu.make_async_remote_copy(
            src_ref=self.sent.at[part, r], dst_ref=self.got.at[part, r],
            send_sem=self.send.at[part, r], recv_sem=self.recv.at[part, r],
            device_id=(other, lax.axis_index("rows")), device_id_type=MESH,
        )

    def push(self, part, r):
        @pl.when(self.place + 2**r < self.count)
        def _():
            self.copy(part, r, self.seq + self.sign * 2**r).start()

    def start(self, part, product, end):
        self.sent[part, 0, 0] = product
        self.sent[part, 0, 1] = end
        self.join[part, 0] = jnp.ones_like(product)
        self.join[part, 1] = jnp.zeros_like(end)
        self.push(part, 0)

    def advance(self, part, r):
        last = r == self.rounds - 1

        @pl.when(self.place >= 2**r)
        def _():
            self.copy(part, r, self.seq - self.sign * 2**r).wait_recv()
            product, end = self.got[part, r, 0], self.got[part, r, 1]
            own = self.join[part, 0]
            self.join[part, 1] = self.join[part, 1] + own * end
            if not last:
                self.join[part, 0] = own * product
                here = self.sent[part, r, 0]
                self.sent[part, r + 1, 0] = here * product
                self.sent[part, r + 1, 1] = self.sent[part, r, 1] + here * end

        if not last:
            @pl.when(self.place < 2**r)
            def _():
                self.sent[part, r + 1] = self.sent[part, r]
            self.push(part, r + 1)

    def finish(self, part):
        for r in range(self.rounds):
            @pl.when(self.place + 2**r < self.count)
            def _():
                self.copy(part, r, self.seq + self.sign * 2**r).wait_send()


def greet_chain(chain):
    barrier = pltpu.get_barrier_semaphore()
    rows = lax.axis_index("rows")
    total = 0
    for other, there in chain.partners():
        @pl.when(there)
        def _():
            pl.semaphore_signal(barrier, inc=1, device_id=(other, rows), device_id_type=MESH)
        total = total + jnp.where(there, 1, 0)
    return barrier, total


def chain_scratch(parts, count, rows, width):
    rounds = max(1, math.ceil(math.log2(count)))
    return [
        pltpu.VMEM((parts, rounds, 2, rows, width), F32),
        pltpu.VMEM((parts, rounds, 2, rows, width), F32),
        pltpu.VMEM((parts, 2, rows, width), F32),
        pltpu.SemaphoreType.DMA((parts, rounds)),
        pltpu.SemaphoreType.DMA((parts, rounds)),
    ]


def front_kernel(
    count, rows, steps, chunk, block,
    tokens, cotangent, reset, gain, w_in, forget_bias, input_bias, w_out,
    x_out, cot_out, middle_out, state_out, decay_out, fade_out, rise_out, weight_out, lean_out,
    tok_v, cot_v, x_v, normed_v, w_v, w_out_v, keep_v, decay_v, update_v, cand_v, fade_v, rise_v, weight_v, lean_v, state_v, middle_v,
    sent, got, join, send, recv, sems, out_sems,
):
    total, width = x_v.shape
    hidden = w_out_v.shape[0]
    parts = hidden // chunk
    size = block * rows
    blocks = steps // block
    chain = Chain(count, 1, sent, got, join, send, recv)
    barrier, greeted = greet_chain(chain)
    loads = [pltpu.make_async_copy(tokens, tok_v, sems.at[0])]
    for j in range(parts):
        for k in range(3):
            loads.append(pltpu.make_async_copy(w_in.at[:, pl.ds(k * hidden + j * chunk, chunk)], w_v.at[j, :, pl.ds(k * chunk, chunk)], sems.at[1 + 3 * j + k]))
    loads.append(pltpu.make_async_copy(cotangent, cot_v, sems.at[1 + 3 * parts]))
    loads.append(pltpu.make_async_copy(w_out, w_out_v, sems.at[2 + 3 * parts]))
    for load in loads:
        load.start()
    loads[0].wait()

    first = lax.axis_index("seq") * steps
    marks = [jnp.broadcast_to(reset[:, k : k + 1], (rows, 128)) for k in range(reset.shape[1])]

    def mark(t, carry):
        hit = marks[0] == first + t
        for one in marks[1:]:
            hit = hit | (one == first + t)
        keep_v[pl.ds(pl.multiple_of(t * rows, rows), rows)] = jnp.where(hit, 0.0, 1.0)
        return carry

    lax.fori_loop(0, steps, mark, 0, unroll=4)
    gains = gain[...]

    def norm(b, carry):
        at = pl.ds(pl.multiple_of(b * size, size), size)
        x = tok_v[:, pl.ds(pl.multiple_of(b * block, block), block), :].astype(F32)
        x = jnp.swapaxes(x, 0, 1).reshape(size, width)
        x_v[at] = x.astype(BF16)
        scale = lax.rsqrt(jnp.mean(x * x, axis=-1, keepdims=True) + EPS)
        normed_v[at] = (x * scale * gains).astype(BF16)
        return carry

    lax.fori_loop(0, blocks, norm, 0)
    outs = [pltpu.make_async_copy(x_v, x_out, out_sems.at[0])]
    outs[0].start()

    def gates(j):
        lanes = pl.ds(j * chunk, chunk)
        shift_f, shift_i = -forget_bias[:, lanes], -input_bias[:, lanes]

        def one(b, carry):
            product, end = carry
            at = pl.ds(pl.multiple_of(b * size, size), size)
            project = dot(normed_v[at], w_v[j])
            neg_f = shift_f - project[:, :chunk]
            neg_i = shift_i - project[:, chunk : 2 * chunk]
            cand = project[:, 2 * chunk :]
            lower = jnp.maximum(jnp.minimum(neg_f, neg_i) - 20.0, 0.0)
            exp_f = jnp.exp(jnp.minimum(neg_f - lower, 80.0))
            exp_i = jnp.exp(jnp.minimum(neg_i - lower, 80.0))
            one_f, one_i = 1.0 + exp_f, 1.0 + exp_i
            share = 1.0 / (one_f + one_i)
            decay, weight = one_i * share, one_f * share
            fade_v[j % 2, at] = (decay * (exp_f * share)).astype(BF16)
            rise_v[j % 2, at] = (weight * (exp_i * share)).astype(BF16)
            weight_v[j % 2, at] = weight.astype(BF16)
            cand_v[at, lanes] = cand
            update = weight * cand
            update_v[at, lanes] = update
            keep = jnp.concatenate([keep_v[at]] * (chunk // 128), axis=1)
            decay = decay * keep
            decay_v[at, lanes] = decay
            for t in range(block):
                here = decay[t * rows : (t + 1) * rows]
                end = here * end + update[t * rows : (t + 1) * rows]
                product = here * product
            return product, end

        start = (jnp.ones((rows, chunk), F32), jnp.zeros((rows, chunk), F32))
        return lax.fori_loop(0, blocks, one, start)

    def scan(j):
        lanes = pl.ds(j * chunk, chunk)

        def one(b, state):
            at = pl.ds(pl.multiple_of(b * size, size), size)
            states = []
            for t in range(block):
                here = pl.ds(pl.multiple_of(b * size + t * rows, rows), rows)
                keep = jnp.concatenate([keep_v[here]] * (chunk // 128), axis=1)
                lean_v[j % 2, here] = (keep * state - cand_v[here, lanes]).astype(BF16)
                state = decay_v[here, lanes] * state + update_v[here, lanes]
                states.append(state.astype(BF16))
            low = jnp.concatenate(states, axis=0)
            state_v[at, lanes] = low
            add = dot(low, w_out_v[lanes])
            if j == 0:
                middle_v[at] = x_v[at].astype(F32) + add
            else:
                middle_v[at] = middle_v[at] + add
            return state

        lax.fori_loop(0, blocks, one, join[j, 1])

    def put(source, target, slot, wait=False):
        copy = pltpu.make_async_copy(source, target, out_sems.at[slot])
        if wait:
            copy.wait()
        else:
            copy.start()

    def gate_outs(j, wait=False):
        lanes = pl.ds(j * chunk, chunk)
        for k, (a, b) in enumerate(((fade_v, fade_out), (rise_v, rise_out), (weight_v, weight_out))):
            put(a.at[j % 2], b.at[:, lanes], 1 + 3 * j + k, wait)
        put(decay_v.at[:, lanes], decay_out.at[:, lanes], 1 + 3 * parts + j, wait)

    def scan_outs(j, wait=False):
        lanes = pl.ds(j * chunk, chunk)
        put(lean_v.at[j % 2], lean_out.at[:, lanes], 1 + 4 * parts + 2 * j, wait)
        put(state_v.at[:, lanes], state_out.at[:, lanes], 2 + 4 * parts + 2 * j, wait)

    ready = 0
    for j in range(parts):
        for k in range(3):
            loads[1 + 3 * j + k].wait()
        if j >= 2:
            gate_outs(j - 2, True)
        product, end = gates(j)
        gate_outs(j)
        if j == 0:
            pl.semaphore_wait(barrier, greeted)
        chain.start(j, product, end)
        for i in range(j - 1, -1, -1):
            if j - 1 - i < chain.rounds:
                chain.advance(i, j - 1 - i)
    for k in range(2):
        loads[1 + 3 * parts + k].wait()

    def turn(b, carry):
        at = pl.ds(pl.multiple_of(b * size, size), size)
        c = cot_v[:, pl.ds(pl.multiple_of(b * block, block), block), :].astype(F32)
        normed_v[at] = jnp.swapaxes(c, 0, 1).reshape(size, width).astype(BF16)
        return carry

    lax.fori_loop(0, blocks, turn, 0)
    put(normed_v, cot_out, 1 + 6 * parts)

    step = parts - 1
    while ready < parts:
        for i in range(parts - 1, -1, -1):
            if 0 <= step - 1 - i < chain.rounds and step >= parts:
                chain.advance(i, step - 1 - i)
        while ready < parts and ready + chain.rounds <= step:
            if ready >= 2:
                scan_outs(ready - 2, True)
            scan(ready)
            scan_outs(ready)
            ready += 1
        step += 1
    put(middle_v, middle_out, 2 + 6 * parts)
    for j in range(parts):
        if j >= parts - 2:
            gate_outs(j, True)
            scan_outs(j, True)
        chain.finish(j)
    outs[0].wait()
    put(normed_v, cot_out, 1 + 6 * parts, True)
    put(middle_v, middle_out, 2 + 6 * parts, True)


def front(tokens, cotangent, reset, gain, w_in, forget_bias, input_bias, w_out, cid=1):
    rows, steps, width = tokens.shape
    hidden = w_out.shape[0]
    total = rows * steps
    count = lax.axis_size("seq")
    chunk, block = 256, 16
    parts = hidden // chunk
    anywhere = pl.BlockSpec(memory_space=pl.ANY)
    vmem = pl.BlockSpec(memory_space=pltpu.VMEM)
    shape = jax.ShapeDtypeStruct
    return pl.pallas_call(
        functools.partial(front_kernel, count, rows, steps, chunk, block),
        out_shape=(
            shape((total, width), BF16), shape((total, width), BF16), shape((total, width), F32),
            shape((total, hidden), BF16), shape((total, hidden), F32), shape((total, hidden), BF16),
            shape((total, hidden), BF16), shape((total, hidden), BF16), shape((total, hidden), BF16),
        ),
        in_specs=[anywhere, anywhere, vmem, vmem, anywhere, vmem, vmem, anywhere],
        out_specs=(anywhere,) * 9,
        scratch_shapes=[
            pltpu.VMEM(tokens.shape, BF16), pltpu.VMEM(tokens.shape, BF16), pltpu.VMEM((total, width), BF16), pltpu.VMEM((total, width), BF16),
            pltpu.VMEM((parts, width, 3 * chunk), BF16), pltpu.VMEM(w_out.shape, BF16), pltpu.VMEM((total, 128), F32),
            pltpu.VMEM((total, hidden), F32), pltpu.VMEM((total, hidden), F32), pltpu.VMEM((total, hidden), F32),
            pltpu.VMEM((2, total, chunk), BF16), pltpu.VMEM((2, total, chunk), BF16), pltpu.VMEM((2, total, chunk), BF16),
            pltpu.VMEM((2, total, chunk), BF16), pltpu.VMEM((total, hidden), BF16), pltpu.VMEM((total, width), F32),
            *chain_scratch(parts, count, rows, chunk),
            pltpu.SemaphoreType.DMA((3 + 3 * parts,)), pltpu.SemaphoreType.DMA((3 + 6 * parts,)),
        ],
        compiler_params=pltpu.CompilerParams(collective_id=cid, has_side_effects=True, vmem_limit_bytes=62 * 2**20),
        cost_estimate=pl.CostEstimate(flops=2 * total * width * 4 * hidden, bytes_accessed=40 * 2**20, transcendentals=3 * total * hidden),
        name="front",
    )(tokens, cotangent, reset, gain.reshape(1, -1), w_in, forget_bias.reshape(1, -1), input_bias.reshape(1, -1), w_out)


class Summing:
    def __init__(self, plan, grads, half_in, part_in, up_in, down_in, last_in, send, recv, local, result):
        self.plan, self.grads = plan, grads
        self.half_in, self.part_in, self.up_in, self.down_in, self.last_in = half_in, part_in, up_in, down_in, last_in
        self.result, self.send, self.recv, self.local = result, send, recv, local
        x, y, z, core = place()
        self.z = z
        first = core == 0
        self.sibling = spot(x, y, z, 1 - core)
        along_x, along_y = spot(1 - x, y, z, core), spot(x, 1 - y, z, core)
        self.near = tuple(jnp.where(first, a, b) for a, b in zip(along_x, along_y))
        self.far = tuple(jnp.where(first, b, a) for a, b in zip(along_x, along_y))
        self.above = spot(x, y, z + 1, core)
        self.below = spot(x, y, z - 1, core)
        near_bit = jnp.where(first, x, y)
        far_bit = jnp.where(first, y, x)
        self.n_half, self.n_part, self.n_line, self.n_tip = SPAN // 2, SPAN // 4, SPAN // 16, SPAN // 32
        self.half = core * self.n_half
        self.other_half = (1 - core) * self.n_half
        self.part = self.half + near_bit * self.n_part
        self.other_part = self.half + (1 - near_bit) * self.n_part
        self.tip = self.part + self.n_line * z + self.n_tip * far_bit
        self.other_tip = self.part + self.n_line * z + self.n_tip * (1 - far_bit)

    def copy(self, kind, unit, source, target, device):
        return pltpu.make_async_remote_copy(
            src_ref=source, dst_ref=target, send_sem=self.send.at[kind, unit], recv_sem=self.recv.at[kind, unit],
            device_id=device, device_id_type=MESH,
        )

    def slot_of(self, u):
        return self.plan[u] if isinstance(u, int) else (u, 0, WIDE)

    def rows(self, u, start, count):
        slot, column, width = self.slot_of(u)
        return self.grads.at[slot, pl.ds(pl.multiple_of(start, 8), count), pl.ds(column, width)]

    def done(self, u, start, count):
        return self.result.at[u, pl.ds(pl.multiple_of(start, 8), count), pl.ds(0, self.slot_of(u)[2])]

    def land(self, ref, u, slots, start, count):
        return ref.at[lax.rem(u, slots), pl.ds(start, count), pl.ds(0, self.slot_of(u)[2])]

    def c_half(self, u):
        return self.copy(0, u, self.rows(u, self.other_half, self.n_half), self.land(self.half_in, u, 4, 0, self.n_half), self.sibling)

    def c_part(self, u):
        return self.copy(1, u, self.rows(u, self.other_part, self.n_part), self.land(self.part_in, u, 4, 0, self.n_part), self.near)

    def c_up(self, u, z):
        low, rest = self.n_line * (z + 1), self.n_line * (3 - z)
        return self.copy(2, u, self.rows(u, self.part + low, rest), self.land(self.up_in, u, 8, low - self.n_line, rest), self.above)

    def c_down(self, u, z):
        rest = self.n_line * z
        return self.copy(3, u, self.rows(u, self.part, rest), self.land(self.down_in, u, 8, 0, rest), self.below)

    def c_last(self, u):
        return self.copy(4, u, self.rows(u, self.other_tip, self.n_tip), self.last_in.at[u, :, pl.ds(0, self.slot_of(u)[2])], self.far)

    def c_own(self, u):
        return pltpu.make_async_copy(self.rows(u, self.tip, self.n_tip), self.done(u, self.tip, self.n_tip), self.local.at[u])

    def c_far(self, u, start):
        return self.copy(5, u, self.rows(u, start, self.n_tip), self.done(u, start, self.n_tip), self.far)

    def c_rise(self, u, z):
        piece = self.done(u, self.part, self.n_line * (z + 1))
        return self.copy(6, u, piece, piece, self.above)

    def c_fall(self, u, z):
        piece = self.done(u, self.part + self.n_line * z, self.n_line * (4 - z))
        return self.copy(7, u, piece, piece, self.below)

    def c_near(self, u, start):
        piece = self.done(u, start, self.n_part)
        return self.copy(8, u, piece, piece, self.near)

    def c_sibling(self, u, start):
        piece = self.done(u, start, self.n_half)
        return self.copy(9, u, piece, piece, self.sibling)

    def add(self, u, start, count, ref):
        slot, column, width = self.slot_of(u)
        step = math.gcd(count, 64)
        lanes = pl.ds(column, width)

        def one(i, carry):
            here = pl.ds(pl.multiple_of(start + i * step, 8), step)
            there = pl.ds(pl.multiple_of(i * step, 8), step)
            self.grads[slot, here, lanes] = self.grads[slot, here, lanes] + ref[there]
            return carry

        lax.fori_loop(0, count // step, one, 0)

    def at_each(self, action):
        for k in range(4):
            pl.when(self.z == k)(functools.partial(action, k))

    def stage(self, s, u):
        z = self.z
        if s == 0:
            self.c_half(u).start()
        elif s == 1:
            self.c_half(u).wait()
            self.add(u, self.half, self.n_half, self.land(self.half_in, u, 4, 0, self.n_half))
            self.c_part(u).start()
        elif s == 2:
            self.c_part(u).wait()
            self.add(u, self.part, self.n_part, self.land(self.part_in, u, 4, 0, self.n_part))
        if 2 <= s <= 5:
            up, down = s - 2, 5 - s

            @pl.when(z == up)
            def _():
                if up > 0:
                    self.c_up(u, up - 1).wait_recv()
                    low, rest = self.n_line * up, self.n_line * (4 - up)
                    self.add(u, self.part + low, rest, self.land(self.up_in, u, 8, low - self.n_line, rest))
                if up < 3:
                    self.c_up(u, up).start()

            @pl.when(z == down)
            def _():
                if down < 3:
                    self.c_down(u, down + 1).wait_recv()
                    rest = self.n_line * (down + 1)
                    self.add(u, self.part, rest, self.land(self.down_in, u, 8, 0, rest))
                if down > 0:
                    self.c_down(u, down).start()
        if s == 5:
            self.c_last(u).start()
        elif s == 6:
            def sent(k):
                if k < 3:
                    self.c_up(u, k).wait_send()
                if k > 0:
                    self.c_down(u, k).wait_send()

            self.at_each(sent)
            self.c_last(u).wait()
            self.add(u, self.tip, self.n_tip, self.last_in.at[u, :, pl.ds(0, self.slot_of(u)[2])])
            self.c_far(u, self.tip).start()
            self.c_own(u).start()
        elif s == 7:
            self.c_far(u, self.tip).wait_send()
            self.c_far(u, self.other_tip).wait_recv()
            self.c_own(u).wait()
        if 7 <= s <= 10:
            up, down = s - 7, 10 - s

            @pl.when(z == up)
            def _():
                if up > 0:
                    self.c_rise(u, up - 1).wait_recv()
                if up < 3:
                    self.c_rise(u, up).start()

            @pl.when(z == down)
            def _():
                if down < 3:
                    self.c_fall(u, down + 1).wait_recv()
                if down > 0:
                    self.c_fall(u, down).start()
        if s == 10:
            self.c_near(u, self.part).start()
        elif s == 11:
            def sent(k):
                if k < 3:
                    self.c_rise(u, k).wait_send()
                if k > 0:
                    self.c_fall(u, k).wait_send()

            self.at_each(sent)
            self.c_near(u, self.part).wait_send()
            self.c_near(u, self.other_part).wait_recv()
            self.c_sibling(u, self.half).start()
        elif s == 12:
            self.c_sibling(u, self.half).wait_send()
            self.c_sibling(u, self.other_half).wait_recv()


def sum_scratch(units, slots):
    return [
        pltpu.VMEM((slots, SPAN, WIDE), F32),
        pltpu.VMEM((4, SPAN // 2, WIDE), F32),
        pltpu.VMEM((4, SPAN // 4, WIDE), F32),
        pltpu.VMEM((8, 3 * SPAN // 16, WIDE), F32),
        pltpu.VMEM((8, 3 * SPAN // 16, WIDE), F32),
        pltpu.VMEM((units, SPAN // 32, WIDE), F32),
        pltpu.SemaphoreType.DMA((KINDS, units)),
        pltpu.SemaphoreType.DMA((KINDS, units)),
        pltpu.SemaphoreType.DMA((units,)),
    ]


class Doubling:
    def __init__(self, own, got, send, recv):
        self.own, self.got, self.send, self.recv = own, got, send, recv
        x, y, z, core = place()
        self.partners = (
            spot(x, y, z, 1 - core), spot(1 - x, y, z, core), spot(x, 1 - y, z, core),
            spot(x, y, z + 1 - 2 * lax.rem(z, 2), core), spot(x, y, z + 2 - 4 * lax.div(z, 2), core),
        )

    def copy(self, k):
        return pltpu.make_async_remote_copy(
            src_ref=self.own.at[k], dst_ref=self.got.at[k], send_sem=self.send.at[k], recv_sem=self.recv.at[k],
            device_id=self.partners[k], device_id_type=MESH,
        )

    def step(self, k):
        if k > 0:
            self.copy(k - 1).wait()
            self.own[k] = self.own[k - 1] + self.got[k - 1]
        if k < DOUBLINGS:
            self.copy(k).start()


def greet_ring(ring):
    barrier = pltpu.get_barrier_semaphore()
    for there in (ring.sibling, ring.near, ring.far):
        pl.semaphore_signal(barrier, inc=1, device_id=there, device_id_type=MESH)

    @pl.when(ring.z > 0)
    def _():
        pl.semaphore_signal(barrier, inc=1, device_id=ring.below, device_id_type=MESH)

    @pl.when(ring.z < 3)
    def _():
        pl.semaphore_signal(barrier, inc=1, device_id=ring.above, device_id_type=MESH)

    return 3 + jnp.where(ring.z > 0, 1, 0) + jnp.where(ring.z < 3, 1, 0)


GELU_A = math.sqrt(2.0 / math.pi)
GELU_B = GELU_A * 0.044715


def back_kernel(
    ringed, count, rows, steps, plan, block,
    x_in, cot_in, middle_in, state_in, decay_in, fade_in, rise_in, weight_in, lean_in,
    gain_one, gain_two, up_bias, down_bias, w_in, w_out, w_up, w_down,
    mixed_out, tokens_out, result, small_out,
    middle_v, second_v, mixed_v, state_v, cot_v, x_v, low_v, cand_v, turned_v, w_in_v, w_out_v, w_up_v, w_down_v,
    decay_s, fade_s, rise_s, weight_s, lean_s, mixed_s, tokens_s, sums_v,
    load_sems, stream_sems, stage_sems,
    sent, got, join, send, recv,
    *ring_refs,
):
    total, width = x_v.shape
    hidden = w_out_v.shape[0]
    inner = w_down_v.shape[0]
    size = block * rows
    blocks = steps // block
    wide = UNIT
    parts = hidden // wide
    big = 512
    per = total // big
    feeds = inner // SPAN
    chain = Chain(count, -1, sent, got, join, send, recv)
    barrier, greeted = greet_chain(chain)
    grads, own_v = ring_refs[:2]
    if ringed:
        ring = Summing(plan, grads, *ring_refs[2:10], result)
        small = Doubling(own_v, *ring_refs[10:])
        greeted = greeted + greet_ring(ring)
    small_v = own_v.at[0]

    loads = [
        pltpu.make_async_copy(source, target, load_sems.at[k])
        for k, (source, target) in enumerate((
            (middle_in, middle_v), (w_up, w_up_v), (cot_in, cot_v), (w_down, w_down_v), (state_in, state_v),
            (w_out, w_out_v), (w_in, w_in_v), (x_in, x_v),
        ))
    ]
    for load in loads:
        load.start()

    def at_block(b, n=size):
        return pl.ds(pl.multiple_of(b * n, n), n)

    flying = {}
    waiting = []
    clock = [0]

    def pace(unit):
        return SLOW if plan[unit][2] > UNIT else FAST

    def tick():
        now = clock[0]
        clock[0] += 1
        if waiting:
            flying[waiting.pop(0)] = now
        if ringed:
            for unit in sorted(flying):
                if now - flying[unit] in pace(unit):
                    ring.stage(pace(unit).index(now - flying[unit]), unit)

    def rolling_tick(i, half):
        for s in reversed(range(STAGES)):
            behind = SLOW[s] + early - half
            if ringed and behind % 2 == 0 and behind // 2 < feeds * per // 2:
                pl.when(i >= behind // 2)(functools.partial(ring.stage, s, i - behind // 2))

    def beat(number, body, ticks, *carry):
        each = number // ticks
        for k in range(ticks):
            carry = lax.fori_loop(each * k, each * k + each, lambda i, c: body(i, *c), carry)
            tick()
        return carry

    def put_unit(unit):
        if not ringed:
            slot, column, length = plan[unit] if isinstance(unit, int) else (unit, 0, WIDE)
            copy = pltpu.make_async_copy(
                grads.at[slot, :, pl.ds(column, length)], result.at[unit, :, pl.ds(0, length)], load_sems.at[0]
            )
            copy.start()
            copy.wait()

    sums_v[...] = jnp.zeros_like(sums_v)
    small_v[...] = jnp.zeros_like(small_v)

    def put_small(row, value):
        for k in range(value.shape[1] // 128):
            small_v[pl.ds(row + k, 1)] = value[:, 128 * k : 128 * k + 128]

    def gather(slot, column, value, fresh):
        lanes = pl.ds(column, value.shape[1])

        @pl.when(fresh)
        def _():
            grads[slot, :, lanes] = value

        @pl.when(jnp.logical_not(fresh))
        def _():
            grads[slot, :, lanes] = grads[slot, :, lanes] + value

    loads[0].wait()
    gains = gain_two[...]
    bias = down_bias[...]

    def norm_two(b, carry):
        at = at_block(b)
        value = middle_v[at]
        scale = lax.rsqrt(jnp.mean(value * value, axis=-1, keepdims=True) + EPS)
        normed = value * scale * gains
        low_v[at] = normed.astype(BF16)
        turned_v[:, at] = jnp.swapaxes(normed, 0, 1).astype(BF16)
        mixed_v[at] = value + bias
        second_v[at] = jnp.zeros_like(value)
        return carry

    lax.fori_loop(0, blocks, norm_two, 0)
    for k in (1, 2, 3):
        loads[k].wait()
    pl.semaphore_wait(barrier, greeted)

    def feed(f, tok):
        at = at_block(tok, big)
        lanes = pl.ds(pl.multiple_of(f * SPAN, SPAN), SPAN)
        cot = cot_v[at]
        pre = dot(low_v[at], w_up_v[:, lanes]) + up_bias[:, lanes]
        back_act = dot_nt(cot, w_down_v[lanes])
        square = pre * pre
        gate = 0.5 * jnp.tanh(pre * (GELU_A + GELU_B * square)) + 0.5
        act = pre * gate
        slope = gate + act * (1.0 - gate) * (2.0 * GELU_A + 6.0 * GELU_B * square)
        back_up = back_act * slope
        sums_v[0:1, lanes] = sums_v[0:1, lanes] + jnp.sum(back_up, axis=0, keepdims=True)
        act, back_up = act.astype(BF16), back_up.astype(BF16)
        mixed_v[at] = mixed_v[at] + dot(act, w_down_v[lanes])
        second_v[at] = second_v[at] + dot_nt(back_up, w_up_v[:, lanes])
        gather(2 * f, 0, dot_tn(act, cot), tok == 0)
        gather(2 * f + 1, 0, dot(turned_v[:, at], back_up), tok == 0)

    early = per - 1

    def feed_pair(i, carry):
        f, tok = lax.div(2 * i, per), lax.rem(2 * i, per)
        for half in range(2):
            feed(f, tok + half)
            if half == 1:
                @pl.when(tok + 2 == per)
                def _():
                    put_unit(2 * f)
                    put_unit(2 * f + 1)
            rolling_tick(i, half)
        return carry

    lax.fori_loop(0, feeds * per // 2, feed_pair, 0)
    clock[0] = feeds * per - early
    flying.update({u: 2 * u for u in range(2 * feeds) if 2 * u < clock[0]})
    waiting.extend(u for u in range(2 * feeds) if 2 * u >= clock[0])

    def stage_copy(buffer, target, b):
        slot = lax.rem(b, 2)
        return pltpu.make_async_copy(buffer.at[slot], target.at[:, pl.ds(pl.multiple_of(b * block, block), block), :], stage_sems.at[slot])

    def finish_two(b, norm_sum, cot_sum):
        at = at_block(b)

        @pl.when(b >= 2)
        def _():
            stage_copy(mixed_s, mixed_out, b - 2).wait()
        mixed = jnp.swapaxes(mixed_v[at].reshape(block, rows, width), 0, 1)
        mixed_s[lax.rem(b, 2)] = mixed.astype(BF16)
        stage_copy(mixed_s, mixed_out, b).start()
        value, grad, cot = middle_v[at], second_v[at], cot_v[at].astype(F32)
        scale = lax.rsqrt(jnp.mean(value * value, axis=-1, keepdims=True) + EPS)
        plain = value * scale
        norm_sum = norm_sum + jnp.sum((grad * plain).reshape(size // 8, 8, width), axis=0)
        cot_sum = cot_sum + jnp.sum(cot.reshape(size // 8, 8, width), axis=0)
        lean = grad * gains
        back = cot + scale * (lean - plain * jnp.mean(lean * plain, axis=-1, keepdims=True))
        second_v[at] = back
        low_v[at] = back.astype(BF16)
        return norm_sum, cot_sum

    zero = jnp.zeros((8, width), F32)
    norm_sum, cot_sum = beat(blocks, finish_two, 2, zero, zero)
    for b in (blocks - 2, blocks - 1):
        stage_copy(mixed_s, mixed_out, b).wait()
    put_small(20, jnp.sum(norm_sum, axis=0, keepdims=True))
    put_small(24, sums_v[0:1])
    put_small(40, jnp.sum(cot_sum, axis=0, keepdims=True))

    loads[4].wait()
    loads[5].wait()

    def stream(buffer, source, j, b, k):
        slot = lax.rem(b, 2)
        lanes = pl.ds(j * wide, wide)
        return pltpu.make_async_copy(source.at[at_block(b), lanes], buffer.at[slot], stream_sems.at[k, slot])

    def half_of(refs, j):
        return refs[j // 2], slice(UNIT * (j % 2), UNIT * (j % 2) + UNIT)

    def first_pass(j):
        flows, lanes = half_of((mixed_v, middle_v), j)
        stream(decay_s, decay_in, j, blocks - 1, 0).start()

        def one(i, product, flow):
            b = blocks - 1 - i
            at = at_block(b)

            @pl.when(b > 0)
            def _():
                stream(decay_s, decay_in, j, b - 1, 0).start()
            back = dot_nt(low_v[at], w_out_v[pl.ds(j * wide, wide)])
            flows[at, lanes] = back
            stream(decay_s, decay_in, j, b, 0).wait()
            slot = lax.rem(b, 2)
            for t in reversed(range(block)):
                here = slice(t * rows, (t + 1) * rows)
                decay = decay_s[slot, here]
                flow = decay * (back[here] + flow)
                product = decay * product
            return product, flow

        product, flow = lax.fori_loop(0, blocks, lambda i, c: one(i, *c), (jnp.ones((rows, wide), F32), jnp.zeros((rows, wide), F32)))
        tick()
        chain.start(j, product, flow)

    def grad_out():
        for j in range(hidden // SPAN):
            def one(tok, carry):
                at = at_block(tok, big)
                gather(2 * feeds + j, 0, dot_tn(state_v[at, pl.ds(j * SPAN, SPAN)], low_v[at]), tok == 0)
                return carry

            lax.fori_loop(0, per, one, 0)
            put_unit(2 * feeds + j)
            waiting.append(2 * feeds + j)
            tick()

    gains_one = gain_one[...]

    def norm_one(b):
        at = at_block(b)
        value = x_v[at].astype(F32)
        scale = lax.rsqrt(jnp.mean(value * value, axis=-1, keepdims=True) + EPS)
        turned_v[:, at] = jnp.swapaxes(value * scale * gains_one, 0, 1).astype(BF16)
        return ()

    work = [functools.partial(first_pass, j) for j in range(parts)]
    work += [grad_out]

    def turn():
        loads[7].wait()
        beat(blocks, norm_one, 1)

    work.append(turn)
    for step in range(max(len(work), parts + chain.rounds)):
        if step < len(work):
            work[step]()
        else:
            tick()
        for i in range(parts):
            if 0 <= step - 1 - i < chain.rounds:
                chain.advance(i, step - 1 - i)

    streams = ((decay_s, decay_in), (fade_s, fade_in), (rise_s, rise_in), (weight_s, weight_in), (lean_s, lean_in))
    cand_refs = (low_v, cand_v)
    input_refs = (cot_v, w_down_v)

    def second_pass(j):
        flows, lanes = half_of((mixed_v, middle_v), j)
        to_input, to_cand = half_of(input_refs, j)[0], half_of(cand_refs, j)[0]
        for k, (buffer, source) in enumerate(streams):
            stream(buffer, source, j, blocks - 1, k).start()

        def one(i, flow, sum_f, sum_i):
            b = blocks - 1 - i
            slot = lax.rem(b, 2)

            @pl.when(b > 0)
            def _():
                for k, (buffer, source) in enumerate(streams):
                    stream(buffer, source, j, b - 1, k).start()
            for k, (buffer, source) in enumerate(streams):
                stream(buffer, source, j, b, k).wait()
            for t in reversed(range(block)):
                here = slice(t * rows, (t + 1) * rows)
                there = pl.ds(pl.multiple_of(b * size + t * rows, rows), rows)
                reach = flows[there, lanes] + flow
                flow = decay_s[slot, here] * reach
                lean = reach * lean_s[slot, here].astype(F32)
                grad_f = fade_s[slot, here].astype(F32) * lean
                grad_i = -(rise_s[slot, here].astype(F32) * lean)
                sum_f, sum_i = sum_f + grad_f, sum_i + grad_i
                state_v[there, wide * j : wide * j + wide] = grad_f.astype(BF16)
                to_input[there, lanes] = grad_i.astype(BF16)
                to_cand[there, lanes] = (weight_s[slot, here].astype(F32) * reach).astype(BF16)
            return flow, sum_f, sum_i

        none = jnp.zeros((rows, wide), F32)
        unused, sum_f, sum_i = beat(blocks, one, 2, join[j, 1], none, none)
        put_small(4 + 2 * j, jnp.sum(sum_f, axis=0, keepdims=True))
        put_small(12 + 2 * j, jnp.sum(sum_i, axis=0, keepdims=True))

    def grad_in(j):
        unit = 2 * feeds + hidden // SPAN + 3 * j

        def one(tok, carry):
            at = at_block(tok, big)
            turned = turned_v[:, at]
            lanes = half_of(input_refs, j)[1]
            pieces = (state_v[at, wide * j : wide * j + wide], half_of(input_refs, j)[0][at, lanes], half_of(cand_refs, j)[0][at, lanes])
            for k, piece in enumerate(pieces):
                gather(*plan[unit + k][:2], dot(turned, piece), tok == 0)
            return carry

        lax.fori_loop(0, per, one, 0)
        for k in range(3):
            put_unit(unit + k)
            waiting.append(unit + k)
        tick()

    for j in range(parts):
        second_pass(j)
        grad_in(j)

    loads[6].wait()

    def finish_one(b, norm_sum):
        at = at_block(b)

        @pl.when(b >= 2)
        def _():
            stage_copy(tokens_s, tokens_out, b - 2).wait()
        grad = dot_nt(state_v[at], w_in_v[:, :hidden])
        for k, refs in enumerate((input_refs, cand_refs)):
            for half in range(2):
                columns = pl.ds((k + 1) * hidden + half * SPAN, SPAN)
                grad = grad + dot_nt(refs[half][at], w_in_v[:, columns])
        value = x_v[at].astype(F32)
        scale = lax.rsqrt(jnp.mean(value * value, axis=-1, keepdims=True) + EPS)
        plain = value * scale
        norm_sum = norm_sum + jnp.sum((grad * plain).reshape(size // 8, 8, width), axis=0)
        lean = grad * gains_one
        back = second_v[at] + scale * (lean - plain * jnp.mean(lean * plain, axis=-1, keepdims=True))
        tokens_s[lax.rem(b, 2)] = jnp.swapaxes(back.reshape(block, rows, width), 0, 1)
        stage_copy(tokens_s, tokens_out, b).start()
        return (norm_sum,)

    (norm_sum,) = beat(blocks, finish_one, 8, jnp.zeros((8, width), F32))
    put_small(0, jnp.sum(norm_sum, axis=0, keepdims=True))
    if ringed:
        step = 0
        while step <= DOUBLINGS or waiting or any(clock[0] <= flying[unit] + pace(unit)[-1] for unit in flying):
            tick()
            if step <= DOUBLINGS:
                small.step(step)
            step += 1
        copy = pltpu.make_async_copy(own_v.at[DOUBLINGS], small_out.at[0], load_sems.at[0])
    else:
        copy = pltpu.make_async_copy(small_v, small_out.at[0], load_sems.at[0])
    copy.start()
    copy.wait()
    for b in (blocks - 2, blocks - 1):
        stage_copy(tokens_s, tokens_out, b).wait()
    for j in range(parts):
        chain.finish(j)


def back(ringed, shape_in, x, cot, middle, state, decay, fade, rise, weight, lean, gain_one, gain_two, up_bias, down_bias, w_in, w_out, w_up, w_down, cid=2):
    rows, steps, width = shape_in
    total = rows * steps
    hidden = w_out.shape[0]
    inner = w_down.shape[0]
    count = lax.axis_size("seq")
    block = 16
    size = block * rows
    wide = UNIT
    parts = hidden // wide
    feeds = inner // SPAN
    whole = 2 * feeds + hidden // SPAN
    plan = [(u, 0, WIDE) for u in range(whole)]
    for j in range(parts):
        slot = (whole + 2 * j) % SLOTS
        plan += [(slot, 0, UNIT), (slot, UNIT, UNIT), (slot + 1, 0, UNIT)]
    units = len(plan)
    anywhere = pl.BlockSpec(memory_space=pl.ANY)
    vmem = pl.BlockSpec(memory_space=pltpu.VMEM)
    shape = jax.ShapeDtypeStruct
    if ringed:
        first, *others = sum_scratch(units, SLOTS)
        more = [first, pltpu.VMEM((DOUBLINGS + 1, SMALL_ROWS, 128), F32), *others]
        more += [pltpu.VMEM((DOUBLINGS, SMALL_ROWS, 128), F32)] + [pltpu.SemaphoreType.DMA((DOUBLINGS,))] * 2
    else:
        more = [pltpu.VMEM((SLOTS, SPAN, WIDE), F32), pltpu.VMEM((1, SMALL_ROWS, 128), F32)]
    return pl.pallas_call(
        functools.partial(back_kernel, ringed, count, rows, steps, plan, block),
        out_shape=(
            shape(shape_in, BF16), shape(shape_in, F32), shape((units, SPAN, WIDE), F32), shape((1, SMALL_ROWS, 128), F32),
        ),
        in_specs=[anywhere] * 9 + [vmem] * 4 + [anywhere] * 4,
        out_specs=(anywhere,) * 4,
        scratch_shapes=[
            pltpu.VMEM((total, width), F32), pltpu.VMEM((total, width), F32), pltpu.VMEM((total, width), F32),
            pltpu.VMEM((total, hidden), BF16), pltpu.VMEM((total, width), BF16), pltpu.VMEM((total, width), BF16), pltpu.VMEM((total, width), BF16),
            pltpu.VMEM((total, width), BF16), pltpu.VMEM((width, total), BF16),
            pltpu.VMEM(w_in.shape, BF16), pltpu.VMEM(w_out.shape, BF16), pltpu.VMEM(w_up.shape, BF16), pltpu.VMEM(w_down.shape, BF16),
            pltpu.VMEM((2, size, wide), F32), pltpu.VMEM((2, size, wide), BF16), pltpu.VMEM((2, size, wide), BF16),
            pltpu.VMEM((2, size, wide), BF16), pltpu.VMEM((2, size, wide), BF16),
            pltpu.VMEM((2, rows, block, width), BF16), pltpu.VMEM((2, rows, block, width), F32), pltpu.VMEM((8, inner), F32),
            pltpu.SemaphoreType.DMA((8,)), pltpu.SemaphoreType.DMA((5, 2)), pltpu.SemaphoreType.DMA((2,)),
            *chain_scratch(parts, count, rows, wide),
            *more,
        ],
        compiler_params=pltpu.CompilerParams(collective_id=cid, has_side_effects=True, vmem_limit_bytes=63 * 2**20),
        cost_estimate=pl.CostEstimate(flops=2 * total * width * (8 * hidden + 6 * inner), bytes_accessed=80 * 2**20, transcendentals=total * inner),
        name="back",
    )(x, cot, middle, state, decay, fade, rise, weight, lean, gain_one.reshape(1, -1), gain_two.reshape(1, -1), up_bias.reshape(1, -1), down_bias.reshape(1, -1), w_in, w_out, w_up, w_down)


def settle_kernel(places, mixed, tokens, units, small, *refs):
    outs, (mixed_v, tokens_v, units_v, reads, writes) = refs[:-5], refs[-5:]
    copies = []
    for k in range(mixed.shape[0] // 4):
        some = pl.ds(4 * k, 4)
        copies.append((tokens.at[some], tokens_v.at[some], outs[1].at[some]))
        copies.append((mixed.at[some], mixed_v.at[some], outs[0].at[some]))
    for u, length, array, row, column in places:
        lanes = pl.ds(0, length)
        copies.append((units.at[u, :, lanes], units_v.at[u, :, lanes], outs[2 + array].at[pl.ds(row, SPAN), pl.ds(column, length)]))
    moves = [
        (pltpu.make_async_copy(a, b, reads.at[k]), pltpu.make_async_copy(b, c, writes.at[k])) for k, (a, b, c) in enumerate(copies)
    ]
    for read, write in moves:
        read.start()
    row = 0
    for out in outs[6:]:
        out[...] = small[0, pl.ds(row, out.shape[0])]
        row += out.shape[0]
    for read, write in moves:
        read.wait()
        write.start()
    for read, write in moves:
        write.wait()


def settle(mixed, tokens, units, small, hidden, inner):
    width = tokens.shape[-1]
    parts = hidden // UNIT
    feeds = inner // SPAN
    places = []
    for f in range(feeds):
        places += [(2 * f, SPAN, 3, f * SPAN, 0), (2 * f + 1, SPAN, 2, 0, f * SPAN)]
    places += [(2 * feeds + j, SPAN, 1, j * SPAN, 0) for j in range(hidden // SPAN)]
    for j in range(parts):
        places += [(len(places) + k, UNIT, 0, 0, k * hidden + j * UNIT) for k in range(3)]
    anywhere = pl.BlockSpec(memory_space=pl.ANY)
    vmem = pl.BlockSpec(memory_space=pltpu.VMEM)
    shape = jax.ShapeDtypeStruct
    lengths = (width, hidden, hidden, width, inner, width)
    return pl.pallas_call(
        functools.partial(settle_kernel, places),
        out_shape=(
            shape(mixed.shape, mixed.dtype), shape(tokens.shape, F32), shape((width, 3 * hidden), F32), shape((hidden, width), F32),
            shape((width, inner), F32), shape((inner, width), F32), *(shape((n // 128, 128), F32) for n in lengths),
        ),
        in_specs=[anywhere] * 3 + [vmem],
        out_specs=(anywhere,) * 6 + (vmem,) * 6,
        scratch_shapes=[
            pltpu.VMEM(mixed.shape, mixed.dtype), pltpu.VMEM(tokens.shape, F32), pltpu.VMEM(units.shape, F32),
            pltpu.SemaphoreType.DMA((mixed.shape[0] // 2 + len(places),)), pltpu.SemaphoreType.DMA((mixed.shape[0] // 2 + len(places),)),
        ],
        compiler_params=pltpu.CompilerParams(vmem_limit_bytes=48 * 2**20),
        name="settle",
    )(mixed, tokens, units, small)


def on_device(tokens, cotangent, reset_pos, norm1_gain, w_in, forget_bias, input_bias, w_out, norm2_gain, w_up, up_bias, w_down, down_bias):
    ringed = lax.axis_size("seq") == 8 and lax.axis_size("rows") == 4
    hidden, inner = w_out.shape[0], w_down.shape[0]
    kept = front(tokens, cotangent, reset_pos, norm1_gain, w_in, forget_bias, input_bias, w_out)
    mixed, grad_tokens, units, small = back(
        ringed, tokens.shape, *kept, norm1_gain, norm2_gain, up_bias, down_bias, w_in, w_out, w_up, w_down
    )
    if not ringed:
        units, small = lax.psum((units, small), ("seq", "rows"))
    mixed, grad_tokens, grad_in, grad_out, grad_up, grad_down, *rest = settle(mixed, grad_tokens, units, small, hidden, inner)
    norm_one, forget, inputs, norm_two, up, down = (one.reshape(-1) for one in rest)
    return mixed, grad_tokens, norm_one, grad_in, forget, inputs, grad_out, norm_two, grad_up, up, grad_down, down


def solution(mesh):
    return jax.shard_map(
        on_device,
        mesh=mesh,
        in_specs=(
            P("rows", "seq", None),
            P("rows", "seq", None),
            P("rows", None),
            P(),
            P(),
            P(),
            P(),
            P(),
            P(),
            P(),
            P(),
            P(),
            P(),
        ),
        out_specs=(
            P("rows", "seq", None),
            P("rows", "seq", None),
            P(),
            P(),
            P(),
            P(),
            P(),
            P(),
            P(),
            P(),
            P(),
            P(),
        ),
        check_vma=False,
    )
```

```python
import functools
import math
import jax
import jax.numpy as jnp
from jax import lax
from jax.experimental import pallas as pl
from jax.experimental.pallas import tpu as pltpu
from jax.sharding import PartitionSpec as P

MESH = pl.DeviceIdType.MESH
EPS = 1e-6
F32 = jnp.float32
BF16 = jnp.bfloat16
STAGES = 13
KINDS = 10
SPAN = 512
UNIT = 256
WIDE = 512
SLOTS = 10
SIDE = 2
SMALL_ROWS = 48
DOUBLINGS = 5
SLOW = (0, 1, 3, 6, 8, 10, 11, 12, 14, 16, 19, 21, 22)
FAST = (0, 1, 4, 8, 11, 13, 15, 17, 19, 22, 26, 29, 30)


def place():
    seq = lax.axis_index("seq")
    rows = lax.axis_index("rows")
    return lax.div(rows, 2), lax.rem(seq, 2), lax.div(seq, 2), lax.rem(rows, 2)


def spot(x, y, z, core):
    return (z * 2 + y, x * 2 + core)


def dot(left, right):
    return jnp.dot(left, right, preferred_element_type=F32)


def dot_nt(left, right):
    return lax.dot_general(left, right, (((1,), (1,)), ((), ())), preferred_element_type=F32)


def dot_tn(left, right):
    return lax.dot_general(left, right, (((0,), (0,)), ((), ())), preferred_element_type=F32)


class Chain:
    def __init__(self, count, sign, sent, got, join, send, recv):
        self.count, self.sign = count, sign
        self.sent, self.got, self.join = sent, got, join
        self.send, self.recv = send, recv
        self.rounds = max(1, math.ceil(math.log2(count)))
        seq = lax.axis_index("seq")
        self.seq = seq
        self.place = seq if sign > 0 else count - 1 - seq

    def partners(self):
        for r in range(self.rounds):
            far = 2**r
            yield self.seq + self.sign * far, self.place + far < self.count
            yield self.seq - self.sign * far, self.place >= far

    def copy(self, part, r, other):
        return pltpu.make_async_remote_copy(
            src_ref=self.sent.at[part, r], dst_ref=self.got.at[part, r],
            send_sem=self.send.at[part, r], recv_sem=self.recv.at[part, r],
            device_id=(other, lax.axis_index("rows")), device_id_type=MESH,
        )

    def push(self, part, r):
        @pl.when(self.place + 2**r < self.count)
        def _():
            self.copy(part, r, self.seq + self.sign * 2**r).start()

    def start(self, part, product, end):
        self.sent[part, 0, 0] = product
        self.sent[part, 0, 1] = end
        self.join[part, 0] = jnp.ones_like(product)
        self.join[part, 1] = jnp.zeros_like(end)
        self.push(part, 0)

    def advance(self, part, r):
        last = r == self.rounds - 1

        @pl.when(self.place >= 2**r)
        def _():
            self.copy(part, r, self.seq - self.sign * 2**r).wait_recv()
            product, end = self.got[part, r, 0], self.got[part, r, 1]
            own = self.join[part, 0]
            self.join[part, 1] = self.join[part, 1] + own * end
            if not last:
                self.join[part, 0] = own * product
                here = self.sent[part, r, 0]
                self.sent[part, r + 1, 0] = here * product
                self.sent[part, r + 1, 1] = self.sent[part, r, 1] + here * end

        if not last:
            @pl.when(self.place < 2**r)
            def _():
                self.sent[part, r + 1] = self.sent[part, r]
            self.push(part, r + 1)

    def finish(self, part):
        for r in range(self.rounds):
            @pl.when(self.place + 2**r < self.count)
            def _():
                self.copy(part, r, self.seq + self.sign * 2**r).wait_send()


def greet_chain(chain):
    barrier = pltpu.get_barrier_semaphore()
    rows = lax.axis_index("rows")
    total = 0
    for other, there in chain.partners():
        @pl.when(there)
        def _():
            pl.semaphore_signal(barrier, inc=1, device_id=(other, rows), device_id_type=MESH)
        total = total + jnp.where(there, 1, 0)
    return barrier, total


def chain_scratch(parts, count, rows, width):
    rounds = max(1, math.ceil(math.log2(count)))
    return [
        pltpu.VMEM((parts, rounds, 2, rows, width), F32),
        pltpu.VMEM((parts, rounds, 2, rows, width), F32),
        pltpu.VMEM((parts, 2, rows, width), F32),
        pltpu.SemaphoreType.DMA((parts, rounds)),
        pltpu.SemaphoreType.DMA((parts, rounds)),
    ]


def front_kernel(
    count, rows, steps, chunk, block,
    tokens, cotangent, reset, gain, w_in, forget_bias, input_bias, w_out,
    x_out, cot_out, middle_out, state_out, decay_out, fade_out, rise_out, weight_out, lean_out,
    tok_v, cot_v, x_v, normed_v, w_v, w_out_v, keep_v, decay_v, update_v, cand_v, fade_v, rise_v, weight_v, lean_v, state_v, middle_v,
    sent, got, join, send, recv, sems, out_sems,
):
    total, width = x_v.shape
    hidden = w_out_v.shape[0]
    parts = hidden // chunk
    size = block * rows
    blocks = steps // block
    chain = Chain(count, 1, sent, got, join, send, recv)
    barrier, greeted = greet_chain(chain)
    loads = [pltpu.make_async_copy(tokens, tok_v, sems.at[0])]
    for j in range(parts):
        for k in range(3):
            loads.append(pltpu.make_async_copy(w_in.at[:, pl.ds(k * hidden + j * chunk, chunk)], w_v.at[j, :, pl.ds(k * chunk, chunk)], sems.at[1 + 3 * j + k]))
    loads.append(pltpu.make_async_copy(cotangent, cot_v, sems.at[1 + 3 * parts]))
    loads.append(pltpu.make_async_copy(w_out, w_out_v, sems.at[2 + 3 * parts]))
    for load in loads:
        load.start()
    loads[0].wait()

    first = lax.axis_index("seq") * steps
    marks = [jnp.broadcast_to(reset[:, k : k + 1], (rows, 128)) for k in range(reset.shape[1])]

    def mark(t, carry):
        hit = marks[0] == first + t
        for one in marks[1:]:
            hit = hit | (one == first + t)
        keep_v[pl.ds(pl.multiple_of(t * rows, rows), rows)] = jnp.where(hit, 0.0, 1.0)
        return carry

    lax.fori_loop(0, steps, mark, 0, unroll=4)
    gains = gain[...]

    def norm(b, carry):
        at = pl.ds(pl.multiple_of(b * size, size), size)
        x = tok_v[:, pl.ds(pl.multiple_of(b * block, block), block), :].astype(F32)
        x = jnp.swapaxes(x, 0, 1).reshape(size, width)
        x_v[at] = x.astype(BF16)
        scale = lax.rsqrt(jnp.mean(x * x, axis=-1, keepdims=True) + EPS)
        normed_v[at] = (x * scale * gains).astype(BF16)
        return carry

    lax.fori_loop(0, blocks, norm, 0)
    outs = [pltpu.make_async_copy(x_v, x_out, out_sems.at[0])]
    outs[0].start()

    def gates(j):
        lanes = pl.ds(j * chunk, chunk)
        shift_f, shift_i = -forget_bias[:, lanes], -input_bias[:, lanes]

        def some(project, at, product, end):
            neg_f = shift_f - project[:, :chunk]
            neg_i = shift_i - project[:, chunk : 2 * chunk]
            cand = project[:, 2 * chunk :]
            lower = jnp.maximum(jnp.minimum(neg_f, neg_i) - 20.0, 0.0)
            exp_f = jnp.exp(jnp.minimum(neg_f - lower, 80.0))
            exp_i = jnp.exp(jnp.minimum(neg_i - lower, 80.0))
            one_f, one_i = 1.0 + exp_f, 1.0 + exp_i
            share = 1.0 / (one_f + one_i)
            decay, weight = one_i * share, one_f * share
            fade_v[j % 2, at] = (decay * (exp_f * share)).astype(BF16)
            rise_v[j % 2, at] = (weight * (exp_i * share)).astype(BF16)
            weight_v[j % 2, at] = weight.astype(BF16)
            cand_v[at, lanes] = cand
            update = weight * cand
            update_v[at, lanes] = update
            decay = decay * jnp.concatenate([keep_v[at]] * (chunk // 128), axis=1)
            decay_v[at, lanes] = decay
            for t in range(block):
                here = decay[t * rows : (t + 1) * rows]
                end = here * end + update[t * rows : (t + 1) * rows]
                product = here * product
            return product, end

        def one(b, carry):
            places = [pl.ds(pl.multiple_of((b * SIDE + k) * size, size), size) for k in range(SIDE)]
            for at in places:
                carry = some(dot(normed_v[at], w_v[j]), at, *carry)
            return carry

        start = (jnp.ones((rows, chunk), F32), jnp.zeros((rows, chunk), F32))
        return lax.fori_loop(0, blocks // SIDE, one, start)

    def scan(j):
        lanes = pl.ds(j * chunk, chunk)

        def one(b, state):
            for t in range(block):
                here = pl.ds(pl.multiple_of(b * size + t * rows, rows), rows)
                keep = jnp.concatenate([keep_v[here]] * (chunk // 128), axis=1)
                lean_v[j % 2, here] = (keep * state - cand_v[here, lanes]).astype(BF16)
                state = decay_v[here, lanes] * state + update_v[here, lanes]
                state_v[here, lanes] = state.astype(BF16)
            return state

        lax.fori_loop(0, blocks, one, join[j, 1])

    def project_out(b, carry):
        at = pl.ds(pl.multiple_of(b * 2 * size, 2 * size), 2 * size)
        middle_v[at] = x_v[at].astype(F32) + dot(state_v[at], w_out_v[...])
        copy = pltpu.make_async_copy(middle_v.at[at], middle_out.at[at], out_sems.at[2 + 6 * parts])
        copy.start()
        return carry

    def put(source, target, slot, wait=False):
        copy = pltpu.make_async_copy(source, target, out_sems.at[slot])
        if wait:
            copy.wait()
        else:
            copy.start()

    def gate_outs(j, wait=False):
        lanes = pl.ds(j * chunk, chunk)
        for k, (a, b) in enumerate(((fade_v, fade_out), (rise_v, rise_out), (weight_v, weight_out))):
            put(a.at[j % 2], b.at[:, lanes], 1 + 3 * j + k, wait)
        put(decay_v.at[:, lanes], decay_out.at[:, lanes], 1 + 3 * parts + j, wait)

    def scan_outs(j, wait=False):
        lanes = pl.ds(j * chunk, chunk)
        put(lean_v.at[j % 2], lean_out.at[:, lanes], 1 + 4 * parts + 2 * j, wait)
        put(state_v.at[:, lanes], state_out.at[:, lanes], 2 + 4 * parts + 2 * j, wait)

    ready = 0
    for j in range(parts):
        for k in range(3):
            loads[1 + 3 * j + k].wait()
        if j >= 2:
            gate_outs(j - 2, True)
        product, end = gates(j)
        gate_outs(j)
        if j == 0:
            pl.semaphore_wait(barrier, greeted)
        chain.start(j, product, end)
        for i in range(j - 1, -1, -1):
            if j - 1 - i < chain.rounds:
                chain.advance(i, j - 1 - i)
    for k in range(2):
        loads[1 + 3 * parts + k].wait()

    def turn(b, carry):
        at = pl.ds(pl.multiple_of(b * size, size), size)
        c = cot_v[:, pl.ds(pl.multiple_of(b * block, block), block), :].astype(F32)
        normed_v[at] = jnp.swapaxes(c, 0, 1).reshape(size, width).astype(BF16)
        return carry

    lax.fori_loop(0, blocks, turn, 0)
    put(normed_v, cot_out, 1 + 6 * parts)

    step = parts - 1
    while ready < parts:
        for i in range(parts - 1, -1, -1):
            if 0 <= step - 1 - i < chain.rounds and step >= parts:
                chain.advance(i, step - 1 - i)
        while ready < parts and ready + chain.rounds <= step:
            if ready >= 2:
                scan_outs(ready - 2, True)
            scan(ready)
            scan_outs(ready)
            ready += 1
        step += 1
    lax.fori_loop(0, blocks // 2, project_out, 0)
    for j in range(parts):
        if j >= parts - 2:
            gate_outs(j, True)
            scan_outs(j, True)
        chain.finish(j)
    outs[0].wait()
    put(normed_v, cot_out, 1 + 6 * parts, True)
    put(middle_v, middle_out, 2 + 6 * parts, True)


def front(tokens, cotangent, reset, gain, w_in, forget_bias, input_bias, w_out, cid=1):
    rows, steps, width = tokens.shape
    hidden = w_out.shape[0]
    total = rows * steps
    count = lax.axis_size("seq")
    chunk, block = 256, 16
    parts = hidden // chunk
    anywhere = pl.BlockSpec(memory_space=pl.ANY)
    vmem = pl.BlockSpec(memory_space=pltpu.VMEM)
    shape = jax.ShapeDtypeStruct
    return pl.pallas_call(
        functools.partial(front_kernel, count, rows, steps, chunk, block),
        out_shape=(
            shape((total, width), BF16), shape((total, width), BF16), shape((total, width), F32),
            shape((total, hidden), BF16), shape((total, hidden), F32), shape((total, hidden), BF16),
            shape((total, hidden), BF16), shape((total, hidden), BF16), shape((total, hidden), BF16),
        ),
        in_specs=[anywhere, anywhere, vmem, vmem, anywhere, vmem, vmem, anywhere],
        out_specs=(anywhere,) * 9,
        scratch_shapes=[
            pltpu.VMEM(tokens.shape, BF16), pltpu.VMEM(tokens.shape, BF16), pltpu.VMEM((total, width), BF16), pltpu.VMEM((total, width), BF16),
            pltpu.VMEM((parts, width, 3 * chunk), BF16), pltpu.VMEM(w_out.shape, BF16), pltpu.VMEM((total, 128), F32),
            pltpu.VMEM((total, hidden), F32), pltpu.VMEM((total, hidden), F32), pltpu.VMEM((total, hidden), F32),
            pltpu.VMEM((2, total, chunk), BF16), pltpu.VMEM((2, total, chunk), BF16), pltpu.VMEM((2, total, chunk), BF16),
            pltpu.VMEM((2, total, chunk), BF16), pltpu.VMEM((total, hidden), BF16), pltpu.VMEM((total, width), F32),
            *chain_scratch(parts, count, rows, chunk),
            pltpu.SemaphoreType.DMA((3 + 3 * parts,)), pltpu.SemaphoreType.DMA((3 + 6 * parts,)),
        ],
        compiler_params=pltpu.CompilerParams(collective_id=cid, has_side_effects=True, vmem_limit_bytes=62 * 2**20),
        cost_estimate=pl.CostEstimate(flops=2 * total * width * 4 * hidden, bytes_accessed=40 * 2**20, transcendentals=3 * total * hidden),
        name="front",
    )(tokens, cotangent, reset, gain.reshape(1, -1), w_in, forget_bias.reshape(1, -1), input_bias.reshape(1, -1), w_out)


class Summing:
    def __init__(self, plan, grads, half_in, part_in, lines_in, last_in, send, recv, local, free, result):
        self.plan, self.grads = plan, grads
        self.whole = sum(width == WIDE for slot, column, width in plan)
        self.half_in, self.part_in, self.lines_in, self.last_in = half_in, part_in, lines_in, last_in
        self.result, self.send, self.recv, self.local, self.free = result, send, recv, local, free
        x, y, z, core = place()
        self.z = z
        first = core == 0
        self.sibling = spot(x, y, z, 1 - core)
        along_x, along_y = spot(1 - x, y, z, core), spot(x, 1 - y, z, core)
        self.near = tuple(jnp.where(first, a, b) for a, b in zip(along_x, along_y))
        self.far = tuple(jnp.where(first, b, a) for a, b in zip(along_x, along_y))
        self.above = spot(x, y, z + 1, core)
        self.below = spot(x, y, z - 1, core)
        near_bit = jnp.where(first, x, y)
        far_bit = jnp.where(first, y, x)
        self.n_half, self.n_part, self.n_line, self.n_tip = SPAN // 2, SPAN // 4, SPAN // 16, SPAN // 32
        self.half = core * self.n_half
        self.other_half = (1 - core) * self.n_half
        self.part = self.half + near_bit * self.n_part
        self.other_part = self.half + (1 - near_bit) * self.n_part
        self.tip = self.part + self.n_line * z + self.n_tip * far_bit
        self.other_tip = self.part + self.n_line * z + self.n_tip * (1 - far_bit)

    def copy(self, kind, unit, source, target, device):
        return pltpu.make_async_remote_copy(
            src_ref=source, dst_ref=target, send_sem=self.send.at[kind, unit], recv_sem=self.recv.at[kind, unit],
            device_id=device, device_id_type=MESH,
        )

    def slot_of(self, u):
        return self.plan[u] if isinstance(u, int) else (u, 0, WIDE)

    def rows(self, u, start, count):
        slot, column, width = self.slot_of(u)
        return self.grads.at[slot, pl.ds(pl.multiple_of(start, 8), count), pl.ds(column, width)]

    def done(self, u, start, count):
        return self.result.at[u, pl.ds(pl.multiple_of(start, 8), count), pl.ds(0, self.slot_of(u)[2])]

    def land(self, ref, wide, u, start, count):
        if self.slot_of(u)[2] == WIDE:
            return ref.at[lax.rem(u, wide), pl.ds(start, count)]
        turn = (u - self.whole) % (2 * (ref.shape[0] - wide))
        return ref.at[wide + turn // 2, pl.ds(start, count), pl.ds(turn % 2 * UNIT, UNIT)]

    def turns(self, kind, u):
        ref, wide = ((self.half_in, 2), (self.part_in, 3), (self.lines_in, 3), (self.lines_in, 3))[kind]
        if self.slot_of(u)[2] == WIDE:
            return wide, 0, self.whole
        return 2 * (ref.shape[0] - wide), self.whole, len(self.plan)

    def claim(self, kind, u):
        apart, first, last = self.turns(kind, u)
        if isinstance(u, int):
            if u - apart >= first:
                pl.semaphore_wait(self.free.at[kind, u - apart], 1)
        else:
            @pl.when(u >= apart)
            def _():
                pl.semaphore_wait(self.free.at[kind, u - apart], 1)

    def release(self, kind, u, sender):
        apart, first, last = self.turns(kind, u)

        def signal():
            pl.semaphore_signal(self.free.at[kind, u], inc=1, device_id=sender, device_id_type=MESH)

        if isinstance(u, int):
            if u + apart < last:
                signal()
        else:
            pl.when(u + apart < last)(signal)

    def land_half(self, u):
        return self.land(self.half_in, 2, u, 0, self.n_half)

    def land_part(self, u):
        return self.land(self.part_in, 3, u, 0, self.n_part)

    def land_up(self, u, z):
        return self.land(self.lines_in, 3, u, 0, self.n_line * (4 - z))

    def land_down(self, u, z):
        return self.land(self.lines_in, 3, u, self.n_line * (4 - z) if z > 0 else 0, self.n_line * (z + 1))

    def land_last(self, u):
        return self.land(self.last_in, self.whole, u, 0, self.n_tip)

    def c_half(self, u):
        return self.copy(0, u, self.rows(u, self.other_half, self.n_half), self.land_half(u), self.sibling)

    def c_part(self, u):
        return self.copy(1, u, self.rows(u, self.other_part, self.n_part), self.land_part(u), self.near)

    def c_up(self, u, z):
        low, rest = self.n_line * (z + 1), self.n_line * (3 - z)
        return self.copy(2, u, self.rows(u, self.part + low, rest), self.land_up(u, z + 1), self.above)

    def c_down(self, u, z):
        rest = self.n_line * z
        return self.copy(3, u, self.rows(u, self.part, rest), self.land_down(u, z - 1), self.below)

    def c_last(self, u):
        return self.copy(4, u, self.rows(u, self.other_tip, self.n_tip), self.land_last(u), self.far)

    def c_own(self, u):
        return pltpu.make_async_copy(self.rows(u, self.tip, self.n_tip), self.done(u, self.tip, self.n_tip), self.local.at[u])

    def c_far(self, u, start):
        return self.copy(5, u, self.rows(u, start, self.n_tip), self.done(u, start, self.n_tip), self.far)

    def c_rise(self, u, z):
        piece = self.done(u, self.part, self.n_line * (z + 1))
        return self.copy(6, u, piece, piece, self.above)

    def c_fall(self, u, z):
        piece = self.done(u, self.part + self.n_line * z, self.n_line * (4 - z))
        return self.copy(7, u, piece, piece, self.below)

    def c_near(self, u, start):
        piece = self.done(u, start, self.n_part)
        return self.copy(8, u, piece, piece, self.near)

    def c_sibling(self, u, start):
        piece = self.done(u, start, self.n_half)
        return self.copy(9, u, piece, piece, self.sibling)

    def add(self, u, start, count, ref):
        slot, column, width = self.slot_of(u)
        step = min(count, 128)
        lanes = pl.ds(column, width)

        def one(i, carry):
            here = pl.ds(pl.multiple_of(start + i * step, 8), step)
            there = pl.ds(pl.multiple_of(i * step, 8), step)
            self.grads[slot, here, lanes] = self.grads[slot, here, lanes] + ref[there]
            return carry

        if count == step:
            one(0, 0)
        else:
            lax.fori_loop(0, count // step, one, 0)

    def settle_sums(self, units):
        def sent(k):
            for u in units:
                if k < 3:
                    self.c_up(u, k).wait_send()
                if k > 0:
                    self.c_down(u, k).wait_send()

        self.at_each(sent)

    def settle_lines(self, units):
        def sent(k):
            for u in units:
                if k < 3:
                    self.c_rise(u, k).wait_send()
                if k > 0:
                    self.c_fall(u, k).wait_send()

        self.at_each(sent)

    def at_each(self, action):
        for k in range(4):
            pl.when(self.z == k)(functools.partial(action, k))

    def stage(self, s, u):
        z = self.z
        if s == 0:
            self.claim(0, u)
            self.c_half(u).start()
        elif s == 1:
            self.c_half(u).wait()
            self.add(u, self.half, self.n_half, self.land_half(u))
            self.release(0, u, self.sibling)
            self.claim(1, u)
            self.c_part(u).start()
        elif s == 2:
            self.c_part(u).wait()
            self.add(u, self.part, self.n_part, self.land_part(u))
            self.release(1, u, self.near)
        if 2 <= s <= 5:
            up, down = s - 2, 5 - s

            @pl.when(z == up)
            def _():
                if up > 0:
                    self.c_up(u, up - 1).wait_recv()
                    low, rest = self.n_line * up, self.n_line * (4 - up)
                    self.add(u, self.part + low, rest, self.land_up(u, up))
                    self.release(2, u, self.below)
                if up < 3:
                    self.claim(2, u)
                    self.c_up(u, up).start()

            @pl.when(z == down)
            def _():
                if down < 3:
                    self.c_down(u, down + 1).wait_recv()
                    rest = self.n_line * (down + 1)
                    self.add(u, self.part, rest, self.land_down(u, down))
                    self.release(3, u, self.above)
                if down > 0:
                    self.claim(3, u)
                    self.c_down(u, down).start()
        if s == 5:
            self.c_last(u).start()
        elif s == 6:
            self.c_last(u).wait()
            self.add(u, self.tip, self.n_tip, self.land_last(u))
            self.c_far(u, self.tip).start()
            self.c_own(u).start()
        elif s == 7:
            self.c_far(u, self.tip).wait_send()
            self.c_far(u, self.other_tip).wait_recv()
            self.c_own(u).wait()
        if 7 <= s <= 10:
            up, down = s - 7, 10 - s

            @pl.when(z == up)
            def _():
                if up > 0:
                    self.c_rise(u, up - 1).wait_recv()
                if up < 3:
                    self.c_rise(u, up).start()

            @pl.when(z == down)
            def _():
                if down < 3:
                    self.c_fall(u, down + 1).wait_recv()
                if down > 0:
                    self.c_fall(u, down).start()
        if s == 10:
            self.c_near(u, self.part).start()
        elif s == 11:
            self.c_near(u, self.part).wait_send()
            self.c_near(u, self.other_part).wait_recv()
            self.c_sibling(u, self.half).start()
        elif s == 12:
            self.c_sibling(u, self.half).wait_send()
            self.c_sibling(u, self.other_half).wait_recv()


def sum_scratch(units, whole, slots):
    pairs = (units - whole + 1) // 2
    return [
        pltpu.VMEM((slots, SPAN, WIDE), F32),
        pltpu.VMEM((2 + min(pairs, 2), SPAN // 2, WIDE), F32),
        pltpu.VMEM((3 + min(pairs, 4), SPAN // 4, WIDE), F32),
        pltpu.VMEM((3 + pairs, 5 * SPAN // 16, WIDE), F32),
        pltpu.VMEM((whole + pairs, SPAN // 32, WIDE), F32),
        pltpu.SemaphoreType.DMA((KINDS, units)),
        pltpu.SemaphoreType.DMA((KINDS, units)),
        pltpu.SemaphoreType.DMA((units,)),
        pltpu.SemaphoreType.REGULAR((4, units)),
    ]


class Doubling:
    def __init__(self, own, got, send, recv):
        self.own, self.got, self.send, self.recv = own, got, send, recv
        x, y, z, core = place()
        self.partners = (
            spot(x, y, z, 1 - core), spot(1 - x, y, z, core), spot(x, 1 - y, z, core),
            spot(x, y, z + 1 - 2 * lax.rem(z, 2), core), spot(x, y, z + 2 - 4 * lax.div(z, 2), core),
        )

    def copy(self, k):
        return pltpu.make_async_remote_copy(
            src_ref=self.own.at[k], dst_ref=self.got.at[k], send_sem=self.send.at[k], recv_sem=self.recv.at[k],
            device_id=self.partners[k], device_id_type=MESH,
        )

    def step(self, k):
        if k > 0:
            self.copy(k - 1).wait()
            self.own[k] = self.own[k - 1] + self.got[k - 1]
        if k < DOUBLINGS:
            self.copy(k).start()


def greet_ring(ring):
    barrier = pltpu.get_barrier_semaphore()
    for there in (ring.sibling, ring.near, ring.far):
        pl.semaphore_signal(barrier, inc=1, device_id=there, device_id_type=MESH)

    @pl.when(ring.z > 0)
    def _():
        pl.semaphore_signal(barrier, inc=1, device_id=ring.below, device_id_type=MESH)

    @pl.when(ring.z < 3)
    def _():
        pl.semaphore_signal(barrier, inc=1, device_id=ring.above, device_id_type=MESH)

    return 3 + jnp.where(ring.z > 0, 1, 0) + jnp.where(ring.z < 3, 1, 0)


GELU_A = math.sqrt(2.0 / math.pi)
GELU_B = GELU_A * 0.044715


def back_kernel(
    ringed, count, rows, steps, plan, block,
    x_in, cot_in, middle_in, state_in, decay_in, fade_in, rise_in, weight_in, lean_in,
    gain_one, gain_two, up_bias, down_bias, w_in, w_out, w_up, w_down,
    mixed_out, tokens_out, result, small_out,
    middle_v, second_v, mixed_v, state_v, cot_v, x_v, low_v, cand_v, turned_v, w_in_v, w_out_v, w_up_v, w_down_v,
    decay_s, fade_s, rise_s, weight_s, lean_s, mixed_s, tokens_s, sums_v,
    load_sems, stream_sems, stage_sems,
    sent, got, join, send, recv,
    *ring_refs,
):
    total, width = x_v.shape
    hidden = w_out_v.shape[0]
    inner = w_down_v.shape[0]
    size = block * rows
    blocks = steps // block
    wide = UNIT
    parts = hidden // wide
    big = 512
    per = total // big
    feeds = inner // SPAN
    chain = Chain(count, -1, sent, got, join, send, recv)
    barrier, greeted = greet_chain(chain)
    grads, own_v = ring_refs[:2]
    if ringed:
        ring = Summing(plan, grads, *ring_refs[2:10], result)
        small = Doubling(own_v, *ring_refs[10:])
        greeted = greeted + greet_ring(ring)
    small_v = own_v.at[0]

    inner_columns = pl.ds(0, inner)
    rest_columns = pl.ds(inner, w_in.shape[1] - inner)
    loads = [
        pltpu.make_async_copy(source, target, load_sems.at[k])
        for k, (source, target) in enumerate((
            (middle_in, middle_v), (w_up, w_up_v), (cot_in, cot_v), (w_down, w_down_v), (state_in, state_v),
            (w_out, w_out_v), (x_in, x_v), (w_in.at[:, rest_columns], w_in_v), (w_in.at[:, inner_columns], w_up_v),
        ))
    ]
    loads[0].start()

    def at_block(b, n=size):
        return pl.ds(pl.multiple_of(b * n, n), n)

    due = {}
    clock = [0.0]

    def travel(unit, s):
        return 2.0 * (SLOW[s] - SLOW[s - 1]) if plan[unit][2] == WIDE else 1.0 * (FAST[s] - FAST[s - 1])

    def enter(unit):
        due[unit] = (0, clock[0])

    def tick(passed):
        clock[0] += passed
        for unit in sorted(due):
            s, when = due[unit]
            if s < STAGES and when <= clock[0] + 1e-6:
                if ringed:
                    ring.stage(s, unit)
                due[unit] = (s + 1, clock[0] + travel(unit, s + 1) if s + 1 < STAGES else 0.0)

    def rolling_tick(i, half):
        for s in reversed(range(STAGES)):
            behind = SLOW[s] + early - half
            if ringed and behind % 2 == 0 and behind // 2 < feeds * per // 2:
                pl.when(i >= behind // 2)(functools.partial(ring.stage, s, i - behind // 2))

    def beat(number, body, ticks, passed, *carry):
        each = number // ticks
        for k in range(ticks):
            carry = lax.fori_loop(each * k, each * k + each, lambda i, c: body(i, *c), carry)
            tick(passed / ticks)
        return carry

    def put_unit(unit):
        if not ringed:
            slot, column, length = plan[unit] if isinstance(unit, int) else (unit, 0, WIDE)
            copy = pltpu.make_async_copy(
                grads.at[slot, :, pl.ds(column, length)], result.at[unit, :, pl.ds(0, length)], load_sems.at[0]
            )
            copy.start()
            copy.wait()

    sums_v[...] = jnp.zeros_like(sums_v)
    small_v[...] = jnp.zeros_like(small_v)

    def put_small(row, value):
        for k in range(value.shape[1] // 128):
            small_v[pl.ds(row + k, 1)] = value[:, 128 * k : 128 * k + 128]

    def gather(slot, value, fresh):
        grads[slot] = jnp.where(fresh, 0.0, grads[slot]) + value

    loads[0].wait()
    for k in (1, 2, 3):
        loads[k].start()
    gains = gain_two[...]
    bias = down_bias[...]

    def norm_two(b, carry):
        at = at_block(b)
        value = middle_v[at]
        scale = lax.rsqrt(jnp.mean(value * value, axis=-1, keepdims=True) + EPS)
        normed = value * scale * gains
        low_v[at] = normed.astype(BF16)
        turned_v[:, at] = jnp.swapaxes(normed, 0, 1).astype(BF16)
        mixed_v[at] = value + bias
        second_v[at] = jnp.zeros_like(value)
        return carry

    lax.fori_loop(0, blocks, norm_two, 0)
    for k in (1, 2, 3):
        loads[k].wait()
    for k in (4, 5, 6, 7):
        loads[k].start()
    pl.semaphore_wait(barrier, greeted)

    def feed(f, tok):
        at = at_block(tok, big)
        lanes = pl.ds(pl.multiple_of(f * SPAN, SPAN), SPAN)
        cot = cot_v[at]
        pre = dot(low_v[at], w_up_v[:, lanes]) + up_bias[:, lanes]
        back_act = dot_nt(cot, w_down_v[lanes])
        square = pre * pre
        gate = 0.5 * jnp.tanh(pre * (GELU_A + GELU_B * square)) + 0.5
        act = pre * gate
        slope = gate + act * (1.0 - gate) * (2.0 * GELU_A + 6.0 * GELU_B * square)
        back_up = back_act * slope
        sums_v[0:1, lanes] = sums_v[0:1, lanes] + jnp.sum(back_up, axis=0, keepdims=True)
        act, back_up = act.astype(BF16), back_up.astype(BF16)
        mixed_v[at] = mixed_v[at] + dot(act, w_down_v[lanes])
        second_v[at] = second_v[at] + dot_nt(back_up, w_up_v[:, lanes])
        gather(2 * f, dot_tn(act, cot), tok == 0)
        gather(2 * f + 1, dot(turned_v[:, at], back_up), tok == 0)

    early = per - 1

    def feed_pair(i, carry):
        f, tok = lax.div(2 * i, per), lax.rem(2 * i, per)
        for half in range(2):
            feed(f, tok + half)
            if half == 1:
                @pl.when(tok + 2 == per)
                def _():
                    put_unit(2 * f)
                    put_unit(2 * f + 1)
            rolling_tick(i, half)
        return carry

    lax.fori_loop(0, feeds * per // 2, feed_pair, 0)
    clock[0] = 2.0 * (feeds * per - 1 - early)
    for u in range(2 * feeds):
        stages = [s for s in range(STAGES) if 4.0 * u + 2.0 * SLOW[s] > clock[0]]
        due[u] = (stages[0], 4.0 * u + 2.0 * SLOW[stages[0]])

    loads[8].start()

    def decays(j):
        slot = j % 2
        return pltpu.make_async_copy(decay_in.at[:, pl.ds(j * wide, wide)], decay_s.at[slot], stream_sems.at[0, slot])

    decays(0).start()
    decays(1).start()

    def stage_copy(buffer, target, b):
        slot = lax.rem(b, 2)
        return pltpu.make_async_copy(buffer.at[slot], target.at[:, pl.ds(pl.multiple_of(b * block, block), block), :], stage_sems.at[slot])

    def finish_two(b, norm_sum, cot_sum):
        at = at_block(b)

        @pl.when(b >= 2)
        def _():
            stage_copy(mixed_s, mixed_out, b - 2).wait()
        mixed = jnp.swapaxes(mixed_v[at].reshape(block, rows, width), 0, 1)
        mixed_s[lax.rem(b, 2)] = mixed.astype(BF16)
        stage_copy(mixed_s, mixed_out, b).start()
        value, grad, cot = middle_v[at], second_v[at], cot_v[at].astype(F32)
        scale = lax.rsqrt(jnp.mean(value * value, axis=-1, keepdims=True) + EPS)
        plain = value * scale
        norm_sum = norm_sum + jnp.sum((grad * plain).reshape(size // 8, 8, width), axis=0)
        cot_sum = cot_sum + jnp.sum(cot.reshape(size // 8, 8, width), axis=0)
        lean = grad * gains
        back = cot + scale * (lean - plain * jnp.mean(lean * plain, axis=-1, keepdims=True))
        second_v[at] = back
        low_v[at] = back.astype(BF16)
        return norm_sum, cot_sum

    zero = jnp.zeros((8, width), F32)
    norm_sum, cot_sum = beat(blocks, finish_two, 2, 2.4, zero, zero)
    for b in (blocks - 2, blocks - 1):
        stage_copy(mixed_s, mixed_out, b).wait()
    put_small(20, jnp.sum(norm_sum, axis=0, keepdims=True))
    put_small(24, sums_v[0:1])
    put_small(40, jnp.sum(cot_sum, axis=0, keepdims=True))

    loads[4].wait()
    loads[5].wait()

    def stream(buffer, source, j, i, k):
        slot = lax.rem(i, 4)
        lanes = pl.ds(j * wide, wide)
        return pltpu.make_async_copy(source.at[at_block(blocks - 1 - i), lanes], buffer.at[slot], stream_sems.at[k, slot])

    def half_of(refs, j):
        return refs[j // 2], slice(UNIT * (j % 2), UNIT * (j % 2) + UNIT)

    def back_states():
        def one(tok, carry):
            at = at_block(tok, big)
            back = dot_nt(low_v[at], w_out_v[...])
            mixed_v[at] = back[:, :SPAN]
            middle_v[at] = back[:, SPAN:]
            return carry

        lax.fori_loop(0, per, one, 0)
        tick(2.0)

    def first_pass(j):
        flows, lanes = half_of((mixed_v, middle_v), j)
        decays(j).wait()

        def one(i, carry):
            product, flow = carry
            b = blocks - 1 - i
            for t in reversed(range(block)):
                there = pl.ds(pl.multiple_of(b * size + t * rows, rows), rows)
                decay = decay_s[j % 2, there]
                flow = decay * (flows[there, lanes] + flow)
                product = decay * product
            return product, flow

        product, flow = lax.fori_loop(0, blocks, one, (jnp.ones((rows, wide), F32), jnp.zeros((rows, wide), F32)))
        chain.start(j, product, flow)
        decays((j + 2) % parts).start()
        tick(0.6)

    def grad_out():
        for j in range(hidden // SPAN):
            def one(tok, carry):
                at = at_block(tok, big)
                gather(2 * feeds + j, dot_tn(state_v[at, pl.ds(j * SPAN, SPAN)], low_v[at]), tok == 0)
                return carry

            lax.fori_loop(0, per, one, 0)
            put_unit(2 * feeds + j)
            enter(2 * feeds + j)
            tick(2.0)

    gains_one = gain_one[...]

    def norm_one(b):
        at = at_block(b)
        value = x_v[at].astype(F32)
        scale = lax.rsqrt(jnp.mean(value * value, axis=-1, keepdims=True) + EPS)
        turned_v[:, at] = jnp.swapaxes(value * scale * gains_one, 0, 1).astype(BF16)
        return ()

    back_states()
    work = [functools.partial(first_pass, j) for j in range(parts)]
    work += [grad_out]

    def turn():
        loads[6].wait()
        beat(blocks, norm_one, 1, 1.6)

    work.append(turn)
    for step in range(max(len(work), parts + chain.rounds)):
        if step < len(work):
            work[step]()
        else:
            tick(1.0)
        for i in range(parts):
            if 0 <= step - 1 - i < chain.rounds:
                chain.advance(i, step - 1 - i)

    streams = ((fade_s, fade_in), (rise_s, rise_in), (weight_s, weight_in), (lean_s, lean_in))

    def stream_all(j, i):
        return [stream(buffer, source, j, i, 1 + k) for k, (buffer, source) in enumerate(streams)]

    for i in range(3):
        for copy in stream_all(0, i):
            copy.start()
    cand_refs = (low_v, cand_v)
    input_refs = (cot_v, w_down_v)

    def second_pass(j):
        flows, lanes = half_of((mixed_v, middle_v), j)
        to_input, to_cand = half_of(input_refs, j)[0], half_of(cand_refs, j)[0]
        decays(j).wait()

        def one(i, flow, sum_f, sum_i):
            b = blocks - 1 - i
            slot = lax.rem(i, 4)

            @pl.when(i + 3 < blocks)
            def _():
                for copy in stream_all(j, i + 3):
                    copy.start()
            if j + 1 < parts:
                @pl.when(i + 3 >= blocks)
                def _():
                    for copy in stream_all(j + 1, i + 3 - blocks):
                        copy.start()
            for copy in stream_all(j, i):
                copy.wait()
            for t in reversed(range(block)):
                here = slice(t * rows, (t + 1) * rows)
                there = pl.ds(pl.multiple_of(b * size + t * rows, rows), rows)
                reach = flows[there, lanes] + flow
                flow = decay_s[j % 2, there] * reach
                lean = reach * lean_s[slot, here].astype(F32)
                grad_f = fade_s[slot, here].astype(F32) * lean
                grad_i = -(rise_s[slot, here].astype(F32) * lean)
                sum_f, sum_i = sum_f + grad_f, sum_i + grad_i
                state_v[there, wide * j : wide * j + wide] = grad_f.astype(BF16)
                to_input[there, lanes] = grad_i.astype(BF16)
                to_cand[there, lanes] = (weight_s[slot, here].astype(F32) * reach).astype(BF16)
            return flow, sum_f, sum_i

        none = jnp.zeros((rows, wide), F32)
        unused, sum_f, sum_i = beat(blocks, one, 1, 1.2, join[j, 1], none, none)
        if j + 2 < parts:
            decays(j + 2).start()
        put_small(4 + 2 * j, jnp.sum(sum_f, axis=0, keepdims=True))
        put_small(12 + 2 * j, jnp.sum(sum_i, axis=0, keepdims=True))

    def grad_in(j):
        unit = 2 * feeds + hidden // SPAN + 3 * j

        lanes = half_of(input_refs, j)[1]
        pieces = ((state_v, slice(wide * j, wide * j + wide)), (half_of(input_refs, j)[0], lanes), (half_of(cand_refs, j)[0], lanes))
        over = [u for u in range(2 * feeds + hidden // SPAN) if plan[u][0] in {plan[unit + k][0] for k in range(3)} and u not in settled]
        settled.update(over)
        assert all(due[u][0] > 7 for u in over)
        if ringed and over:
            ring.settle_sums(over)
        for k, (ref, columns) in enumerate(pieces):
            slot, column, length = plan[unit + k]
            grads[slot, :, pl.ds(column, length)] = dot(turned_v[...], ref[:, columns])
            put_unit(unit + k)
            enter(unit + k)
            tick(0.5)

    settled = set()
    for j in range(parts):
        second_pass(j)
        grad_in(j)

    for k in (7, 8):
        loads[k].wait()
    project_refs = [(state_v, slice(0, hidden), w_up_v, 0)]
    for k, refs in enumerate((input_refs, cand_refs)):
        for half in range(2):
            column = (k + 1) * hidden + half * SPAN
            wide_ref, column = (w_up_v, column) if column < inner else (w_in_v, column - inner)
            project_refs.append((refs[half], slice(None), wide_ref, column))

    def finish_one(tok, norm_sum):
        at = at_block(tok, big)
        grad_all = jnp.zeros((big, width), F32)
        for ref, columns, weight, column in project_refs:
            piece = ref[at, columns]
            grad_all = grad_all + dot_nt(piece, weight[:, column : column + piece.shape[1]])
        for k in range(big // size):
            b = tok * (big // size) + k

            @pl.when(b >= 2)
            def _():
                stage_copy(tokens_s, tokens_out, b - 2).wait()
            here = at_block(b)
            grad = grad_all[k * size : k * size + size]
            value = x_v[here].astype(F32)
            scale = lax.rsqrt(jnp.mean(value * value, axis=-1, keepdims=True) + EPS)
            plain = value * scale
            norm_sum = norm_sum + jnp.sum((grad * plain).reshape(size // 8, 8, width), axis=0)
            lean = grad * gains_one
            back = second_v[here] + scale * (lean - plain * jnp.mean(lean * plain, axis=-1, keepdims=True))
            tokens_s[lax.rem(b, 2)] = jnp.swapaxes(back.reshape(block, rows, width), 0, 1)
            stage_copy(tokens_s, tokens_out, b).start()
        return (norm_sum,)

    (norm_sum,) = beat(per, finish_one, 4, 9.0, jnp.zeros((8, width), F32))
    put_small(0, jnp.sum(norm_sum, axis=0, keepdims=True))
    if ringed:
        step = 0
        while step <= DOUBLINGS or any(due[unit][0] < STAGES for unit in due):
            tick(1.0)
            if step <= DOUBLINGS:
                small.step(step)
            step += 1
        ring.settle_sums([u for u in due if u not in settled])
        ring.settle_lines(list(due))
        copy = pltpu.make_async_copy(own_v.at[DOUBLINGS], small_out.at[0], load_sems.at[0])
    else:
        copy = pltpu.make_async_copy(small_v, small_out.at[0], load_sems.at[0])
    copy.start()
    copy.wait()
    for b in (blocks - 2, blocks - 1):
        stage_copy(tokens_s, tokens_out, b).wait()
    for j in range(parts):
        chain.finish(j)


def back(ringed, shape_in, x, cot, middle, state, decay, fade, rise, weight, lean, gain_one, gain_two, up_bias, down_bias, w_in, w_out, w_up, w_down, cid=2):
    rows, steps, width = shape_in
    total = rows * steps
    hidden = w_out.shape[0]
    inner = w_down.shape[0]
    count = lax.axis_size("seq")
    block = 16
    size = block * rows
    wide = UNIT
    parts = hidden // wide
    feeds = inner // SPAN
    whole = 2 * feeds + hidden // SPAN
    plan = [(u, 0, WIDE) for u in range(whole)]
    for k in range(3 * parts):
        plan.append(((whole + k // 2) % SLOTS, k % 2 * UNIT, UNIT))
    units = len(plan)
    anywhere = pl.BlockSpec(memory_space=pl.ANY)
    vmem = pl.BlockSpec(memory_space=pltpu.VMEM)
    shape = jax.ShapeDtypeStruct
    if ringed:
        first, *others = sum_scratch(units, whole, SLOTS)
        more = [first, pltpu.VMEM((DOUBLINGS + 1, SMALL_ROWS, 128), F32), *others]
        more += [pltpu.VMEM((DOUBLINGS, SMALL_ROWS, 128), F32)] + [pltpu.SemaphoreType.DMA((DOUBLINGS,))] * 2
    else:
        more = [pltpu.VMEM((SLOTS, SPAN, WIDE), F32), pltpu.VMEM((1, SMALL_ROWS, 128), F32)]
    return pl.pallas_call(
        functools.partial(back_kernel, ringed, count, rows, steps, plan, block),
        out_shape=(
            shape(shape_in, BF16), shape(shape_in, F32), shape((units, SPAN, WIDE), F32), shape((1, SMALL_ROWS, 128), F32),
        ),
        in_specs=[anywhere] * 9 + [vmem] * 4 + [anywhere] * 4,
        out_specs=(anywhere,) * 4,
        scratch_shapes=[
            pltpu.VMEM((total, width), F32), pltpu.VMEM((total, width), F32), pltpu.VMEM((total, width), F32),
            pltpu.VMEM((total, hidden), BF16), pltpu.VMEM((total, width), BF16), pltpu.VMEM((total, width), BF16), pltpu.VMEM((total, width), BF16),
            pltpu.VMEM((total, width), BF16), pltpu.VMEM((width, total), BF16),
            pltpu.VMEM((width, w_in.shape[1] - inner), BF16), pltpu.VMEM(w_out.shape, BF16), pltpu.VMEM(w_up.shape, BF16), pltpu.VMEM(w_down.shape, BF16),
            pltpu.VMEM((2, total, wide), F32), pltpu.VMEM((4, size, wide), BF16), pltpu.VMEM((4, size, wide), BF16),
            pltpu.VMEM((4, size, wide), BF16), pltpu.VMEM((4, size, wide), BF16),
            pltpu.VMEM((2, rows, block, width), BF16), pltpu.VMEM((2, rows, block, width), F32), pltpu.VMEM((8, inner), F32),
            pltpu.SemaphoreType.DMA((9,)), pltpu.SemaphoreType.DMA((5, 4)), pltpu.SemaphoreType.DMA((2,)),
            *chain_scratch(parts, count, rows, wide),
            *more,
        ],
        compiler_params=pltpu.CompilerParams(collective_id=cid, has_side_effects=True, vmem_limit_bytes=63 * 2**20 + 2**19),
        cost_estimate=pl.CostEstimate(flops=2 * total * width * (8 * hidden + 6 * inner), bytes_accessed=80 * 2**20, transcendentals=total * inner),
        name="back",
    )(x, cot, middle, state, decay, fade, rise, weight, lean, gain_one.reshape(1, -1), gain_two.reshape(1, -1), up_bias.reshape(1, -1), down_bias.reshape(1, -1), w_in, w_out, w_up, w_down)


def settle_kernel(places, mixed, tokens, units, small, *refs):
    outs, (mixed_v, tokens_v, units_v, reads, writes) = refs[:-5], refs[-5:]
    copies = []
    for k in range(mixed.shape[0] // 4):
        some = pl.ds(4 * k, 4)
        copies.append((tokens.at[some], tokens_v.at[some], outs[1].at[some]))
        copies.append((mixed.at[some], mixed_v.at[some], outs[0].at[some]))
    for u, length, array, row, column in places:
        lanes = pl.ds(0, length)
        copies.append((units.at[u, :, lanes], units_v.at[u, :, lanes], outs[2 + array].at[pl.ds(row, SPAN), pl.ds(column, length)]))
    moves = [
        (pltpu.make_async_copy(a, b, reads.at[k]), pltpu.make_async_copy(b, c, writes.at[k])) for k, (a, b, c) in enumerate(copies)
    ]
    for read, write in moves:
        read.start()
    row = 0
    for out in outs[6:]:
        out[...] = small[0, pl.ds(row, out.shape[0])]
        row += out.shape[0]
    for read, write in moves:
        read.wait()
        write.start()
    for read, write in moves:
        write.wait()


def settle(mixed, tokens, units, small, hidden, inner):
    width = tokens.shape[-1]
    parts = hidden // UNIT
    feeds = inner // SPAN
    places = []
    for f in range(feeds):
        places += [(2 * f, SPAN, 3, f * SPAN, 0), (2 * f + 1, SPAN, 2, 0, f * SPAN)]
    places += [(2 * feeds + j, SPAN, 1, j * SPAN, 0) for j in range(hidden // SPAN)]
    for j in range(parts):
        places += [(len(places) + k, UNIT, 0, 0, k * hidden + j * UNIT) for k in range(3)]
    anywhere = pl.BlockSpec(memory_space=pl.ANY)
    vmem = pl.BlockSpec(memory_space=pltpu.VMEM)
    shape = jax.ShapeDtypeStruct
    lengths = (width, hidden, hidden, width, inner, width)
    return pl.pallas_call(
        functools.partial(settle_kernel, places),
        out_shape=(
            shape(mixed.shape, mixed.dtype), shape(tokens.shape, F32), shape((width, 3 * hidden), F32), shape((hidden, width), F32),
            shape((width, inner), F32), shape((inner, width), F32), *(shape((n // 128, 128), F32) for n in lengths),
        ),
        in_specs=[anywhere] * 3 + [vmem],
        out_specs=(anywhere,) * 6 + (vmem,) * 6,
        scratch_shapes=[
            pltpu.VMEM(mixed.shape, mixed.dtype), pltpu.VMEM(tokens.shape, F32), pltpu.VMEM(units.shape, F32),
            pltpu.SemaphoreType.DMA((mixed.shape[0] // 2 + len(places),)), pltpu.SemaphoreType.DMA((mixed.shape[0] // 2 + len(places),)),
        ],
        compiler_params=pltpu.CompilerParams(vmem_limit_bytes=48 * 2**20),
        name="settle",
    )(mixed, tokens, units, small)


def on_device(tokens, cotangent, reset_pos, norm1_gain, w_in, forget_bias, input_bias, w_out, norm2_gain, w_up, up_bias, w_down, down_bias):
    ringed = lax.axis_size("seq") == 8 and lax.axis_size("rows") == 4
    hidden, inner = w_out.shape[0], w_down.shape[0]
    kept = front(tokens, cotangent, reset_pos, norm1_gain, w_in, forget_bias, input_bias, w_out)
    mixed, grad_tokens, units, small = back(
        ringed, tokens.shape, *kept, norm1_gain, norm2_gain, up_bias, down_bias, w_in, w_out, w_up, w_down
    )
    if not ringed:
        units, small = lax.psum((units, small), ("seq", "rows"))
    mixed, grad_tokens, grad_in, grad_out, grad_up, grad_down, *rest = settle(mixed, grad_tokens, units, small, hidden, inner)
    norm_one, forget, inputs, norm_two, up, down = (one.reshape(-1) for one in rest)
    return mixed, grad_tokens, norm_one, grad_in, forget, inputs, grad_out, norm_two, grad_up, up, grad_down, down


def solution(mesh):
    return jax.shard_map(
        on_device,
        mesh=mesh,
        in_specs=(
            P("rows", "seq", None),
            P("rows", "seq", None),
            P("rows", None),
            P(),
            P(),
            P(),
            P(),
            P(),
            P(),
            P(),
            P(),
            P(),
            P(),
        ),
        out_specs=(
            P("rows", "seq", None),
            P("rows", "seq", None),
            P(),
            P(),
            P(),
            P(),
            P(),
            P(),
            P(),
            P(),
            P(),
            P(),
        ),
        check_vma=False,
    )
```

```python
import functools
import math
import jax
import jax.numpy as jnp
from jax import lax
from jax.experimental import pallas as pl
from jax.experimental.pallas import tpu as pltpu
from jax.sharding import PartitionSpec as P

MESH = pl.DeviceIdType.MESH
EPS = 1e-6
F32 = jnp.float32
BF16 = jnp.bfloat16
STAGES = 13
KINDS = 10
SPAN = 512
UNIT = 256
WIDE = 512
SLOTS = 10
SIDE = 8
SMALL_ROWS = 48
DOUBLINGS = 5
SLOW = (0, 1, 3, 6, 8, 10, 11, 12, 14, 16, 19, 21, 22)
FAST = (0, 1, 4, 8, 11, 13, 15, 17, 19, 22, 26, 29, 30)


def place():
    seq = lax.axis_index("seq")
    rows = lax.axis_index("rows")
    return lax.div(rows, 2), lax.rem(seq, 2), lax.div(seq, 2), lax.rem(rows, 2)


def spot(x, y, z, core):
    return (z * 2 + y, x * 2 + core)


def dot(left, right):
    return jnp.dot(left, right, preferred_element_type=F32)


def dot_nt(left, right):
    return lax.dot_general(left, right, (((1,), (1,)), ((), ())), preferred_element_type=F32)


def dot_tn(left, right):
    return lax.dot_general(left, right, (((0,), (0,)), ((), ())), preferred_element_type=F32)


class Chain:
    def __init__(self, count, sign, sent, got, join, send, recv):
        self.count, self.sign = count, sign
        self.sent, self.got, self.join = sent, got, join
        self.send, self.recv = send, recv
        self.rounds = max(1, math.ceil(math.log2(count)))
        seq = lax.axis_index("seq")
        self.seq = seq
        self.place = seq if sign > 0 else count - 1 - seq

    def partners(self):
        for r in range(self.rounds):
            far = 2**r
            yield self.seq + self.sign * far, self.place + far < self.count
            yield self.seq - self.sign * far, self.place >= far

    def copy(self, part, r, other):
        return pltpu.make_async_remote_copy(
            src_ref=self.sent.at[part, r], dst_ref=self.got.at[part, r],
            send_sem=self.send.at[part, r], recv_sem=self.recv.at[part, r],
            device_id=(other, lax.axis_index("rows")), device_id_type=MESH,
        )

    def push(self, part, r):
        @pl.when(self.place + 2**r < self.count)
        def _():
            self.copy(part, r, self.seq + self.sign * 2**r).start()

    def start(self, part, product, end):
        self.sent[part, 0, 0] = product
        self.sent[part, 0, 1] = end
        self.join[part, 0] = jnp.ones_like(product)
        self.join[part, 1] = jnp.zeros_like(end)
        self.push(part, 0)

    def advance(self, part, r):
        last = r == self.rounds - 1

        @pl.when(self.place >= 2**r)
        def _():
            self.copy(part, r, self.seq - self.sign * 2**r).wait_recv()
            product, end = self.got[part, r, 0], self.got[part, r, 1]
            own = self.join[part, 0]
            self.join[part, 1] = self.join[part, 1] + own * end
            if not last:
                self.join[part, 0] = own * product
                here = self.sent[part, r, 0]
                self.sent[part, r + 1, 0] = here * product
                self.sent[part, r + 1, 1] = self.sent[part, r, 1] + here * end

        if not last:
            @pl.when(self.place < 2**r)
            def _():
                self.sent[part, r + 1] = self.sent[part, r]
            self.push(part, r + 1)

    def finish(self, part):
        for r in range(self.rounds):
            @pl.when(self.place + 2**r < self.count)
            def _():
                self.copy(part, r, self.seq + self.sign * 2**r).wait_send()


def greet_chain(chain):
    barrier = pltpu.get_barrier_semaphore()
    rows = lax.axis_index("rows")
    total = 0
    for other, there in chain.partners():
        @pl.when(there)
        def _():
            pl.semaphore_signal(barrier, inc=1, device_id=(other, rows), device_id_type=MESH)
        total = total + jnp.where(there, 1, 0)
    return barrier, total


def chain_scratch(parts, count, rows, width):
    rounds = max(1, math.ceil(math.log2(count)))
    return [
        pltpu.VMEM((parts, rounds, 2, rows, width), F32),
        pltpu.VMEM((parts, rounds, 2, rows, width), F32),
        pltpu.VMEM((parts, 2, rows, width), F32),
        pltpu.SemaphoreType.DMA((parts, rounds)),
        pltpu.SemaphoreType.DMA((parts, rounds)),
    ]


def front_kernel(
    count, rows, steps, chunk, block,
    tokens, cotangent, reset_in, gain, w_in, forget_bias, input_bias, w_out,
    x_out, cot_out, middle_out, state_out, decay_out, fade_out, rise_out, weight_out, lean_out,
    reset, tok_v, cot_v, x_v, normed_v, w_v, w_out_v, keep_v, decay_v, update_v, cand_v, fade_v, rise_v, weight_v, lean_v, state_v, middle_v,
    sent, got, join, send, recv, sems, out_sems,
):
    total, width = x_v.shape
    hidden = w_out_v.shape[0]
    parts = hidden // chunk
    size = block * rows
    blocks = steps // block
    side = math.gcd(blocks, SIDE)
    chain = Chain(count, 1, sent, got, join, send, recv)
    barrier, greeted = greet_chain(chain)
    loads = [pltpu.make_async_copy(tokens, tok_v, sems.at[0])]
    for j in range(parts):
        for k in range(3):
            loads.append(pltpu.make_async_copy(w_in.at[:, pl.ds(k * hidden + j * chunk, chunk)], w_v.at[j, :, pl.ds(k * chunk, chunk)], sems.at[1 + 3 * j + k]))
    loads.append(pltpu.make_async_copy(cotangent, cot_v, sems.at[1 + 3 * parts]))
    loads.append(pltpu.make_async_copy(w_out, w_out_v, sems.at[2 + 3 * parts]))
    marks_in = pltpu.make_async_copy(reset_in, reset, sems.at[3 + 3 * parts])
    marks_in.start()
    for load in loads:
        load.start()
    marks_in.wait()
    loads[0].wait()

    first = lax.axis_index("seq") * steps
    marks = [jnp.broadcast_to(reset[:, k : k + 1], (rows, 128)) for k in range(reset.shape[1])]

    def mark(t, carry):
        hit = marks[0] == first + t
        for one in marks[1:]:
            hit = hit | (one == first + t)
        keep_v[pl.ds(pl.multiple_of(t * rows, rows), rows)] = jnp.where(hit, 0.0, 1.0)
        return carry

    lax.fori_loop(0, steps, mark, 0, unroll=4)
    gains = gain[...]

    def norm(b, carry):
        at = pl.ds(pl.multiple_of(b * size, size), size)
        x = tok_v[:, pl.ds(pl.multiple_of(b * block, block), block), :].astype(F32)
        x = jnp.swapaxes(x, 0, 1).reshape(size, width)
        x_v[at] = x.astype(BF16)
        scale = lax.rsqrt(jnp.mean(x * x, axis=-1, keepdims=True) + EPS)
        normed_v[at] = (x * scale * gains).astype(BF16)
        return carry

    lax.fori_loop(0, blocks, norm, 0)
    outs = [pltpu.make_async_copy(x_v, x_out, out_sems.at[0])]
    outs[0].start()

    def gates(j):
        lanes = pl.ds(j * chunk, chunk)
        shift_f, shift_i = -forget_bias[:, lanes], -input_bias[:, lanes]

        def some(project, at, product, end):
            neg_f = shift_f - project[:, :chunk]
            neg_i = shift_i - project[:, chunk : 2 * chunk]
            cand = project[:, 2 * chunk :]
            lower = jnp.maximum(jnp.minimum(neg_f, neg_i) - 20.0, 0.0)
            exp_f = jnp.exp(jnp.minimum(neg_f - lower, 80.0))
            exp_i = jnp.exp(jnp.minimum(neg_i - lower, 80.0))
            one_f, one_i = 1.0 + exp_f, 1.0 + exp_i
            share = 1.0 / (one_f + one_i)
            decay, weight = one_i * share, one_f * share
            fade_v[j % 2, at] = (decay * (exp_f * share)).astype(BF16)
            rise_v[j % 2, at] = (weight * (exp_i * share)).astype(BF16)
            weight_v[j % 2, at] = weight.astype(BF16)
            cand_v[at, lanes] = cand
            update = weight * cand
            update_v[at, lanes] = update
            decay = decay * jnp.concatenate([keep_v[at]] * (chunk // 128), axis=1)
            decay_v[at, lanes] = decay
            for t in range(block):
                here = decay[t * rows : (t + 1) * rows]
                end = here * end + update[t * rows : (t + 1) * rows]
                product = here * product
            return product, end

        def one(b, carry):
            places = [pl.ds(pl.multiple_of((b * side + k) * size, size), size) for k in range(side)]
            for at in places:
                carry = some(dot(normed_v[at], w_v[j]), at, *carry)
            return carry

        start = (jnp.ones((rows, chunk), F32), jnp.zeros((rows, chunk), F32))
        return lax.fori_loop(0, blocks // side, one, start)

    def scan(j):
        lanes = pl.ds(j * chunk, chunk)

        def one(b, state):
            for t in range(block):
                here = pl.ds(pl.multiple_of(b * size + t * rows, rows), rows)
                keep = jnp.concatenate([keep_v[here]] * (chunk // 128), axis=1)
                lean_v[j % 2, here] = (keep * state - cand_v[here, lanes]).astype(BF16)
                state = decay_v[here, lanes] * state + update_v[here, lanes]
                state_v[here, lanes] = state.astype(BF16)
            return state

        lax.fori_loop(0, blocks, one, join[j, 1])

    def project_out(b, carry):
        at = pl.ds(pl.multiple_of(b * 2 * size, 2 * size), 2 * size)
        middle_v[at] = x_v[at].astype(F32) + dot(state_v[at], w_out_v[...])
        copy = pltpu.make_async_copy(middle_v.at[at], middle_out.at[at], out_sems.at[2 + 6 * parts])
        copy.start()
        return carry

    def put(source, target, slot, wait=False):
        copy = pltpu.make_async_copy(source, target, out_sems.at[slot])
        if wait:
            copy.wait()
        else:
            copy.start()

    def gate_outs(j, wait=False):
        lanes = pl.ds(j * chunk, chunk)
        for k, (a, b) in enumerate(((fade_v, fade_out), (rise_v, rise_out), (weight_v, weight_out))):
            put(a.at[j % 2], b.at[:, lanes], 1 + 3 * j + k, wait)
        put(decay_v.at[:, lanes], decay_out.at[:, lanes], 1 + 3 * parts + j, wait)

    def scan_outs(j, wait=False):
        lanes = pl.ds(j * chunk, chunk)
        put(lean_v.at[j % 2], lean_out.at[:, lanes], 1 + 4 * parts + 2 * j, wait)
        put(state_v.at[:, lanes], state_out.at[:, lanes], 2 + 4 * parts + 2 * j, wait)

    ready = 0
    for j in range(parts):
        for k in range(3):
            loads[1 + 3 * j + k].wait()
        if j >= 2:
            gate_outs(j - 2, True)
        product, end = gates(j)
        gate_outs(j)
        if j == 0:
            pl.semaphore_wait(barrier, greeted)
        chain.start(j, product, end)
        for i in range(j - 1, -1, -1):
            if j - 1 - i < chain.rounds:
                chain.advance(i, j - 1 - i)
    for k in range(2):
        loads[1 + 3 * parts + k].wait()

    def turn(b, carry):
        at = pl.ds(pl.multiple_of(b * size, size), size)
        c = cot_v[:, pl.ds(pl.multiple_of(b * block, block), block), :].astype(F32)
        normed_v[at] = jnp.swapaxes(c, 0, 1).reshape(size, width).astype(BF16)
        return carry

    lax.fori_loop(0, blocks, turn, 0)
    put(normed_v, cot_out, 1 + 6 * parts)

    step = parts - 1
    while ready < parts:
        for i in range(parts - 1, -1, -1):
            if 0 <= step - 1 - i < chain.rounds and step >= parts:
                chain.advance(i, step - 1 - i)
        while ready < parts and ready + chain.rounds <= step:
            if ready >= 2:
                scan_outs(ready - 2, True)
            scan(ready)
            scan_outs(ready)
            ready += 1
        step += 1
    lax.fori_loop(0, blocks // 2, project_out, 0)
    for j in range(parts):
        if j >= parts - 2:
            gate_outs(j, True)
            scan_outs(j, True)
        chain.finish(j)
    outs[0].wait()
    put(normed_v, cot_out, 1 + 6 * parts, True)
    put(middle_v, middle_out, 2 + 6 * parts, True)


def front(tokens, cotangent, reset, gain, w_in, forget_bias, input_bias, w_out, cid=1):
    rows, steps, width = tokens.shape
    hidden = w_out.shape[0]
    total = rows * steps
    count = lax.axis_size("seq")
    chunk, block = 256, 16
    parts = hidden // chunk
    anywhere = pl.BlockSpec(memory_space=pl.ANY)
    vmem = pl.BlockSpec(memory_space=pltpu.VMEM)
    shape = jax.ShapeDtypeStruct
    return pl.pallas_call(
        functools.partial(front_kernel, count, rows, steps, chunk, block),
        out_shape=(
            shape((total, width), BF16), shape((total, width), BF16), shape((total, width), F32),
            shape((total, hidden), BF16), shape((total, hidden), F32), shape((total, hidden), BF16),
            shape((total, hidden), BF16), shape((total, hidden), BF16), shape((total, hidden), BF16),
        ),
        in_specs=[anywhere, anywhere, anywhere, vmem, anywhere, vmem, vmem, anywhere],
        out_specs=(anywhere,) * 9,
        scratch_shapes=[
            pltpu.VMEM(reset.shape, jnp.int32), pltpu.VMEM(tokens.shape, BF16), pltpu.VMEM(tokens.shape, BF16), pltpu.VMEM((total, width), BF16), pltpu.VMEM((total, width), BF16),
            pltpu.VMEM((parts, width, 3 * chunk), BF16), pltpu.VMEM(w_out.shape, BF16), pltpu.VMEM((total, 128), F32),
            pltpu.VMEM((total, hidden), F32), pltpu.VMEM((total, hidden), F32), pltpu.VMEM((total, hidden), F32),
            pltpu.VMEM((2, total, chunk), BF16), pltpu.VMEM((2, total, chunk), BF16), pltpu.VMEM((2, total, chunk), BF16),
            pltpu.VMEM((2, total, chunk), BF16), pltpu.VMEM((total, hidden), BF16), pltpu.VMEM((total, width), F32),
            *chain_scratch(parts, count, rows, chunk),
            pltpu.SemaphoreType.DMA((4 + 3 * parts,)), pltpu.SemaphoreType.DMA((3 + 6 * parts,)),
        ],
        compiler_params=pltpu.CompilerParams(collective_id=cid, has_side_effects=True, vmem_limit_bytes=62 * 2**20),
        cost_estimate=pl.CostEstimate(flops=2 * total * width * 4 * hidden, bytes_accessed=40 * 2**20, transcendentals=3 * total * hidden),
        name="front",
    )(tokens, cotangent, reset, gain.reshape(1, -1), w_in, forget_bias.reshape(1, -1), input_bias.reshape(1, -1), w_out)


class Summing:
    def __init__(self, plan, grads, half_in, part_in, lines_in, last_in, send, recv, local, free, result):
        self.plan, self.grads = plan, grads
        self.whole = sum(width == WIDE for slot, column, width in plan)
        self.half_in, self.part_in, self.lines_in, self.last_in = half_in, part_in, lines_in, last_in
        self.result, self.send, self.recv, self.local, self.free = result, send, recv, local, free
        x, y, z, core = place()
        self.z = z
        first = core == 0
        self.sibling = spot(x, y, z, 1 - core)
        along_x, along_y = spot(1 - x, y, z, core), spot(x, 1 - y, z, core)
        self.near = tuple(jnp.where(first, a, b) for a, b in zip(along_x, along_y))
        self.far = tuple(jnp.where(first, b, a) for a, b in zip(along_x, along_y))
        self.above = spot(x, y, z + 1, core)
        self.below = spot(x, y, z - 1, core)
        near_bit = jnp.where(first, x, y)
        far_bit = jnp.where(first, y, x)
        self.n_half, self.n_part, self.n_line, self.n_tip = SPAN // 2, SPAN // 4, SPAN // 16, SPAN // 32
        self.half = core * self.n_half
        self.other_half = (1 - core) * self.n_half
        self.part = self.half + near_bit * self.n_part
        self.other_part = self.half + (1 - near_bit) * self.n_part
        self.tip = self.part + self.n_line * z + self.n_tip * far_bit
        self.other_tip = self.part + self.n_line * z + self.n_tip * (1 - far_bit)

    def copy(self, kind, unit, source, target, device):
        return pltpu.make_async_remote_copy(
            src_ref=source, dst_ref=target, send_sem=self.send.at[kind, unit], recv_sem=self.recv.at[kind, unit],
            device_id=device, device_id_type=MESH,
        )

    def slot_of(self, u):
        return self.plan[u] if isinstance(u, int) else (u, 0, WIDE)

    def rows(self, u, start, count):
        slot, column, width = self.slot_of(u)
        return self.grads.at[slot, pl.ds(pl.multiple_of(start, 8), count), pl.ds(column, width)]

    def done(self, u, start, count):
        return self.result.at[u, pl.ds(pl.multiple_of(start, 8), count), pl.ds(0, self.slot_of(u)[2])]

    def land(self, ref, wide, u, start, count):
        if self.slot_of(u)[2] == WIDE:
            return ref.at[lax.rem(u, wide), pl.ds(start, count)]
        turn = (u - self.whole) % (2 * (ref.shape[0] - wide))
        return ref.at[wide + turn // 2, pl.ds(start, count), pl.ds(turn % 2 * UNIT, UNIT)]

    def turns(self, kind, u):
        ref, wide = ((self.half_in, 2), (self.part_in, 3), (self.lines_in, 3), (self.lines_in, 3))[kind]
        if self.slot_of(u)[2] == WIDE:
            return wide, 0, self.whole
        return 2 * (ref.shape[0] - wide), self.whole, len(self.plan)

    def claim(self, kind, u):
        apart, first, last = self.turns(kind, u)
        if isinstance(u, int):
            if u - apart >= first:
                pl.semaphore_wait(self.free.at[kind, u - apart], 1)
        else:
            @pl.when(u >= apart)
            def _():
                pl.semaphore_wait(self.free.at[kind, u - apart], 1)

    def release(self, kind, u, sender):
        apart, first, last = self.turns(kind, u)

        def signal():
            pl.semaphore_signal(self.free.at[kind, u], inc=1, device_id=sender, device_id_type=MESH)

        if isinstance(u, int):
            if u + apart < last:
                signal()
        else:
            pl.when(u + apart < last)(signal)

    def land_half(self, u):
        return self.land(self.half_in, 2, u, 0, self.n_half)

    def land_part(self, u):
        return self.land(self.part_in, 3, u, 0, self.n_part)

    def land_up(self, u, z):
        return self.land(self.lines_in, 3, u, 0, self.n_line * (4 - z))

    def land_down(self, u, z):
        return self.land(self.lines_in, 3, u, self.n_line * (4 - z) if z > 0 else 0, self.n_line * (z + 1))

    def land_last(self, u):
        return self.land(self.last_in, self.whole, u, 0, self.n_tip)

    def c_half(self, u):
        return self.copy(0, u, self.rows(u, self.other_half, self.n_half), self.land_half(u), self.sibling)

    def c_part(self, u):
        return self.copy(1, u, self.rows(u, self.other_part, self.n_part), self.land_part(u), self.near)

    def c_up(self, u, z):
        low, rest = self.n_line * (z + 1), self.n_line * (3 - z)
        return self.copy(2, u, self.rows(u, self.part + low, rest), self.land_up(u, z + 1), self.above)

    def c_down(self, u, z):
        rest = self.n_line * z
        return self.copy(3, u, self.rows(u, self.part, rest), self.land_down(u, z - 1), self.below)

    def c_last(self, u):
        return self.copy(4, u, self.rows(u, self.other_tip, self.n_tip), self.land_last(u), self.far)

    def c_own(self, u):
        return pltpu.make_async_copy(self.rows(u, self.tip, self.n_tip), self.done(u, self.tip, self.n_tip), self.local.at[u])

    def c_far(self, u, start):
        return self.copy(5, u, self.rows(u, start, self.n_tip), self.done(u, start, self.n_tip), self.far)

    def c_rise(self, u, z):
        piece = self.done(u, self.part, self.n_line * (z + 1))
        return self.copy(6, u, piece, piece, self.above)

    def c_fall(self, u, z):
        piece = self.done(u, self.part + self.n_line * z, self.n_line * (4 - z))
        return self.copy(7, u, piece, piece, self.below)

    def c_near(self, u, start):
        piece = self.done(u, start, self.n_part)
        return self.copy(8, u, piece, piece, self.near)

    def c_sibling(self, u, start):
        piece = self.done(u, start, self.n_half)
        return self.copy(9, u, piece, piece, self.sibling)

    def add(self, u, start, count, ref):
        slot, column, width = self.slot_of(u)
        step = min(count, 128)
        lanes = pl.ds(column, width)

        def one(i, carry):
            here = pl.ds(pl.multiple_of(start + i * step, 8), step)
            there = pl.ds(pl.multiple_of(i * step, 8), step)
            self.grads[slot, here, lanes] = self.grads[slot, here, lanes] + ref[there]
            return carry

        if count == step:
            one(0, 0)
        else:
            lax.fori_loop(0, count // step, one, 0)

    def settle_sums(self, units):
        def sent(k):
            for u in units:
                if k < 3:
                    self.c_up(u, k).wait_send()
                if k > 0:
                    self.c_down(u, k).wait_send()

        self.at_each(sent)

    def settle_lines(self, units):
        def sent(k):
            for u in units:
                if k < 3:
                    self.c_rise(u, k).wait_send()
                if k > 0:
                    self.c_fall(u, k).wait_send()

        self.at_each(sent)

    def at_each(self, action):
        for k in range(4):
            pl.when(self.z == k)(functools.partial(action, k))

    def stage(self, s, u):
        z = self.z
        if s == 0:
            self.claim(0, u)
            self.c_half(u).start()
        elif s == 1:
            self.c_half(u).wait()
            self.add(u, self.half, self.n_half, self.land_half(u))
            self.release(0, u, self.sibling)
            self.claim(1, u)
            self.c_part(u).start()
        elif s == 2:
            self.c_part(u).wait()
            self.add(u, self.part, self.n_part, self.land_part(u))
            self.release(1, u, self.near)
        if 2 <= s <= 5:
            up, down = s - 2, 5 - s

            @pl.when(z == up)
            def _():
                if up > 0:
                    self.c_up(u, up - 1).wait_recv()
                    low, rest = self.n_line * up, self.n_line * (4 - up)
                    self.add(u, self.part + low, rest, self.land_up(u, up))
                    self.release(2, u, self.below)
                if up < 3:
                    self.claim(2, u)
                    self.c_up(u, up).start()

            @pl.when(z == down)
            def _():
                if down < 3:
                    self.c_down(u, down + 1).wait_recv()
                    rest = self.n_line * (down + 1)
                    self.add(u, self.part, rest, self.land_down(u, down))
                    self.release(3, u, self.above)
                if down > 0:
                    self.claim(3, u)
                    self.c_down(u, down).start()
        if s == 5:
            self.c_last(u).start()
        elif s == 6:
            self.c_last(u).wait()
            self.add(u, self.tip, self.n_tip, self.land_last(u))
            self.c_far(u, self.tip).start()
            self.c_own(u).start()
        elif s == 7:
            self.c_far(u, self.tip).wait_send()
            self.c_far(u, self.other_tip).wait_recv()
            self.c_own(u).wait()
        if 7 <= s <= 10:
            up, down = s - 7, 10 - s

            @pl.when(z == up)
            def _():
                if up > 0:
                    self.c_rise(u, up - 1).wait_recv()
                if up < 3:
                    self.c_rise(u, up).start()

            @pl.when(z == down)
            def _():
                if down < 3:
                    self.c_fall(u, down + 1).wait_recv()
                if down > 0:
                    self.c_fall(u, down).start()
        if s == 10:
            self.c_near(u, self.part).start()
        elif s == 11:
            self.c_near(u, self.part).wait_send()
            self.c_near(u, self.other_part).wait_recv()
            self.c_sibling(u, self.half).start()
        elif s == 12:
            self.c_sibling(u, self.half).wait_send()
            self.c_sibling(u, self.other_half).wait_recv()


def sum_scratch(units, whole, slots):
    pairs = (units - whole + 1) // 2
    return [
        pltpu.VMEM((slots, SPAN, WIDE), F32),
        pltpu.VMEM((2 + min(pairs, 2), SPAN // 2, WIDE), F32),
        pltpu.VMEM((3 + min(pairs, 4), SPAN // 4, WIDE), F32),
        pltpu.VMEM((3 + pairs, 5 * SPAN // 16, WIDE), F32),
        pltpu.VMEM((whole + pairs, SPAN // 32, WIDE), F32),
        pltpu.SemaphoreType.DMA((KINDS, units)),
        pltpu.SemaphoreType.DMA((KINDS, units)),
        pltpu.SemaphoreType.DMA((units,)),
        pltpu.SemaphoreType.REGULAR((4, units)),
    ]


class Doubling:
    def __init__(self, own, got, send, recv):
        self.own, self.got, self.send, self.recv = own, got, send, recv
        x, y, z, core = place()
        self.partners = (
            spot(x, y, z, 1 - core), spot(1 - x, y, z, core), spot(x, 1 - y, z, core),
            spot(x, y, z + 1 - 2 * lax.rem(z, 2), core), spot(x, y, z + 2 - 4 * lax.div(z, 2), core),
        )

    def copy(self, k):
        return pltpu.make_async_remote_copy(
            src_ref=self.own.at[k], dst_ref=self.got.at[k], send_sem=self.send.at[k], recv_sem=self.recv.at[k],
            device_id=self.partners[k], device_id_type=MESH,
        )

    def step(self, k):
        if k > 0:
            self.copy(k - 1).wait()
            self.own[k] = self.own[k - 1] + self.got[k - 1]
        if k < DOUBLINGS:
            self.copy(k).start()


def greet_ring(ring):
    barrier = pltpu.get_barrier_semaphore()
    for there in (ring.sibling, ring.near, ring.far):
        pl.semaphore_signal(barrier, inc=1, device_id=there, device_id_type=MESH)

    @pl.when(ring.z > 0)
    def _():
        pl.semaphore_signal(barrier, inc=1, device_id=ring.below, device_id_type=MESH)

    @pl.when(ring.z < 3)
    def _():
        pl.semaphore_signal(barrier, inc=1, device_id=ring.above, device_id_type=MESH)

    return 3 + jnp.where(ring.z > 0, 1, 0) + jnp.where(ring.z < 3, 1, 0)


GELU_A = math.sqrt(2.0 / math.pi)
GELU_B = GELU_A * 0.044715


def back_kernel(
    ringed, count, rows, steps, plan, block,
    x_in, cot_in, middle_in, state_in, decay_in, fade_in, rise_in, weight_in, lean_in,
    gain_one, gain_two, up_bias, down_bias, w_in, w_out, w_up, w_down,
    mixed_out, tokens_out, result, small_out,
    middle_v, second_v, mixed_v, state_v, cot_v, x_v, low_v, cand_v, turned_v, w_in_v, w_out_v, w_up_v, w_down_v,
    decay_s, fade_s, rise_s, weight_s, lean_s, mixed_s, tokens_s, sums_v,
    load_sems, stream_sems, stage_sems,
    sent, got, join, send, recv,
    *ring_refs,
):
    total, width = x_v.shape
    hidden = w_out_v.shape[0]
    inner = w_down_v.shape[0]
    size = block * rows
    blocks = steps // block
    wide = UNIT
    parts = hidden // wide
    big = 512
    per = total // big
    feeds = inner // SPAN
    chain = Chain(count, -1, sent, got, join, send, recv)
    barrier, greeted = greet_chain(chain)
    grads, own_v = ring_refs[:2]
    if ringed:
        ring = Summing(plan, grads, *ring_refs[2:10], result)
        small = Doubling(own_v, *ring_refs[10:])
        greeted = greeted + greet_ring(ring)
    small_v = own_v.at[0]

    inner_columns = pl.ds(0, inner)
    rest_columns = pl.ds(inner, w_in.shape[1] - inner)
    loads = [
        pltpu.make_async_copy(source, target, load_sems.at[k])
        for k, (source, target) in enumerate((
            (middle_in, middle_v), (w_up, w_up_v), (cot_in, cot_v), (w_down, w_down_v), (state_in, state_v),
            (w_out, w_out_v), (x_in, x_v), (w_in.at[:, rest_columns], w_in_v), (w_in.at[:, inner_columns], w_up_v),
        ))
    ]
    loads[0].start()

    def at_block(b, n=size):
        return pl.ds(pl.multiple_of(b * n, n), n)

    due = {}
    clock = [0.0]

    def travel(unit, s):
        return 2.0 * (SLOW[s] - SLOW[s - 1]) if plan[unit][2] == WIDE else 1.0 * (FAST[s] - FAST[s - 1])

    def enter(unit):
        due[unit] = (0, clock[0])

    def tick(passed):
        clock[0] += passed
        for unit in sorted(due):
            s, when = due[unit]
            if s < STAGES and when <= clock[0] + 1e-6:
                if ringed:
                    ring.stage(s, unit)
                due[unit] = (s + 1, clock[0] + travel(unit, s + 1) if s + 1 < STAGES else 0.0)

    def rolling_tick(i, half):
        for s in reversed(range(STAGES)):
            behind = SLOW[s] + early - half
            if ringed and behind % 2 == 0 and behind // 2 < feeds * per // 2:
                pl.when(i >= behind // 2)(functools.partial(ring.stage, s, i - behind // 2))

    def beat(number, body, ticks, passed, *carry):
        each = number // ticks
        for k in range(ticks):
            carry = lax.fori_loop(each * k, each * k + each, lambda i, c: body(i, *c), carry)
            tick(passed / ticks)
        return carry

    def put_unit(unit):
        if not ringed:
            slot, column, length = plan[unit] if isinstance(unit, int) else (unit, 0, WIDE)
            copy = pltpu.make_async_copy(
                grads.at[slot, :, pl.ds(column, length)], result.at[unit, :, pl.ds(0, length)], load_sems.at[0]
            )
            copy.start()
            copy.wait()

    sums_v[...] = jnp.zeros_like(sums_v)
    small_v[...] = jnp.zeros_like(small_v)

    def put_small(row, value):
        for k in range(value.shape[1] // 128):
            small_v[pl.ds(row + k, 1)] = value[:, 128 * k : 128 * k + 128]

    def gather(slot, value, fresh):
        grads[slot] = jnp.where(fresh, 0.0, grads[slot]) + value

    loads[0].wait()
    for k in (1, 2, 3):
        loads[k].start()
    gains = gain_two[...]
    bias = down_bias[...]

    def norm_two(b, carry):
        at = at_block(b)
        value = middle_v[at]
        scale = lax.rsqrt(jnp.mean(value * value, axis=-1, keepdims=True) + EPS)
        normed = value * scale * gains
        low_v[at] = normed.astype(BF16)
        turned_v[:, at] = jnp.swapaxes(normed, 0, 1).astype(BF16)
        mixed_v[at] = value + bias
        second_v[at] = jnp.zeros_like(value)
        return carry

    lax.fori_loop(0, blocks, norm_two, 0)
    for k in (1, 2, 3):
        loads[k].wait()
    for k in (4, 5, 6, 7):
        loads[k].start()
    pl.semaphore_wait(barrier, greeted)

    def feed(f, tok):
        at = at_block(tok, big)
        lanes = pl.ds(pl.multiple_of(f * SPAN, SPAN), SPAN)
        cot = cot_v[at]
        pre = dot(low_v[at], w_up_v[:, lanes]) + up_bias[:, lanes]
        back_act = dot_nt(cot, w_down_v[lanes])
        square = pre * pre
        gate = 0.5 * jnp.tanh(pre * (GELU_A + GELU_B * square)) + 0.5
        act = pre * gate
        slope = gate + act * (1.0 - gate) * (2.0 * GELU_A + 6.0 * GELU_B * square)
        back_up = back_act * slope
        sums_v[0:1, lanes] = sums_v[0:1, lanes] + jnp.sum(back_up, axis=0, keepdims=True)
        act, back_up = act.astype(BF16), back_up.astype(BF16)
        mixed_v[at] = mixed_v[at] + dot(act, w_down_v[lanes])
        second_v[at] = second_v[at] + dot_nt(back_up, w_up_v[:, lanes])
        gather(2 * f, dot_tn(act, cot), tok == 0)
        gather(2 * f + 1, dot(turned_v[:, at], back_up), tok == 0)

    early = per - 1

    def feed_pair(i, carry):
        f, tok = lax.div(2 * i, per), lax.rem(2 * i, per)
        for half in range(2):
            feed(f, tok + half)
            if half == 1:
                @pl.when(tok + 2 == per)
                def _():
                    put_unit(2 * f)
                    put_unit(2 * f + 1)
            rolling_tick(i, half)
        return carry

    lax.fori_loop(0, feeds * per // 2, feed_pair, 0)
    clock[0] = 2.0 * (feeds * per - 1 - early)
    for u in range(2 * feeds):
        stages = [s for s in range(STAGES) if 4.0 * u + 2.0 * SLOW[s] > clock[0]]
        due[u] = (stages[0], 4.0 * u + 2.0 * SLOW[stages[0]])

    def decays(j):
        slot = j % 2
        return pltpu.make_async_copy(decay_in.at[:, pl.ds(j * wide, wide)], decay_s.at[slot], stream_sems.at[0, slot])

    decays(0).start()
    decays(1).start()

    streams = ((fade_s, fade_in), (rise_s, rise_in), (weight_s, weight_in), (lean_s, lean_in))
    depth = blocks // 2

    def streamed(k, half, i):
        if half == 0:
            return streams[k][0].at[i]
        each = inner // (len(streams) * wide)
        row, column = lax.div(i, each) * size, (lax.rem(i, each) * len(streams) + k) * wide
        return w_up_v.at[pl.ds(pl.multiple_of(row, size), size), pl.ds(pl.multiple_of(column, wide), wide)]

    def stream(j, half, i):
        b = blocks - 1 - half * depth - i
        return [
            pltpu.make_async_copy(source.at[at_block(b), pl.ds(j * wide, wide)], streamed(k, half, i), stream_sems.at[1 + k, half * depth + i])
            for k, (buffer, source) in enumerate(streams)
        ]

    for half in range(2):
        for i in range(depth):
            for copy in stream(0, half, i):
                copy.start()

    def stage_copy(buffer, target, b):
        slot = lax.rem(b, 2)
        return pltpu.make_async_copy(buffer.at[slot], target.at[:, pl.ds(pl.multiple_of(b * block, block), block), :], stage_sems.at[slot])

    def finish_two(b, norm_sum, cot_sum):
        at = at_block(b)

        @pl.when(b >= 2)
        def _():
            stage_copy(mixed_s, mixed_out, b - 2).wait()
        mixed = jnp.swapaxes(mixed_v[at].reshape(block, rows, width), 0, 1)
        mixed_s[lax.rem(b, 2)] = mixed.astype(BF16)
        stage_copy(mixed_s, mixed_out, b).start()
        value, grad, cot = middle_v[at], second_v[at], cot_v[at].astype(F32)
        scale = lax.rsqrt(jnp.mean(value * value, axis=-1, keepdims=True) + EPS)
        plain = value * scale
        norm_sum = norm_sum + jnp.sum((grad * plain).reshape(size // 8, 8, width), axis=0)
        cot_sum = cot_sum + jnp.sum(cot.reshape(size // 8, 8, width), axis=0)
        lean = grad * gains
        back = cot + scale * (lean - plain * jnp.mean(lean * plain, axis=-1, keepdims=True))
        second_v[at] = back
        low_v[at] = back.astype(BF16)
        return norm_sum, cot_sum

    zero = jnp.zeros((8, width), F32)
    norm_sum, cot_sum = beat(blocks, finish_two, 2, 2.4, zero, zero)
    for b in (blocks - 2, blocks - 1):
        stage_copy(mixed_s, mixed_out, b).wait()
    put_small(20, jnp.sum(norm_sum, axis=0, keepdims=True))
    put_small(24, sums_v[0:1])
    put_small(40, jnp.sum(cot_sum, axis=0, keepdims=True))

    loads[4].wait()
    loads[5].wait()

    def half_of(refs, j):
        return refs[j // 2], slice(UNIT * (j % 2), UNIT * (j % 2) + UNIT)

    def back_states():
        def one(tok, carry):
            at = at_block(tok, big)
            back = dot_nt(low_v[at], w_out_v[...])
            mixed_v[at] = back[:, :SPAN]
            middle_v[at] = back[:, SPAN:]
            return carry

        lax.fori_loop(0, per, one, 0)
        tick(2.0)

    def first_pass(j):
        flows, lanes = half_of((mixed_v, middle_v), j)
        decays(j).wait()

        def one(i, carry):
            product, flow = carry
            b = blocks - 1 - i
            for t in reversed(range(block)):
                there = pl.ds(pl.multiple_of(b * size + t * rows, rows), rows)
                decay = decay_s[j % 2, there]
                flow = decay * (flows[there, lanes] + flow)
                product = decay * product
            return product, flow

        product, flow = lax.fori_loop(0, blocks, one, (jnp.ones((rows, wide), F32), jnp.zeros((rows, wide), F32)))
        chain.start(j, product, flow)
        decays((j + 2) % parts).start()
        tick(0.6)

    def grad_out():
        for j in range(hidden // SPAN):
            def one(tok, carry):
                at = at_block(tok, big)
                gather(2 * feeds + j, dot_tn(state_v[at, pl.ds(j * SPAN, SPAN)], low_v[at]), tok == 0)
                return carry

            lax.fori_loop(0, per, one, 0)
            put_unit(2 * feeds + j)
            enter(2 * feeds + j)
            tick(2.0)

    gains_one = gain_one[...]

    def norm_one(b):
        at = at_block(b)
        value = x_v[at].astype(F32)
        scale = lax.rsqrt(jnp.mean(value * value, axis=-1, keepdims=True) + EPS)
        turned_v[:, at] = jnp.swapaxes(value * scale * gains_one, 0, 1).astype(BF16)
        return ()

    back_states()
    work = [functools.partial(first_pass, j) for j in range(parts)]
    work += [grad_out]

    def turn():
        loads[6].wait()
        beat(blocks, norm_one, 1, 1.6)

    work.append(turn)
    for step in range(max(len(work), parts + chain.rounds)):
        if step < len(work):
            work[step]()
        else:
            tick(1.0)
        for i in range(parts):
            if 0 <= step - 1 - i < chain.rounds:
                chain.advance(i, step - 1 - i)

    cand_refs = (low_v, cand_v)
    input_refs = (cot_v, w_down_v)

    def second_pass(j):
        flows, lanes = half_of((mixed_v, middle_v), j)
        to_input, to_cand = half_of(input_refs, j)[0], half_of(cand_refs, j)[0]
        decays(j).wait()

        def one(half, i, carry):
            flow, sum_f, sum_i = carry
            b = blocks - 1 - half * depth - i
            for copy in stream(j, half, i):
                copy.wait()
            fade, rise, weight, lean_part = (streamed(k, half, i) for k in range(len(streams)))
            for t in reversed(range(block)):
                here = pl.ds(t * rows, rows)
                there = pl.ds(pl.multiple_of(b * size + t * rows, rows), rows)
                reach = flows[there, lanes] + flow
                flow = decay_s[j % 2, there] * reach
                lean = reach * lean_part[here].astype(F32)
                grad_f = fade[here].astype(F32) * lean
                grad_i = -(rise[here].astype(F32) * lean)
                sum_f, sum_i = sum_f + grad_f, sum_i + grad_i
                state_v[there, wide * j : wide * j + wide] = grad_f.astype(BF16)
                to_input[there, lanes] = grad_i.astype(BF16)
                to_cand[there, lanes] = (weight[here].astype(F32) * reach).astype(BF16)
            if j + 1 < parts:
                for copy in stream(j + 1, half, i):
                    copy.start()
            return flow, sum_f, sum_i

        none = jnp.zeros((rows, wide), F32)
        carry = (join[j, 1], none, none)
        for half in range(2):
            carry = lax.fori_loop(0, depth, functools.partial(one, half), carry)
        unused, sum_f, sum_i = carry
        tick(1.2)
        if j + 2 < parts:
            decays(j + 2).start()
        put_small(4 + 2 * j, jnp.sum(sum_f, axis=0, keepdims=True))
        put_small(12 + 2 * j, jnp.sum(sum_i, axis=0, keepdims=True))

    def grad_in(j):
        unit = 2 * feeds + hidden // SPAN + 3 * j

        lanes = half_of(input_refs, j)[1]
        pieces = ((state_v, slice(wide * j, wide * j + wide)), (half_of(input_refs, j)[0], lanes), (half_of(cand_refs, j)[0], lanes))
        over = [u for u in range(2 * feeds + hidden // SPAN) if plan[u][0] in {plan[unit + k][0] for k in range(3)} and u not in settled]
        settled.update(over)
        assert all(due[u][0] > 7 for u in over)
        if ringed and over:
            ring.settle_sums(over)
        for k, (ref, columns) in enumerate(pieces):
            slot, column, length = plan[unit + k]
            grads[slot, :, pl.ds(column, length)] = dot(turned_v[...], ref[:, columns])
            put_unit(unit + k)
            enter(unit + k)
            tick(0.5)

    settled = set()
    for j in range(parts):
        second_pass(j)
        if j == parts - 1:
            loads[8].start()
        grad_in(j)

    for k in (7, 8):
        loads[k].wait()
    project_refs = [(state_v, slice(0, hidden), w_up_v, 0)]
    for k, refs in enumerate((input_refs, cand_refs)):
        for half in range(2):
            column = (k + 1) * hidden + half * SPAN
            wide_ref, column = (w_up_v, column) if column < inner else (w_in_v, column - inner)
            project_refs.append((refs[half], slice(None), wide_ref, column))

    def finish_one(tok, norm_sum):
        at = at_block(tok, big)
        grad_all = jnp.zeros((big, width), F32)
        for ref, columns, weight, column in project_refs:
            piece = ref[at, columns]
            grad_all = grad_all + dot_nt(piece, weight[:, column : column + piece.shape[1]])
        for k in range(big // size):
            b = tok * (big // size) + k

            @pl.when(b >= 2)
            def _():
                stage_copy(tokens_s, tokens_out, b - 2).wait()
            here = at_block(b)
            grad = grad_all[k * size : k * size + size]
            value = x_v[here].astype(F32)
            scale = lax.rsqrt(jnp.mean(value * value, axis=-1, keepdims=True) + EPS)
            plain = value * scale
            norm_sum = norm_sum + jnp.sum((grad * plain).reshape(size // 8, 8, width), axis=0)
            lean = grad * gains_one
            back = second_v[here] + scale * (lean - plain * jnp.mean(lean * plain, axis=-1, keepdims=True))
            tokens_s[lax.rem(b, 2)] = jnp.swapaxes(back.reshape(block, rows, width), 0, 1)
            stage_copy(tokens_s, tokens_out, b).start()
        return (norm_sum,)

    (norm_sum,) = beat(per, finish_one, 4, 9.0, jnp.zeros((8, width), F32))
    put_small(0, jnp.sum(norm_sum, axis=0, keepdims=True))
    if ringed:
        step = 0
        while step <= DOUBLINGS or any(due[unit][0] < STAGES for unit in due):
            tick(1.0)
            if step <= DOUBLINGS:
                small.step(step)
            step += 1
        ring.settle_sums([u for u in due if u not in settled])
        ring.settle_lines(list(due))
        copy = pltpu.make_async_copy(own_v.at[DOUBLINGS], small_out.at[0], load_sems.at[0])
    else:
        copy = pltpu.make_async_copy(small_v, small_out.at[0], load_sems.at[0])
    copy.start()
    copy.wait()
    for b in (blocks - 2, blocks - 1):
        stage_copy(tokens_s, tokens_out, b).wait()
    for j in range(parts):
        chain.finish(j)


def back(ringed, shape_in, x, cot, middle, state, decay, fade, rise, weight, lean, gain_one, gain_two, up_bias, down_bias, w_in, w_out, w_up, w_down, cid=2):
    rows, steps, width = shape_in
    total = rows * steps
    hidden = w_out.shape[0]
    inner = w_down.shape[0]
    count = lax.axis_size("seq")
    block = 16
    size = block * rows
    wide = UNIT
    parts = hidden // wide
    feeds = inner // SPAN
    whole = 2 * feeds + hidden // SPAN
    plan = [(u, 0, WIDE) for u in range(whole)]
    for k in range(3 * parts):
        plan.append(((whole + k // 2) % SLOTS, k % 2 * UNIT, UNIT))
    units = len(plan)
    anywhere = pl.BlockSpec(memory_space=pl.ANY)
    vmem = pl.BlockSpec(memory_space=pltpu.VMEM)
    shape = jax.ShapeDtypeStruct
    if ringed:
        first, *others = sum_scratch(units, whole, SLOTS)
        more = [first, pltpu.VMEM((DOUBLINGS + 1, SMALL_ROWS, 128), F32), *others]
        more += [pltpu.VMEM((DOUBLINGS, SMALL_ROWS, 128), F32)] + [pltpu.SemaphoreType.DMA((DOUBLINGS,))] * 2
    else:
        more = [pltpu.VMEM((SLOTS, SPAN, WIDE), F32), pltpu.VMEM((1, SMALL_ROWS, 128), F32)]
    return pl.pallas_call(
        functools.partial(back_kernel, ringed, count, rows, steps, plan, block),
        out_shape=(
            shape(shape_in, BF16), shape(shape_in, F32), shape((units, SPAN, WIDE), F32), shape((1, SMALL_ROWS, 128), F32),
        ),
        in_specs=[anywhere] * 9 + [vmem] * 4 + [anywhere] * 4,
        out_specs=(anywhere,) * 4,
        scratch_shapes=[
            pltpu.VMEM((total, width), F32), pltpu.VMEM((total, width), F32), pltpu.VMEM((total, width), F32),
            pltpu.VMEM((total, hidden), BF16), pltpu.VMEM((total, width), BF16), pltpu.VMEM((total, width), BF16), pltpu.VMEM((total, width), BF16),
            pltpu.VMEM((total, width), BF16), pltpu.VMEM((width, total), BF16),
            pltpu.VMEM((width, w_in.shape[1] - inner), BF16), pltpu.VMEM(w_out.shape, BF16), pltpu.VMEM(w_up.shape, BF16), pltpu.VMEM(w_down.shape, BF16),
            pltpu.VMEM((2, total, wide), F32), pltpu.VMEM((4, size, wide), BF16), pltpu.VMEM((4, size, wide), BF16),
            pltpu.VMEM((4, size, wide), BF16), pltpu.VMEM((4, size, wide), BF16),
            pltpu.VMEM((2, rows, block, width), BF16), pltpu.VMEM((2, rows, block, width), F32), pltpu.VMEM((8, inner), F32),
            pltpu.SemaphoreType.DMA((9,)), pltpu.SemaphoreType.DMA((5, 8)), pltpu.SemaphoreType.DMA((2,)),
            *chain_scratch(parts, count, rows, wide),
            *more,
        ],
        compiler_params=pltpu.CompilerParams(collective_id=cid, has_side_effects=True, vmem_limit_bytes=63 * 2**20 + 2**19),
        cost_estimate=pl.CostEstimate(flops=2 * total * width * (8 * hidden + 6 * inner), bytes_accessed=80 * 2**20, transcendentals=total * inner),
        name="back",
    )(x, cot, middle, state, decay, fade, rise, weight, lean, gain_one.reshape(1, -1), gain_two.reshape(1, -1), up_bias.reshape(1, -1), down_bias.reshape(1, -1), w_in, w_out, w_up, w_down)


def settle_kernel(places, mixed, tokens, units, small, *refs):
    outs, (mixed_v, tokens_v, units_v, reads, writes) = refs[:-5], refs[-5:]
    copies = []
    for k in range(mixed.shape[0] // 4):
        some = pl.ds(4 * k, 4)
        copies.append((tokens.at[some], tokens_v.at[some], outs[1].at[some]))
        copies.append((mixed.at[some], mixed_v.at[some], outs[0].at[some]))
    for u, length, array, row, column in places:
        lanes = pl.ds(0, length)
        copies.append((units.at[u, :, lanes], units_v.at[u, :, lanes], outs[2 + array].at[pl.ds(row, SPAN), pl.ds(column, length)]))
    moves = [
        (pltpu.make_async_copy(a, b, reads.at[k]), pltpu.make_async_copy(b, c, writes.at[k])) for k, (a, b, c) in enumerate(copies)
    ]
    for read, write in moves:
        read.start()
    row = 0
    for out in outs[6:]:
        out[...] = small[0, pl.ds(row, out.shape[0])]
        row += out.shape[0]
    for read, write in moves:
        read.wait()
        write.start()
    for read, write in moves:
        write.wait()


def settle(mixed, tokens, units, small, hidden, inner):
    width = tokens.shape[-1]
    parts = hidden // UNIT
    feeds = inner // SPAN
    places = []
    for f in range(feeds):
        places += [(2 * f, SPAN, 3, f * SPAN, 0), (2 * f + 1, SPAN, 2, 0, f * SPAN)]
    places += [(2 * feeds + j, SPAN, 1, j * SPAN, 0) for j in range(hidden // SPAN)]
    for j in range(parts):
        places += [(len(places) + k, UNIT, 0, 0, k * hidden + j * UNIT) for k in range(3)]
    anywhere = pl.BlockSpec(memory_space=pl.ANY)
    vmem = pl.BlockSpec(memory_space=pltpu.VMEM)
    shape = jax.ShapeDtypeStruct
    lengths = (width, hidden, hidden, width, inner, width)
    return pl.pallas_call(
        functools.partial(settle_kernel, places),
        out_shape=(
            shape(mixed.shape, mixed.dtype), shape(tokens.shape, F32), shape((width, 3 * hidden), F32), shape((hidden, width), F32),
            shape((width, inner), F32), shape((inner, width), F32), *(shape((n // 128, 128), F32) for n in lengths),
        ),
        in_specs=[anywhere] * 3 + [vmem],
        out_specs=(anywhere,) * 6 + (vmem,) * 6,
        scratch_shapes=[
            pltpu.VMEM(mixed.shape, mixed.dtype), pltpu.VMEM(tokens.shape, F32), pltpu.VMEM(units.shape, F32),
            pltpu.SemaphoreType.DMA((mixed.shape[0] // 2 + len(places),)), pltpu.SemaphoreType.DMA((mixed.shape[0] // 2 + len(places),)),
        ],
        compiler_params=pltpu.CompilerParams(vmem_limit_bytes=63 * 2**20),
        name="settle",
    )(mixed, tokens, units, small)


def on_device(tokens, cotangent, reset_pos, norm1_gain, w_in, forget_bias, input_bias, w_out, norm2_gain, w_up, up_bias, w_down, down_bias):
    ringed = lax.axis_size("seq") == 8 and lax.axis_size("rows") == 4
    hidden, inner = w_out.shape[0], w_down.shape[0]
    kept = front(tokens, cotangent, reset_pos, norm1_gain, w_in, forget_bias, input_bias, w_out)
    mixed, grad_tokens, units, small = back(
        ringed, tokens.shape, *kept, norm1_gain, norm2_gain, up_bias, down_bias, w_in, w_out, w_up, w_down
    )
    if not ringed:
        units, small = lax.psum((units, small), ("seq", "rows"))
    mixed, grad_tokens, grad_in, grad_out, grad_up, grad_down, *rest = settle(mixed, grad_tokens, units, small, hidden, inner)
    norm_one, forget, inputs, norm_two, up, down = (one.reshape(-1) for one in rest)
    return mixed, grad_tokens, norm_one, grad_in, forget, inputs, grad_out, norm_two, grad_up, up, grad_down, down


def solution(mesh):
    return jax.shard_map(
        on_device,
        mesh=mesh,
        in_specs=(
            P("rows", "seq", None),
            P("rows", "seq", None),
            P("rows", None),
            P(),
            P(),
            P(),
            P(),
            P(),
            P(),
            P(),
            P(),
            P(),
            P(),
        ),
        out_specs=(
            P("rows", "seq", None),
            P("rows", "seq", None),
            P(),
            P(),
            P(),
            P(),
            P(),
            P(),
            P(),
            P(),
            P(),
            P(),
        ),
        check_vma=False,
    )
```

```python
import functools
import math
import jax
import jax.numpy as jnp
from jax import lax
from jax.experimental import pallas as pl
from jax.experimental.pallas import tpu as pltpu
from jax.sharding import PartitionSpec as P

MESH = pl.DeviceIdType.MESH
EPS = 1e-6
F32 = jnp.float32
BF16 = jnp.bfloat16
STAGES = 13
KINDS = 10
SPAN = 512
UNIT = 256
WIDE = 512
SLOTS = 10
SIDE = 8
SMALL_ROWS = 48
DOUBLINGS = 5
SLOW = (0, 1, 3, 6, 8, 10, 11, 12, 14, 16, 19, 21, 22)
FAST = (0, 1, 5, 10, 14, 17, 19, 22, 24, 28, 33, 37, 38)


def place():
    seq = lax.axis_index("seq")
    rows = lax.axis_index("rows")
    return lax.div(rows, 2), lax.rem(seq, 2), lax.div(seq, 2), lax.rem(rows, 2)


def spot(x, y, z, core):
    return (z * 2 + y, x * 2 + core)


def dot(left, right):
    return jnp.dot(left, right, preferred_element_type=F32)


def dot_nt(left, right):
    return lax.dot_general(left, right, (((1,), (1,)), ((), ())), preferred_element_type=F32)


def dot_tn(left, right):
    return lax.dot_general(left, right, (((0,), (0,)), ((), ())), preferred_element_type=F32)


class Chain:
    def __init__(self, count, sign, sent, got, join, send, recv):
        self.count, self.sign = count, sign
        self.sent, self.got, self.join = sent, got, join
        self.send, self.recv = send, recv
        self.rounds = max(1, math.ceil(math.log2(count)))
        seq = lax.axis_index("seq")
        self.seq = seq
        self.place = seq if sign > 0 else count - 1 - seq

    def partners(self):
        for r in range(self.rounds):
            far = 2**r
            yield self.seq + self.sign * far, self.place + far < self.count
            yield self.seq - self.sign * far, self.place >= far

    def copy(self, part, r, other):
        return pltpu.make_async_remote_copy(
            src_ref=self.sent.at[part, r], dst_ref=self.got.at[part, r],
            send_sem=self.send.at[part, r], recv_sem=self.recv.at[part, r],
            device_id=(other, lax.axis_index("rows")), device_id_type=MESH,
        )

    def push(self, part, r):
        @pl.when(self.place + 2**r < self.count)
        def _():
            self.copy(part, r, self.seq + self.sign * 2**r).start()

    def start(self, part, product, end):
        self.sent[part, 0, 0] = product
        self.sent[part, 0, 1] = end
        self.join[part, 0] = jnp.ones_like(product)
        self.join[part, 1] = jnp.zeros_like(end)
        self.push(part, 0)

    def advance(self, part, r):
        last = r == self.rounds - 1

        @pl.when(self.place >= 2**r)
        def _():
            self.copy(part, r, self.seq - self.sign * 2**r).wait_recv()
            product, end = self.got[part, r, 0], self.got[part, r, 1]
            own = self.join[part, 0]
            self.join[part, 1] = self.join[part, 1] + own * end
            if not last:
                self.join[part, 0] = own * product
                here = self.sent[part, r, 0]
                self.sent[part, r + 1, 0] = here * product
                self.sent[part, r + 1, 1] = self.sent[part, r, 1] + here * end

        if not last:
            @pl.when(self.place < 2**r)
            def _():
                self.sent[part, r + 1] = self.sent[part, r]
            self.push(part, r + 1)

    def finish(self, part):
        for r in range(self.rounds):
            @pl.when(self.place + 2**r < self.count)
            def _():
                self.copy(part, r, self.seq + self.sign * 2**r).wait_send()


def greet_chain(chain):
    barrier = pltpu.get_barrier_semaphore()
    rows = lax.axis_index("rows")
    total = 0
    for other, there in chain.partners():
        @pl.when(there)
        def _():
            pl.semaphore_signal(barrier, inc=1, device_id=(other, rows), device_id_type=MESH)
        total = total + jnp.where(there, 1, 0)
    return barrier, total


def chain_scratch(parts, count, rows, width):
    rounds = max(1, math.ceil(math.log2(count)))
    return [
        pltpu.VMEM((parts, rounds, 2, rows, width), F32),
        pltpu.VMEM((parts, rounds, 2, rows, width), F32),
        pltpu.VMEM((parts, 2, rows, width), F32),
        pltpu.SemaphoreType.DMA((parts, rounds)),
        pltpu.SemaphoreType.DMA((parts, rounds)),
    ]


def front_kernel(
    count, rows, steps, chunk, block,
    tokens, cotangent, reset_in, gain, w_in, forget_bias, input_bias, w_out,
    x_out, cot_out, middle_out, state_out, decay_out, fade_out, rise_out, weight_out, lean_out,
    reset, tok_v, cot_v, x_v, normed_v, w_v, w_out_v, keep_v, decay_v, update_v, cand_v, fade_v, rise_v, weight_v, lean_v, state_v, middle_v,
    sent, got, join, send, recv, sems, out_sems,
):
    total, width = x_v.shape
    hidden = w_out_v.shape[0]
    parts = hidden // chunk
    size = block * rows
    blocks = steps // block
    side = math.gcd(blocks, SIDE)
    chain = Chain(count, 1, sent, got, join, send, recv)
    barrier, greeted = greet_chain(chain)
    loads = [pltpu.make_async_copy(tokens, tok_v, sems.at[0])]
    for j in range(parts):
        for k in range(3):
            loads.append(pltpu.make_async_copy(w_in.at[:, pl.ds(k * hidden + j * chunk, chunk)], w_v.at[j, :, pl.ds(k * chunk, chunk)], sems.at[1 + 3 * j + k]))
    loads.append(pltpu.make_async_copy(cotangent, cot_v, sems.at[1 + 3 * parts]))
    loads.append(pltpu.make_async_copy(w_out, w_out_v, sems.at[2 + 3 * parts]))
    marks_in = pltpu.make_async_copy(reset_in, reset, sems.at[3 + 3 * parts])
    marks_in.start()
    for load in loads:
        load.start()
    marks_in.wait()
    loads[0].wait()

    first = lax.axis_index("seq") * steps
    marks = [jnp.broadcast_to(reset[:, k : k + 1], (rows, 128)) for k in range(reset.shape[1])]

    def mark(t, carry):
        hit = marks[0] == first + t
        for one in marks[1:]:
            hit = hit | (one == first + t)
        keep_v[pl.ds(pl.multiple_of(t * rows, rows), rows)] = jnp.where(hit, 0.0, 1.0)
        return carry

    lax.fori_loop(0, steps, mark, 0, unroll=4)
    gains = gain[...]

    def norm(b, carry):
        at = pl.ds(pl.multiple_of(b * size, size), size)
        x = tok_v[:, pl.ds(pl.multiple_of(b * block, block), block), :].astype(F32)
        x = jnp.swapaxes(x, 0, 1).reshape(size, width)
        x_v[at] = x.astype(BF16)
        scale = lax.rsqrt(jnp.mean(x * x, axis=-1, keepdims=True) + EPS)
        normed_v[at] = (x * scale * gains).astype(BF16)
        return carry

    lax.fori_loop(0, blocks, norm, 0)
    outs = [pltpu.make_async_copy(x_v, x_out, out_sems.at[0])]
    outs[0].start()

    def gates(j):
        lanes = pl.ds(j * chunk, chunk)
        shift_f, shift_i = -forget_bias[:, lanes], -input_bias[:, lanes]

        def some(project, at, product, end):
            neg_f = shift_f - project[:, :chunk]
            neg_i = shift_i - project[:, chunk : 2 * chunk]
            cand = project[:, 2 * chunk :]
            lower = jnp.maximum(jnp.minimum(neg_f, neg_i) - 20.0, 0.0)
            exp_f = jnp.exp(jnp.minimum(neg_f - lower, 80.0))
            exp_i = jnp.exp(jnp.minimum(neg_i - lower, 80.0))
            one_f, one_i = 1.0 + exp_f, 1.0 + exp_i
            share = 1.0 / (one_f + one_i)
            decay, weight = one_i * share, one_f * share
            fade_v[j % 2, at] = (decay * (exp_f * share)).astype(BF16)
            rise_v[j % 2, at] = (weight * (exp_i * share)).astype(BF16)
            weight_v[j % 2, at] = weight.astype(BF16)
            cand_v[at, lanes] = cand
            update = weight * cand
            update_v[at, lanes] = update
            decay = decay * jnp.concatenate([keep_v[at]] * (chunk // 128), axis=1)
            decay_v[at, lanes] = decay
            for t in range(block):
                here = decay[t * rows : (t + 1) * rows]
                end = here * end + update[t * rows : (t + 1) * rows]
                product = here * product
            return product, end

        def one(b, carry):
            places = [pl.ds(pl.multiple_of((b * side + k) * size, size), size) for k in range(side)]
            for at in places:
                carry = some(dot(normed_v[at], w_v[j]), at, *carry)
            return carry

        start = (jnp.ones((rows, chunk), F32), jnp.zeros((rows, chunk), F32))
        return lax.fori_loop(0, blocks // side, one, start)

    def scan(j):
        lanes = pl.ds(j * chunk, chunk)

        def one(b, state):
            for t in range(block):
                here = pl.ds(pl.multiple_of(b * size + t * rows, rows), rows)
                keep = jnp.concatenate([keep_v[here]] * (chunk // 128), axis=1)
                lean_v[j % 2, here] = (keep * state - cand_v[here, lanes]).astype(BF16)
                state = decay_v[here, lanes] * state + update_v[here, lanes]
                state_v[here, lanes] = state.astype(BF16)
            return state

        lax.fori_loop(0, blocks, one, join[j, 1])

    def project_out(b, carry):
        at = pl.ds(pl.multiple_of(b * 2 * size, 2 * size), 2 * size)
        middle_v[at] = x_v[at].astype(F32) + dot(state_v[at], w_out_v[...])
        copy = pltpu.make_async_copy(middle_v.at[at], middle_out.at[at], out_sems.at[2 + 6 * parts])
        copy.start()
        return carry

    def put(source, target, slot, wait=False):
        copy = pltpu.make_async_copy(source, target, out_sems.at[slot])
        if wait:
            copy.wait()
        else:
            copy.start()

    def gate_outs(j, wait=False):
        lanes = pl.ds(j * chunk, chunk)
        for k, (a, b) in enumerate(((fade_v, fade_out), (rise_v, rise_out), (weight_v, weight_out))):
            put(a.at[j % 2], b.at[:, lanes], 1 + 3 * j + k, wait)
        put(decay_v.at[:, lanes], decay_out.at[:, lanes], 1 + 3 * parts + j, wait)

    def scan_outs(j, wait=False):
        lanes = pl.ds(j * chunk, chunk)
        put(lean_v.at[j % 2], lean_out.at[:, lanes], 1 + 4 * parts + 2 * j, wait)
        put(state_v.at[:, lanes], state_out.at[:, lanes], 2 + 4 * parts + 2 * j, wait)

    ready = 0
    for j in range(parts):
        for k in range(3):
            loads[1 + 3 * j + k].wait()
        if j >= 2:
            gate_outs(j - 2, True)
        product, end = gates(j)
        gate_outs(j)
        if j == 0:
            pl.semaphore_wait(barrier, greeted)
        chain.start(j, product, end)
        for i in range(j - 1, -1, -1):
            if j - 1 - i < chain.rounds:
                chain.advance(i, j - 1 - i)
    for k in range(2):
        loads[1 + 3 * parts + k].wait()

    def turn(b, carry):
        at = pl.ds(pl.multiple_of(b * size, size), size)
        c = cot_v[:, pl.ds(pl.multiple_of(b * block, block), block), :].astype(F32)
        normed_v[at] = jnp.swapaxes(c, 0, 1).reshape(size, width).astype(BF16)
        return carry

    lax.fori_loop(0, blocks, turn, 0)
    put(normed_v, cot_out, 1 + 6 * parts)

    step = parts - 1
    while ready < parts:
        for i in range(parts - 1, -1, -1):
            if 0 <= step - 1 - i < chain.rounds and step >= parts:
                chain.advance(i, step - 1 - i)
        while ready < parts and ready + chain.rounds <= step:
            if ready >= 2:
                scan_outs(ready - 2, True)
            scan(ready)
            scan_outs(ready)
            ready += 1
        step += 1
    lax.fori_loop(0, blocks // 2, project_out, 0)
    for j in range(parts):
        if j >= parts - 2:
            gate_outs(j, True)
            scan_outs(j, True)
        chain.finish(j)
    outs[0].wait()
    put(normed_v, cot_out, 1 + 6 * parts, True)
    put(middle_v, middle_out, 2 + 6 * parts, True)


def front(tokens, cotangent, reset, gain, w_in, forget_bias, input_bias, w_out, cid=1):
    rows, steps, width = tokens.shape
    hidden = w_out.shape[0]
    total = rows * steps
    count = lax.axis_size("seq")
    chunk, block = 256, 16
    parts = hidden // chunk
    anywhere = pl.BlockSpec(memory_space=pl.ANY)
    vmem = pl.BlockSpec(memory_space=pltpu.VMEM)
    shape = jax.ShapeDtypeStruct
    return pl.pallas_call(
        functools.partial(front_kernel, count, rows, steps, chunk, block),
        out_shape=(
            shape((total, width), BF16), shape((total, width), BF16), shape((total, width), F32),
            shape((total, hidden), BF16), shape((total, hidden), F32), shape((total, hidden), BF16),
            shape((total, hidden), BF16), shape((total, hidden), BF16), shape((total, hidden), BF16),
        ),
        in_specs=[anywhere, anywhere, anywhere, vmem, anywhere, vmem, vmem, anywhere],
        out_specs=(anywhere,) * 9,
        scratch_shapes=[
            pltpu.VMEM(reset.shape, jnp.int32), pltpu.VMEM(tokens.shape, BF16), pltpu.VMEM(tokens.shape, BF16), pltpu.VMEM((total, width), BF16), pltpu.VMEM((total, width), BF16),
            pltpu.VMEM((parts, width, 3 * chunk), BF16), pltpu.VMEM(w_out.shape, BF16), pltpu.VMEM((total, 128), F32),
            pltpu.VMEM((total, hidden), F32), pltpu.VMEM((total, hidden), F32), pltpu.VMEM((total, hidden), F32),
            pltpu.VMEM((2, total, chunk), BF16), pltpu.VMEM((2, total, chunk), BF16), pltpu.VMEM((2, total, chunk), BF16),
            pltpu.VMEM((2, total, chunk), BF16), pltpu.VMEM((total, hidden), BF16), pltpu.VMEM((total, width), F32),
            *chain_scratch(parts, count, rows, chunk),
            pltpu.SemaphoreType.DMA((4 + 3 * parts,)), pltpu.SemaphoreType.DMA((3 + 6 * parts,)),
        ],
        compiler_params=pltpu.CompilerParams(collective_id=cid, has_side_effects=True, vmem_limit_bytes=62 * 2**20),
        cost_estimate=pl.CostEstimate(flops=2 * total * width * 4 * hidden, bytes_accessed=40 * 2**20, transcendentals=3 * total * hidden),
        name="front",
    )(tokens, cotangent, reset, gain.reshape(1, -1), w_in, forget_bias.reshape(1, -1), input_bias.reshape(1, -1), w_out)


class Summing:
    def __init__(self, plan, grads, half_in, part_in, lines_in, last_in, send, recv, local, free, result):
        self.plan, self.grads = plan, grads
        self.whole = sum(width == WIDE for slot, column, width in plan)
        self.half_in, self.part_in, self.lines_in, self.last_in = half_in, part_in, lines_in, last_in
        self.result, self.send, self.recv, self.local, self.free = result, send, recv, local, free
        x, y, z, core = place()
        self.z = z
        first = core == 0
        self.sibling = spot(x, y, z, 1 - core)
        along_x, along_y = spot(1 - x, y, z, core), spot(x, 1 - y, z, core)
        self.near = tuple(jnp.where(first, a, b) for a, b in zip(along_x, along_y))
        self.far = tuple(jnp.where(first, b, a) for a, b in zip(along_x, along_y))
        self.above = spot(x, y, z + 1, core)
        self.below = spot(x, y, z - 1, core)
        near_bit = jnp.where(first, x, y)
        far_bit = jnp.where(first, y, x)
        self.n_half, self.n_part, self.n_line, self.n_tip = SPAN // 2, SPAN // 4, SPAN // 16, SPAN // 32
        self.half = core * self.n_half
        self.other_half = (1 - core) * self.n_half
        self.part = self.half + near_bit * self.n_part
        self.other_part = self.half + (1 - near_bit) * self.n_part
        self.tip = self.part + self.n_line * z + self.n_tip * far_bit
        self.other_tip = self.part + self.n_line * z + self.n_tip * (1 - far_bit)

    def copy(self, kind, unit, source, target, device):
        return pltpu.make_async_remote_copy(
            src_ref=source, dst_ref=target, send_sem=self.send.at[kind, unit], recv_sem=self.recv.at[kind, unit],
            device_id=device, device_id_type=MESH,
        )

    def slot_of(self, u):
        return self.plan[u] if isinstance(u, int) else (u, 0, WIDE)

    def rows(self, u, start, count):
        slot, column, width = self.slot_of(u)
        return self.grads.at[slot, pl.ds(pl.multiple_of(start, 8), count), pl.ds(column, width)]

    def done(self, u, start, count):
        return self.result.at[u, pl.ds(pl.multiple_of(start, 8), count), pl.ds(0, self.slot_of(u)[2])]

    def land(self, ref, wide, u, start, count):
        if self.slot_of(u)[2] == WIDE:
            return ref.at[lax.rem(u, wide), pl.ds(start, count)]
        turn = (u - self.whole) % (2 * (ref.shape[0] - wide))
        return ref.at[wide + turn // 2, pl.ds(start, count), pl.ds(turn % 2 * UNIT, UNIT)]

    def turns(self, kind, u):
        ref, wide = ((self.half_in, 2), (self.part_in, 3), (self.lines_in, 3), (self.lines_in, 3))[kind]
        if self.slot_of(u)[2] == WIDE:
            return wide, 0, self.whole
        return 2 * (ref.shape[0] - wide), self.whole, len(self.plan)

    def claim(self, kind, u):
        apart, first, last = self.turns(kind, u)
        if isinstance(u, int):
            if u - apart >= first:
                pl.semaphore_wait(self.free.at[kind, u - apart], 1)
        else:
            @pl.when(u >= apart)
            def _():
                pl.semaphore_wait(self.free.at[kind, u - apart], 1)

    def release(self, kind, u, sender):
        apart, first, last = self.turns(kind, u)

        def signal():
            pl.semaphore_signal(self.free.at[kind, u], inc=1, device_id=sender, device_id_type=MESH)

        if isinstance(u, int):
            if u + apart < last:
                signal()
        else:
            pl.when(u + apart < last)(signal)

    def land_half(self, u):
        return self.land(self.half_in, 2, u, 0, self.n_half)

    def land_part(self, u):
        return self.land(self.part_in, 3, u, 0, self.n_part)

    def land_up(self, u, z):
        return self.land(self.lines_in, 3, u, 0, self.n_line * (4 - z))

    def land_down(self, u, z):
        return self.land(self.lines_in, 3, u, self.n_line * (4 - z) if z > 0 else 0, self.n_line * (z + 1))

    def land_last(self, u):
        return self.land(self.last_in, self.whole, u, 0, self.n_tip)

    def c_half(self, u):
        return self.copy(0, u, self.rows(u, self.other_half, self.n_half), self.land_half(u), self.sibling)

    def c_part(self, u):
        return self.copy(1, u, self.rows(u, self.other_part, self.n_part), self.land_part(u), self.near)

    def c_up(self, u, z):
        low, rest = self.n_line * (z + 1), self.n_line * (3 - z)
        return self.copy(2, u, self.rows(u, self.part + low, rest), self.land_up(u, z + 1), self.above)

    def c_down(self, u, z):
        rest = self.n_line * z
        return self.copy(3, u, self.rows(u, self.part, rest), self.land_down(u, z - 1), self.below)

    def c_last(self, u):
        return self.copy(4, u, self.rows(u, self.other_tip, self.n_tip), self.land_last(u), self.far)

    def c_own(self, u):
        return pltpu.make_async_copy(self.rows(u, self.tip, self.n_tip), self.done(u, self.tip, self.n_tip), self.local.at[u])

    def c_far(self, u, start):
        return self.copy(5, u, self.rows(u, start, self.n_tip), self.done(u, start, self.n_tip), self.far)

    def c_rise(self, u, z):
        piece = self.done(u, self.part, self.n_line * (z + 1))
        return self.copy(6, u, piece, piece, self.above)

    def c_fall(self, u, z):
        piece = self.done(u, self.part + self.n_line * z, self.n_line * (4 - z))
        return self.copy(7, u, piece, piece, self.below)

    def c_near(self, u, start):
        piece = self.done(u, start, self.n_part)
        return self.copy(8, u, piece, piece, self.near)

    def c_sibling(self, u, start):
        piece = self.done(u, start, self.n_half)
        return self.copy(9, u, piece, piece, self.sibling)

    def add(self, u, start, count, ref):
        slot, column, width = self.slot_of(u)
        step = min(count, 128)
        lanes = pl.ds(column, width)

        def one(i, carry):
            here = pl.ds(pl.multiple_of(start + i * step, 8), step)
            there = pl.ds(pl.multiple_of(i * step, 8), step)
            self.grads[slot, here, lanes] = self.grads[slot, here, lanes] + ref[there]
            return carry

        if count == step:
            one(0, 0)
        else:
            lax.fori_loop(0, count // step, one, 0)

    def settle_sums(self, units):
        def sent(k):
            for u in units:
                if k < 3:
                    self.c_up(u, k).wait_send()
                if k > 0:
                    self.c_down(u, k).wait_send()

        self.at_each(sent)

    def settle_lines(self, units):
        def sent(k):
            for u in units:
                if k < 3:
                    self.c_rise(u, k).wait_send()
                if k > 0:
                    self.c_fall(u, k).wait_send()

        self.at_each(sent)

    def at_each(self, action):
        for k in range(4):
            pl.when(self.z == k)(functools.partial(action, k))

    def stage(self, s, u):
        z = self.z
        if s == 0:
            self.claim(0, u)
            self.c_half(u).start()
        elif s == 1:
            self.c_half(u).wait()
            self.add(u, self.half, self.n_half, self.land_half(u))
            self.release(0, u, self.sibling)
            self.claim(1, u)
            self.c_part(u).start()
        elif s == 2:
            self.c_part(u).wait()
            self.add(u, self.part, self.n_part, self.land_part(u))
            self.release(1, u, self.near)
        if 2 <= s <= 5:
            up, down = s - 2, 5 - s

            @pl.when(z == up)
            def _():
                if up > 0:
                    self.c_up(u, up - 1).wait_recv()
                    low, rest = self.n_line * up, self.n_line * (4 - up)
                    self.add(u, self.part + low, rest, self.land_up(u, up))
                    self.release(2, u, self.below)
                if up < 3:
                    self.claim(2, u)
                    self.c_up(u, up).start()

            @pl.when(z == down)
            def _():
                if down < 3:
                    self.c_down(u, down + 1).wait_recv()
                    rest = self.n_line * (down + 1)
                    self.add(u, self.part, rest, self.land_down(u, down))
                    self.release(3, u, self.above)
                if down > 0:
                    self.claim(3, u)
                    self.c_down(u, down).start()
        if s == 5:
            self.c_last(u).start()
        elif s == 6:
            self.c_last(u).wait()
            self.add(u, self.tip, self.n_tip, self.land_last(u))
            self.c_far(u, self.tip).start()
            self.c_own(u).start()
        elif s == 7:
            self.c_far(u, self.tip).wait_send()
            self.c_far(u, self.other_tip).wait_recv()
            self.c_own(u).wait()
        if 7 <= s <= 10:
            up, down = s - 7, 10 - s

            @pl.when(z == up)
            def _():
                if up > 0:
                    self.c_rise(u, up - 1).wait_recv()
                if up < 3:
                    self.c_rise(u, up).start()

            @pl.when(z == down)
            def _():
                if down < 3:
                    self.c_fall(u, down + 1).wait_recv()
                if down > 0:
                    self.c_fall(u, down).start()
        if s == 10:
            self.c_near(u, self.part).start()
        elif s == 11:
            self.c_near(u, self.part).wait_send()
            self.c_near(u, self.other_part).wait_recv()
            self.c_sibling(u, self.half).start()
        elif s == 12:
            self.c_sibling(u, self.half).wait_send()
            self.c_sibling(u, self.other_half).wait_recv()


def sum_scratch(units, whole, slots):
    pairs = (units - whole + 1) // 2
    return [
        pltpu.VMEM((slots, SPAN, WIDE), F32),
        pltpu.VMEM((2 + min(pairs, 2), SPAN // 2, WIDE), F32),
        pltpu.VMEM((3 + min(pairs, 4), SPAN // 4, WIDE), F32),
        pltpu.VMEM((3 + pairs, 5 * SPAN // 16, WIDE), F32),
        pltpu.VMEM((whole + pairs, SPAN // 32, WIDE), F32),
        pltpu.SemaphoreType.DMA((KINDS, units)),
        pltpu.SemaphoreType.DMA((KINDS, units)),
        pltpu.SemaphoreType.DMA((units,)),
        pltpu.SemaphoreType.REGULAR((4, units)),
    ]


class Doubling:
    def __init__(self, own, got, send, recv):
        self.own, self.got, self.send, self.recv = own, got, send, recv
        x, y, z, core = place()
        self.partners = (
            spot(x, y, z, 1 - core), spot(1 - x, y, z, core), spot(x, 1 - y, z, core),
            spot(x, y, z + 1 - 2 * lax.rem(z, 2), core), spot(x, y, z + 2 - 4 * lax.div(z, 2), core),
        )

    def copy(self, k):
        return pltpu.make_async_remote_copy(
            src_ref=self.own.at[k], dst_ref=self.got.at[k], send_sem=self.send.at[k], recv_sem=self.recv.at[k],
            device_id=self.partners[k], device_id_type=MESH,
        )

    def step(self, k):
        if k > 0:
            self.copy(k - 1).wait()
            self.own[k] = self.own[k - 1] + self.got[k - 1]
        if k < DOUBLINGS:
            self.copy(k).start()


def greet_ring(ring):
    barrier = pltpu.get_barrier_semaphore()
    for there in (ring.sibling, ring.near, ring.far):
        pl.semaphore_signal(barrier, inc=1, device_id=there, device_id_type=MESH)

    @pl.when(ring.z > 0)
    def _():
        pl.semaphore_signal(barrier, inc=1, device_id=ring.below, device_id_type=MESH)

    @pl.when(ring.z < 3)
    def _():
        pl.semaphore_signal(barrier, inc=1, device_id=ring.above, device_id_type=MESH)

    return 3 + jnp.where(ring.z > 0, 1, 0) + jnp.where(ring.z < 3, 1, 0)


GELU_A = math.sqrt(2.0 / math.pi)
GELU_B = GELU_A * 0.044715


def back_kernel(
    ringed, count, rows, steps, plan, block,
    x_in, cot_in, middle_in, state_in, decay_in, fade_in, rise_in, weight_in, lean_in,
    gain_one, gain_two, up_bias, down_bias, w_in, w_out, w_up, w_down,
    mixed_out, tokens_out, result, small_out,
    middle_v, second_v, mixed_v, state_v, cot_v, x_v, low_v, cand_v, turned_v, w_in_v, w_out_v, w_up_v, w_down_v,
    decay_s, fade_s, rise_s, weight_s, lean_s, mixed_s, tokens_s, sums_v,
    load_sems, stream_sems, stage_sems,
    sent, got, join, send, recv,
    *ring_refs,
):
    total, width = x_v.shape
    hidden = w_out_v.shape[0]
    inner = w_down_v.shape[0]
    size = block * rows
    blocks = steps // block
    wide = UNIT
    parts = hidden // wide
    big = 512
    per = total // big
    feeds = inner // SPAN
    chain = Chain(count, -1, sent, got, join, send, recv)
    barrier, greeted = greet_chain(chain)
    grads, own_v = ring_refs[:2]
    if ringed:
        ring = Summing(plan, grads, *ring_refs[2:10], result)
        small = Doubling(own_v, *ring_refs[10:])
        greeted = greeted + greet_ring(ring)
    small_v = own_v.at[0]

    inner_columns = pl.ds(0, inner)
    rest_columns = pl.ds(inner, w_in.shape[1] - inner)
    loads = [
        pltpu.make_async_copy(source, target, load_sems.at[k])
        for k, (source, target) in enumerate((
            (middle_in, middle_v), (w_up, w_up_v), (cot_in, cot_v), (w_down, w_down_v), (state_in, state_v),
            (w_out, w_out_v), (x_in, x_v), (w_in.at[:, rest_columns], w_in_v), (w_in.at[:, inner_columns], w_up_v),
        ))
    ]
    loads[0].start()

    def at_block(b, n=size):
        return pl.ds(pl.multiple_of(b * n, n), n)

    due = {}
    clock = [0.0]

    def travel(unit, s):
        return 2.0 * (SLOW[s] - SLOW[s - 1]) if plan[unit][2] == WIDE else 1.0 * (FAST[s] - FAST[s - 1])

    def enter(unit):
        due[unit] = (0, clock[0])

    def tick(passed):
        clock[0] += passed
        for unit in sorted(due):
            s, when = due[unit]
            if s < STAGES and when <= clock[0] + 1e-6:
                if ringed:
                    ring.stage(s, unit)
                due[unit] = (s + 1, clock[0] + travel(unit, s + 1) if s + 1 < STAGES else 0.0)

    def rolling_tick(i, half):
        for s in reversed(range(STAGES)):
            behind = SLOW[s] + early - half
            if ringed and behind % 2 == 0 and behind // 2 < feeds * per // 2:
                pl.when(i >= behind // 2)(functools.partial(ring.stage, s, i - behind // 2))

    def beat(number, body, ticks, passed, *carry):
        each = number // ticks
        for k in range(ticks):
            carry = lax.fori_loop(each * k, each * k + each, lambda i, c: body(i, *c), carry)
            tick(passed / ticks)
        return carry

    def put_unit(unit):
        if not ringed:
            slot, column, length = plan[unit] if isinstance(unit, int) else (unit, 0, WIDE)
            copy = pltpu.make_async_copy(
                grads.at[slot, :, pl.ds(column, length)], result.at[unit, :, pl.ds(0, length)], load_sems.at[0]
            )
            copy.start()
            copy.wait()

    sums_v[...] = jnp.zeros_like(sums_v)
    small_v[...] = jnp.zeros_like(small_v)

    def put_small(row, value):
        for k in range(value.shape[1] // 128):
            small_v[pl.ds(row + k, 1)] = value[:, 128 * k : 128 * k + 128]

    def gather(slot, value, fresh):
        grads[slot] = jnp.where(fresh, 0.0, grads[slot]) + value

    loads[0].wait()
    for k in (1, 2, 3):
        loads[k].start()
    gains = gain_two[...]
    bias = down_bias[...]

    def norm_two(b, carry):
        at = at_block(b)
        value = middle_v[at]
        scale = lax.rsqrt(jnp.mean(value * value, axis=-1, keepdims=True) + EPS)
        normed = value * scale * gains
        low_v[at] = normed.astype(BF16)
        turned_v[:, at] = jnp.swapaxes(normed, 0, 1).astype(BF16)
        mixed_v[at] = value + bias
        second_v[at] = jnp.zeros_like(value)
        return carry

    lax.fori_loop(0, blocks, norm_two, 0)
    for k in (1, 2, 3):
        loads[k].wait()
    for k in (4, 5, 6, 7):
        loads[k].start()
    pl.semaphore_wait(barrier, greeted)

    def feed(f, tok):
        at = at_block(tok, big)
        lanes = pl.ds(pl.multiple_of(f * SPAN, SPAN), SPAN)
        cot = cot_v[at]
        pre = dot(low_v[at], w_up_v[:, lanes]) + up_bias[:, lanes]
        back_act = dot_nt(cot, w_down_v[lanes])
        square = pre * pre
        gate = 0.5 * jnp.tanh(pre * (GELU_A + GELU_B * square)) + 0.5
        act = pre * gate
        slope = gate + act * (1.0 - gate) * (2.0 * GELU_A + 6.0 * GELU_B * square)
        back_up = back_act * slope
        sums_v[0:1, lanes] = sums_v[0:1, lanes] + jnp.sum(back_up, axis=0, keepdims=True)
        act, back_up = act.astype(BF16), back_up.astype(BF16)
        mixed_v[at] = mixed_v[at] + dot(act, w_down_v[lanes])
        second_v[at] = second_v[at] + dot_nt(back_up, w_up_v[:, lanes])
        gather(2 * f, dot_tn(act, cot), tok == 0)
        gather(2 * f + 1, dot(turned_v[:, at], back_up), tok == 0)

    early = per - 1

    def feed_pair(i, carry):
        f, tok = lax.div(2 * i, per), lax.rem(2 * i, per)
        for half in range(2):
            feed(f, tok + half)
            if half == 1:
                @pl.when(tok + 2 == per)
                def _():
                    put_unit(2 * f)
                    put_unit(2 * f + 1)
            rolling_tick(i, half)
        return carry

    lax.fori_loop(0, feeds * per // 2, feed_pair, 0)
    clock[0] = 2.0 * (feeds * per - 1 - early)
    for u in range(2 * feeds):
        stages = [s for s in range(STAGES) if 4.0 * u + 2.0 * SLOW[s] > clock[0]]
        due[u] = (stages[0], 4.0 * u + 2.0 * SLOW[stages[0]])

    def decays(j):
        slot = j % 2
        return pltpu.make_async_copy(decay_in.at[:, pl.ds(j * wide, wide)], decay_s.at[slot], stream_sems.at[0, slot])

    decays(0).start()
    decays(1).start()

    streams = ((fade_s, fade_in), (rise_s, rise_in), (weight_s, weight_in), (lean_s, lean_in))
    depth = blocks // 2

    def streamed(k, half, i):
        if half == 0:
            return streams[k][0].at[i]
        each = inner // (len(streams) * wide)
        row, column = lax.div(i, each) * size, (lax.rem(i, each) * len(streams) + k) * wide
        return w_up_v.at[pl.ds(pl.multiple_of(row, size), size), pl.ds(pl.multiple_of(column, wide), wide)]

    def stream(j, half, i):
        b = blocks - 1 - half * depth - i
        return [
            pltpu.make_async_copy(source.at[at_block(b), pl.ds(j * wide, wide)], streamed(k, half, i), stream_sems.at[1 + k, half * depth + i])
            for k, (buffer, source) in enumerate(streams)
        ]

    for half in range(2):
        for i in range(depth):
            for copy in stream(0, half, i):
                copy.start()

    def stage_copy(buffer, target, b):
        slot = lax.rem(b, 2)
        return pltpu.make_async_copy(buffer.at[slot], target.at[:, pl.ds(pl.multiple_of(b * block, block), block), :], stage_sems.at[slot])

    def finish_two(b, norm_sum, cot_sum):
        at = at_block(b)

        @pl.when(b >= 2)
        def _():
            stage_copy(mixed_s, mixed_out, b - 2).wait()
        mixed = jnp.swapaxes(mixed_v[at].reshape(block, rows, width), 0, 1)
        mixed_s[lax.rem(b, 2)] = mixed.astype(BF16)
        stage_copy(mixed_s, mixed_out, b).start()
        value, grad, cot = middle_v[at], second_v[at], cot_v[at].astype(F32)
        scale = lax.rsqrt(jnp.mean(value * value, axis=-1, keepdims=True) + EPS)
        plain = value * scale
        norm_sum = norm_sum + jnp.sum((grad * plain).reshape(size // 8, 8, width), axis=0)
        cot_sum = cot_sum + jnp.sum(cot.reshape(size // 8, 8, width), axis=0)
        lean = grad * gains
        back = cot + scale * (lean - plain * jnp.mean(lean * plain, axis=-1, keepdims=True))
        second_v[at] = back
        low_v[at] = back.astype(BF16)
        return norm_sum, cot_sum

    zero = jnp.zeros((8, width), F32)
    norm_sum, cot_sum = beat(blocks, finish_two, 2, 2.4, zero, zero)
    for b in (blocks - 2, blocks - 1):
        stage_copy(mixed_s, mixed_out, b).wait()
    put_small(20, jnp.sum(norm_sum, axis=0, keepdims=True))
    put_small(24, sums_v[0:1])
    put_small(40, jnp.sum(cot_sum, axis=0, keepdims=True))

    loads[4].wait()
    loads[5].wait()

    def half_of(refs, j):
        return refs[j // 2], slice(UNIT * (j % 2), UNIT * (j % 2) + UNIT)

    def back_states():
        def one(tok, carry):
            at = at_block(tok, big)
            back = dot_nt(low_v[at], w_out_v[...])
            mixed_v[at] = back[:, :SPAN]
            middle_v[at] = back[:, SPAN:]
            return carry

        lax.fori_loop(0, per, one, 0)
        tick(2.0)

    def first_pass(j):
        flows, lanes = half_of((mixed_v, middle_v), j)
        decays(j).wait()

        def one(i, carry):
            product, flow = carry
            b = blocks - 1 - i
            for t in reversed(range(block)):
                there = pl.ds(pl.multiple_of(b * size + t * rows, rows), rows)
                decay = decay_s[j % 2, there]
                flow = decay * (flows[there, lanes] + flow)
                product = decay * product
            return product, flow

        product, flow = lax.fori_loop(0, blocks, one, (jnp.ones((rows, wide), F32), jnp.zeros((rows, wide), F32)))
        chain.start(j, product, flow)
        decays((j + 2) % parts).start()
        tick(0.6)

    def grad_out():
        for j in range(hidden // SPAN):
            def one(tok, carry):
                at = at_block(tok, big)
                gather(2 * feeds + j, dot_tn(state_v[at, pl.ds(j * SPAN, SPAN)], low_v[at]), tok == 0)
                return carry

            lax.fori_loop(0, per, one, 0)
            put_unit(2 * feeds + j)
            enter(2 * feeds + j)
            tick(2.0)

    gains_one = gain_one[...]

    def norm_one(b):
        at = at_block(b)
        value = x_v[at].astype(F32)
        scale = lax.rsqrt(jnp.mean(value * value, axis=-1, keepdims=True) + EPS)
        turned_v[:, at] = jnp.swapaxes(value * scale * gains_one, 0, 1).astype(BF16)
        return ()

    back_states()
    work = [functools.partial(first_pass, j) for j in range(parts)]
    work += [grad_out]

    def turn():
        loads[6].wait()
        beat(blocks, norm_one, 1, 1.6)

    work.append(turn)
    for step in range(max(len(work), parts + chain.rounds)):
        if step < len(work):
            work[step]()
        else:
            tick(1.0)
        for i in range(parts):
            if 0 <= step - 1 - i < chain.rounds:
                chain.advance(i, step - 1 - i)

    cand_refs = (low_v, cand_v)
    input_refs = (cot_v, w_down_v)

    def second_pass(j):
        flows, lanes = half_of((mixed_v, middle_v), j)
        to_input, to_cand = half_of(input_refs, j)[0], half_of(cand_refs, j)[0]
        decays(j).wait()

        def one(half, i, carry):
            flow, sum_f, sum_i = carry
            b = blocks - 1 - half * depth - i
            for copy in stream(j, half, i):
                copy.wait()
            fade, rise, weight, lean_part = (streamed(k, half, i) for k in range(len(streams)))
            for t in reversed(range(block)):
                here = pl.ds(t * rows, rows)
                there = pl.ds(pl.multiple_of(b * size + t * rows, rows), rows)
                reach = flows[there, lanes] + flow
                flow = decay_s[j % 2, there] * reach
                lean = reach * lean_part[here].astype(F32)
                grad_f = fade[here].astype(F32) * lean
                grad_i = -(rise[here].astype(F32) * lean)
                sum_f, sum_i = sum_f + grad_f, sum_i + grad_i
                state_v[there, wide * j : wide * j + wide] = grad_f.astype(BF16)
                to_input[there, lanes] = grad_i.astype(BF16)
                to_cand[there, lanes] = (weight[here].astype(F32) * reach).astype(BF16)
            if j + 1 < parts:
                for copy in stream(j + 1, half, i):
                    copy.start()
            return flow, sum_f, sum_i

        none = jnp.zeros((rows, wide), F32)
        carry = (join[j, 1], none, none)
        for half in range(2):
            carry = lax.fori_loop(0, depth, functools.partial(one, half), carry)
        unused, sum_f, sum_i = carry
        tick(1.2)
        if j + 2 < parts:
            decays(j + 2).start()
        put_small(4 + 2 * j, jnp.sum(sum_f, axis=0, keepdims=True))
        put_small(12 + 2 * j, jnp.sum(sum_i, axis=0, keepdims=True))

    def grad_in(j):
        unit = 2 * feeds + hidden // SPAN + 3 * j

        lanes = half_of(input_refs, j)[1]
        pieces = ((state_v, slice(wide * j, wide * j + wide)), (half_of(input_refs, j)[0], lanes), (half_of(cand_refs, j)[0], lanes))
        over = [u for u in range(2 * feeds + hidden // SPAN) if plan[u][0] in {plan[unit + k][0] for k in range(3)} and u not in settled]
        settled.update(over)
        assert all(due[u][0] > 7 for u in over)
        if ringed and over:
            ring.settle_sums(over)
        for k, (ref, columns) in enumerate(pieces):
            slot, column, length = plan[unit + k]
            grads[slot, :, pl.ds(column, length)] = dot(turned_v[...], ref[:, columns])
            put_unit(unit + k)
            enter(unit + k)
            tick(0.5)

    settled = set()
    for j in range(parts):
        second_pass(j)
        if j == parts - 1:
            loads[8].start()
        grad_in(j)

    for k in (7, 8):
        loads[k].wait()
    project_refs = [(state_v, slice(0, hidden), w_up_v, 0)]
    for k, refs in enumerate((input_refs, cand_refs)):
        for half in range(2):
            column = (k + 1) * hidden + half * SPAN
            wide_ref, column = (w_up_v, column) if column < inner else (w_in_v, column - inner)
            project_refs.append((refs[half], slice(None), wide_ref, column))

    def finish_one(tok, norm_sum):
        at = at_block(tok, big)
        grad_all = jnp.zeros((big, width), F32)
        for ref, columns, weight, column in project_refs:
            piece = ref[at, columns]
            grad_all = grad_all + dot_nt(piece, weight[:, column : column + piece.shape[1]])
        for k in range(big // size):
            b = tok * (big // size) + k

            @pl.when(b >= 2)
            def _():
                stage_copy(tokens_s, tokens_out, b - 2).wait()
            here = at_block(b)
            grad = grad_all[k * size : k * size + size]
            value = x_v[here].astype(F32)
            scale = lax.rsqrt(jnp.mean(value * value, axis=-1, keepdims=True) + EPS)
            plain = value * scale
            norm_sum = norm_sum + jnp.sum((grad * plain).reshape(size // 8, 8, width), axis=0)
            lean = grad * gains_one
            back = second_v[here] + scale * (lean - plain * jnp.mean(lean * plain, axis=-1, keepdims=True))
            tokens_s[lax.rem(b, 2)] = jnp.swapaxes(back.reshape(block, rows, width), 0, 1)
            stage_copy(tokens_s, tokens_out, b).start()
        return (norm_sum,)

    (norm_sum,) = beat(per, finish_one, 4, 9.0, jnp.zeros((8, width), F32))
    put_small(0, jnp.sum(norm_sum, axis=0, keepdims=True))
    if ringed:
        step = 0
        while step <= DOUBLINGS or any(due[unit][0] < STAGES for unit in due):
            tick(1.0)
            if step <= DOUBLINGS:
                small.step(step)
            step += 1
        ring.settle_sums([u for u in due if u not in settled])
        ring.settle_lines(list(due))
        copy = pltpu.make_async_copy(own_v.at[DOUBLINGS], small_out.at[0], load_sems.at[0])
    else:
        copy = pltpu.make_async_copy(small_v, small_out.at[0], load_sems.at[0])
    copy.start()
    copy.wait()
    for b in (blocks - 2, blocks - 1):
        stage_copy(tokens_s, tokens_out, b).wait()
    for j in range(parts):
        chain.finish(j)


def back(ringed, shape_in, x, cot, middle, state, decay, fade, rise, weight, lean, gain_one, gain_two, up_bias, down_bias, w_in, w_out, w_up, w_down, cid=2):
    rows, steps, width = shape_in
    total = rows * steps
    hidden = w_out.shape[0]
    inner = w_down.shape[0]
    count = lax.axis_size("seq")
    block = 16
    size = block * rows
    wide = UNIT
    parts = hidden // wide
    feeds = inner // SPAN
    whole = 2 * feeds + hidden // SPAN
    plan = [(u, 0, WIDE) for u in range(whole)]
    for k in range(3 * parts):
        plan.append(((whole + k // 2) % SLOTS, k % 2 * UNIT, UNIT))
    units = len(plan)
    anywhere = pl.BlockSpec(memory_space=pl.ANY)
    vmem = pl.BlockSpec(memory_space=pltpu.VMEM)
    shape = jax.ShapeDtypeStruct
    if ringed:
        first, *others = sum_scratch(units, whole, SLOTS)
        more = [first, pltpu.VMEM((DOUBLINGS + 1, SMALL_ROWS, 128), F32), *others]
        more += [pltpu.VMEM((DOUBLINGS, SMALL_ROWS, 128), F32)] + [pltpu.SemaphoreType.DMA((DOUBLINGS,))] * 2
    else:
        more = [pltpu.VMEM((SLOTS, SPAN, WIDE), F32), pltpu.VMEM((1, SMALL_ROWS, 128), F32)]
    return pl.pallas_call(
        functools.partial(back_kernel, ringed, count, rows, steps, plan, block),
        out_shape=(
            shape(shape_in, BF16), shape(shape_in, F32), shape((units, SPAN, WIDE), F32), shape((1, SMALL_ROWS, 128), F32),
        ),
        in_specs=[anywhere] * 9 + [vmem] * 4 + [anywhere] * 4,
        out_specs=(anywhere,) * 4,
        scratch_shapes=[
            pltpu.VMEM((total, width), F32), pltpu.VMEM((total, width), F32), pltpu.VMEM((total, width), F32),
            pltpu.VMEM((total, hidden), BF16), pltpu.VMEM((total, width), BF16), pltpu.VMEM((total, width), BF16), pltpu.VMEM((total, width), BF16),
            pltpu.VMEM((total, width), BF16), pltpu.VMEM((width, total), BF16),
            pltpu.VMEM((width, w_in.shape[1] - inner), BF16), pltpu.VMEM(w_out.shape, BF16), pltpu.VMEM(w_up.shape, BF16), pltpu.VMEM(w_down.shape, BF16),
            pltpu.VMEM((2, total, wide), F32), pltpu.VMEM((4, size, wide), BF16), pltpu.VMEM((4, size, wide), BF16),
            pltpu.VMEM((4, size, wide), BF16), pltpu.VMEM((4, size, wide), BF16),
            pltpu.VMEM((2, rows, block, width), BF16), pltpu.VMEM((2, rows, block, width), F32), pltpu.VMEM((8, inner), F32),
            pltpu.SemaphoreType.DMA((9,)), pltpu.SemaphoreType.DMA((5, 8)), pltpu.SemaphoreType.DMA((2,)),
            *chain_scratch(parts, count, rows, wide),
            *more,
        ],
        compiler_params=pltpu.CompilerParams(collective_id=cid, has_side_effects=True, vmem_limit_bytes=63 * 2**20 + 2**19),
        cost_estimate=pl.CostEstimate(flops=2 * total * width * (8 * hidden + 6 * inner), bytes_accessed=80 * 2**20, transcendentals=total * inner),
        name="back",
    )(x, cot, middle, state, decay, fade, rise, weight, lean, gain_one.reshape(1, -1), gain_two.reshape(1, -1), up_bias.reshape(1, -1), down_bias.reshape(1, -1), w_in, w_out, w_up, w_down)


def settle_kernel(places, mixed, tokens, units, small, *refs):
    outs, (mixed_v, tokens_v, units_v, reads, writes) = refs[:-5], refs[-5:]
    copies = []
    for k in range(mixed.shape[0] // 4):
        some = pl.ds(4 * k, 4)
        copies.append((tokens.at[some], tokens_v.at[some], outs[1].at[some]))
        copies.append((mixed.at[some], mixed_v.at[some], outs[0].at[some]))
    for u, length, array, row, column in places:
        lanes = pl.ds(0, length)
        copies.append((units.at[u, :, lanes], units_v.at[u, :, lanes], outs[2 + array].at[pl.ds(row, SPAN), pl.ds(column, length)]))
    moves = [
        (pltpu.make_async_copy(a, b, reads.at[k]), pltpu.make_async_copy(b, c, writes.at[k])) for k, (a, b, c) in enumerate(copies)
    ]
    for read, write in moves:
        read.start()
    row = 0
    for out in outs[6:]:
        out[...] = small[0, pl.ds(row, out.shape[0])]
        row += out.shape[0]
    for read, write in moves:
        read.wait()
        write.start()
    for read, write in moves:
        write.wait()


def settle(mixed, tokens, units, small, hidden, inner):
    width = tokens.shape[-1]
    parts = hidden // UNIT
    feeds = inner // SPAN
    places = []
    for f in range(feeds):
        places += [(2 * f, SPAN, 3, f * SPAN, 0), (2 * f + 1, SPAN, 2, 0, f * SPAN)]
    places += [(2 * feeds + j, SPAN, 1, j * SPAN, 0) for j in range(hidden // SPAN)]
    for j in range(parts):
        places += [(len(places) + k, UNIT, 0, 0, k * hidden + j * UNIT) for k in range(3)]
    anywhere = pl.BlockSpec(memory_space=pl.ANY)
    vmem = pl.BlockSpec(memory_space=pltpu.VMEM)
    shape = jax.ShapeDtypeStruct
    lengths = (width, hidden, hidden, width, inner, width)
    return pl.pallas_call(
        functools.partial(settle_kernel, places),
        out_shape=(
            shape(mixed.shape, mixed.dtype), shape(tokens.shape, F32), shape((width, 3 * hidden), F32), shape((hidden, width), F32),
            shape((width, inner), F32), shape((inner, width), F32), *(shape((n // 128, 128), F32) for n in lengths),
        ),
        in_specs=[anywhere] * 3 + [vmem],
        out_specs=(anywhere,) * 6 + (vmem,) * 6,
        scratch_shapes=[
            pltpu.VMEM(mixed.shape, mixed.dtype), pltpu.VMEM(tokens.shape, F32), pltpu.VMEM(units.shape, F32),
            pltpu.SemaphoreType.DMA((mixed.shape[0] // 2 + len(places),)), pltpu.SemaphoreType.DMA((mixed.shape[0] // 2 + len(places),)),
        ],
        compiler_params=pltpu.CompilerParams(vmem_limit_bytes=63 * 2**20),
        name="settle",
    )(mixed, tokens, units, small)


def on_device(tokens, cotangent, reset_pos, norm1_gain, w_in, forget_bias, input_bias, w_out, norm2_gain, w_up, up_bias, w_down, down_bias):
    ringed = lax.axis_size("seq") == 8 and lax.axis_size("rows") == 4
    hidden, inner = w_out.shape[0], w_down.shape[0]
    kept = front(tokens, cotangent, reset_pos, norm1_gain, w_in, forget_bias, input_bias, w_out)
    mixed, grad_tokens, units, small = back(
        ringed, tokens.shape, *kept, norm1_gain, norm2_gain, up_bias, down_bias, w_in, w_out, w_up, w_down
    )
    if not ringed:
        units, small = lax.psum((units, small), ("seq", "rows"))
    mixed, grad_tokens, grad_in, grad_out, grad_up, grad_down, *rest = settle(mixed, grad_tokens, units, small, hidden, inner)
    norm_one, forget, inputs, norm_two, up, down = (one.reshape(-1) for one in rest)
    return mixed, grad_tokens, norm_one, grad_in, forget, inputs, grad_out, norm_two, grad_up, up, grad_down, down


def solution(mesh):
    return jax.shard_map(
        on_device,
        mesh=mesh,
        in_specs=(
            P("rows", "seq", None),
            P("rows", "seq", None),
            P("rows", None),
            P(),
            P(),
            P(),
            P(),
            P(),
            P(),
            P(),
            P(),
            P(),
            P(),
        ),
        out_specs=(
            P("rows", "seq", None),
            P("rows", "seq", None),
            P(),
            P(),
            P(),
            P(),
            P(),
            P(),
            P(),
            P(),
            P(),
            P(),
        ),
        check_vma=False,
    )
```

```python
import functools
import math
import jax
import jax.numpy as jnp
from jax import lax
from jax.experimental import pallas as pl
from jax.experimental.pallas import tpu as pltpu
from jax.sharding import PartitionSpec as P

MESH = pl.DeviceIdType.MESH
EPS = 1e-6
F32 = jnp.float32
BF16 = jnp.bfloat16
STAGES = 13
KINDS = 10
SPAN = 512
UNIT = 256
WIDE = 512
SLOTS = 10
SIDE = 2
SMALL_ROWS = 48
DOUBLINGS = 5
SLOW = (0, 1, 3, 6, 8, 10, 11, 12, 14, 16, 19, 21, 22)
FAST = (0, 1, 5, 10, 14, 17, 19, 22, 24, 28, 33, 37, 38)


def place():
    seq = lax.axis_index("seq")
    rows = lax.axis_index("rows")
    return lax.div(rows, 2), lax.rem(seq, 2), lax.div(seq, 2), lax.rem(rows, 2)


def spot(x, y, z, core):
    return (z * 2 + y, x * 2 + core)


def dot(left, right):
    return jnp.dot(left, right, preferred_element_type=F32)


def dot_nt(left, right):
    return lax.dot_general(left, right, (((1,), (1,)), ((), ())), preferred_element_type=F32)


def dot_tn(left, right):
    return lax.dot_general(left, right, (((0,), (0,)), ((), ())), preferred_element_type=F32)


class Chain:
    def __init__(self, count, sign, sent, got, join, send, recv):
        self.count, self.sign = count, sign
        self.sent, self.got, self.join = sent, got, join
        self.send, self.recv = send, recv
        self.rounds = max(1, math.ceil(math.log2(count)))
        seq = lax.axis_index("seq")
        self.seq = seq
        self.place = seq if sign > 0 else count - 1 - seq

    def partners(self):
        for r in range(self.rounds):
            far = 2**r
            yield self.seq + self.sign * far, self.place + far < self.count
            yield self.seq - self.sign * far, self.place >= far

    def copy(self, part, r, other):
        return pltpu.make_async_remote_copy(
            src_ref=self.sent.at[part, r], dst_ref=self.got.at[part, r],
            send_sem=self.send.at[part, r], recv_sem=self.recv.at[part, r],
            device_id=(other, lax.axis_index("rows")), device_id_type=MESH,
        )

    def push(self, part, r):
        @pl.when(self.place + 2**r < self.count)
        def _():
            self.copy(part, r, self.seq + self.sign * 2**r).start()

    def start(self, part, product, end):
        self.sent[part, 0, 0] = product
        self.sent[part, 0, 1] = end
        self.join[part, 0] = jnp.ones_like(product)
        self.join[part, 1] = jnp.zeros_like(end)
        self.push(part, 0)

    def advance(self, part, r):
        last = r == self.rounds - 1

        @pl.when(self.place >= 2**r)
        def _():
            self.copy(part, r, self.seq - self.sign * 2**r).wait_recv()
            product, end = self.got[part, r, 0], self.got[part, r, 1]
            own = self.join[part, 0]
            self.join[part, 1] = self.join[part, 1] + own * end
            if not last:
                self.join[part, 0] = own * product
                here = self.sent[part, r, 0]
                self.sent[part, r + 1, 0] = here * product
                self.sent[part, r + 1, 1] = self.sent[part, r, 1] + here * end

        if not last:
            @pl.when(self.place < 2**r)
            def _():
                self.sent[part, r + 1] = self.sent[part, r]
            self.push(part, r + 1)

    def finish(self, part):
        for r in range(self.rounds):
            @pl.when(self.place + 2**r < self.count)
            def _():
                self.copy(part, r, self.seq + self.sign * 2**r).wait_send()


def greet_chain(chain):
    barrier = pltpu.get_barrier_semaphore()
    rows = lax.axis_index("rows")
    total = 0
    for other, there in chain.partners():
        @pl.when(there)
        def _():
            pl.semaphore_signal(barrier, inc=1, device_id=(other, rows), device_id_type=MESH)
        total = total + jnp.where(there, 1, 0)
    return barrier, total


def chain_scratch(parts, count, rows, width):
    rounds = max(1, math.ceil(math.log2(count)))
    return [
        pltpu.VMEM((parts, rounds, 2, rows, width), F32),
        pltpu.VMEM((parts, rounds, 2, rows, width), F32),
        pltpu.VMEM((parts, 2, rows, width), F32),
        pltpu.SemaphoreType.DMA((parts, rounds)),
        pltpu.SemaphoreType.DMA((parts, rounds)),
    ]


def front_kernel(
    count, rows, steps, chunk, block,
    tokens, cotangent, reset_in, gain, w_in, forget_bias, input_bias, w_out,
    x_out, cot_out, middle_out, state_out, decay_out, fade_out, rise_out, weight_out, lean_out,
    reset, tok_v, cot_v, x_v, normed_v, w_v, w_out_v, keep_v, decay_v, update_v, cand_v, fade_v, rise_v, weight_v, lean_v, state_v, middle_v,
    sent, got, join, send, recv, sems, out_sems,
):
    total, width = x_v.shape
    hidden = w_out_v.shape[0]
    parts = hidden // chunk
    size = block * rows
    blocks = steps // block
    side = math.gcd(blocks, SIDE)
    chain = Chain(count, 1, sent, got, join, send, recv)
    barrier, greeted = greet_chain(chain)
    loads = [pltpu.make_async_copy(tokens, tok_v, sems.at[0])]
    for j in range(parts):
        for k in range(3):
            loads.append(pltpu.make_async_copy(w_in.at[:, pl.ds(k * hidden + j * chunk, chunk)], w_v.at[j, :, pl.ds(k * chunk, chunk)], sems.at[1 + 3 * j + k]))
    loads.append(pltpu.make_async_copy(cotangent, cot_v, sems.at[1 + 3 * parts]))
    loads.append(pltpu.make_async_copy(w_out, w_out_v, sems.at[2 + 3 * parts]))
    marks_in = pltpu.make_async_copy(reset_in, reset, sems.at[3 + 3 * parts])
    marks_in.start()
    for load in loads:
        load.start()
    marks_in.wait()
    loads[0].wait()

    first = lax.axis_index("seq") * steps
    marks = [jnp.broadcast_to(reset[:, k : k + 1], (rows, 128)) for k in range(reset.shape[1])]

    def mark(t, carry):
        hit = marks[0] == first + t
        for one in marks[1:]:
            hit = hit | (one == first + t)
        keep_v[pl.ds(pl.multiple_of(t * rows, rows), rows)] = jnp.where(hit, 0.0, 1.0)
        return carry

    lax.fori_loop(0, steps, mark, 0, unroll=4)
    gains = gain[...]

    def norm(b, carry):
        at = pl.ds(pl.multiple_of(b * size, size), size)
        x = tok_v[:, pl.ds(pl.multiple_of(b * block, block), block), :].astype(F32)
        x = jnp.swapaxes(x, 0, 1).reshape(size, width)
        x_v[at] = x.astype(BF16)
        scale = lax.rsqrt(jnp.mean(x * x, axis=-1, keepdims=True) + EPS)
        normed_v[at] = (x * scale * gains).astype(BF16)
        return carry

    lax.fori_loop(0, blocks, norm, 0)
    outs = [pltpu.make_async_copy(x_v, x_out, out_sems.at[0])]
    outs[0].start()

    def gates(j):
        lanes = pl.ds(j * chunk, chunk)
        shift_f, shift_i = -forget_bias[:, lanes], -input_bias[:, lanes]

        def some(project, at, product, end):
            neg_f = shift_f - project[:, :chunk]
            neg_i = shift_i - project[:, chunk : 2 * chunk]
            cand = project[:, 2 * chunk :]
            lower = jnp.maximum(jnp.minimum(neg_f, neg_i) - 20.0, 0.0)
            exp_f = jnp.exp(jnp.minimum(neg_f - lower, 80.0))
            exp_i = jnp.exp(jnp.minimum(neg_i - lower, 80.0))
            one_f, one_i = 1.0 + exp_f, 1.0 + exp_i
            share = 1.0 / (one_f + one_i)
            decay, weight = one_i * share, one_f * share
            fade_v[j % 2, at] = (decay * (exp_f * share)).astype(BF16)
            rise_v[j % 2, at] = (weight * (exp_i * share)).astype(BF16)
            weight_v[j % 2, at] = weight.astype(BF16)
            cand_v[at, lanes] = cand
            update = weight * cand
            update_v[at, lanes] = update
            decay = decay * jnp.concatenate([keep_v[at]] * (chunk // 128), axis=1)
            decay_v[at, lanes] = decay
            for t in range(block):
                here = decay[t * rows : (t + 1) * rows]
                end = here * end + update[t * rows : (t + 1) * rows]
                product = here * product
            return product, end

        def one(b, carry):
            places = [pl.ds(pl.multiple_of((b * side + k) * size, size), size) for k in range(side)]
            for at in places:
                carry = some(dot(normed_v[at], w_v[j]), at, *carry)
            return carry

        start = (jnp.ones((rows, chunk), F32), jnp.zeros((rows, chunk), F32))
        return lax.fori_loop(0, blocks // side, one, start)

    def scan(j):
        lanes = pl.ds(j * chunk, chunk)

        def one(b, state):
            for t in range(block):
                here = pl.ds(pl.multiple_of(b * size + t * rows, rows), rows)
                keep = jnp.concatenate([keep_v[here]] * (chunk // 128), axis=1)
                lean_v[j % 2, here] = (keep * state - cand_v[here, lanes]).astype(BF16)
                state = decay_v[here, lanes] * state + update_v[here, lanes]
                state_v[here, lanes] = state.astype(BF16)
            return state

        lax.fori_loop(0, blocks, one, join[j, 1])

    def project_out(b, carry):
        at = pl.ds(pl.multiple_of(b * 2 * size, 2 * size), 2 * size)
        middle_v[at] = x_v[at].astype(F32) + dot(state_v[at], w_out_v[...])
        copy = pltpu.make_async_copy(middle_v.at[at], middle_out.at[at], out_sems.at[2 + 6 * parts])
        copy.start()
        return carry

    def put(source, target, slot, wait=False):
        copy = pltpu.make_async_copy(source, target, out_sems.at[slot])
        if wait:
            copy.wait()
        else:
            copy.start()

    def gate_outs(j, wait=False):
        lanes = pl.ds(j * chunk, chunk)
        for k, (a, b) in enumerate(((fade_v, fade_out), (rise_v, rise_out), (weight_v, weight_out))):
            put(a.at[j % 2], b.at[:, lanes], 1 + 3 * j + k, wait)
        put(decay_v.at[:, lanes], decay_out.at[:, lanes], 1 + 3 * parts + j, wait)

    def scan_outs(j, wait=False):
        lanes = pl.ds(j * chunk, chunk)
        put(lean_v.at[j % 2], lean_out.at[:, lanes], 1 + 4 * parts + 2 * j, wait)
        put(state_v.at[:, lanes], state_out.at[:, lanes], 2 + 4 * parts + 2 * j, wait)

    ready = 0
    for j in range(parts):
        for k in range(3):
            loads[1 + 3 * j + k].wait()
        if j >= 2:
            gate_outs(j - 2, True)
        product, end = gates(j)
        gate_outs(j)
        if j == 0:
            pl.semaphore_wait(barrier, greeted)
        chain.start(j, product, end)
        for i in range(j - 1, -1, -1):
            if j - 1 - i < chain.rounds:
                chain.advance(i, j - 1 - i)
    for k in range(2):
        loads[1 + 3 * parts + k].wait()

    def turn(b, carry):
        at = pl.ds(pl.multiple_of(b * size, size), size)
        c = cot_v[:, pl.ds(pl.multiple_of(b * block, block), block), :].astype(F32)
        normed_v[at] = jnp.swapaxes(c, 0, 1).reshape(size, width).astype(BF16)
        return carry

    lax.fori_loop(0, blocks, turn, 0)
    put(normed_v, cot_out, 1 + 6 * parts)

    step = parts - 1
    while ready < parts:
        for i in range(parts - 1, -1, -1):
            if 0 <= step - 1 - i < chain.rounds and step >= parts:
                chain.advance(i, step - 1 - i)
        while ready < parts and ready + chain.rounds <= step:
            if ready >= 2:
                scan_outs(ready - 2, True)
            scan(ready)
            scan_outs(ready)
            ready += 1
        step += 1
    lax.fori_loop(0, blocks // 2, project_out, 0)
    for j in range(parts):
        if j >= parts - 2:
            gate_outs(j, True)
            scan_outs(j, True)
        chain.finish(j)
    outs[0].wait()
    put(normed_v, cot_out, 1 + 6 * parts, True)
    put(middle_v, middle_out, 2 + 6 * parts, True)


def front(tokens, cotangent, reset, gain, w_in, forget_bias, input_bias, w_out, cid=1):
    rows, steps, width = tokens.shape
    hidden = w_out.shape[0]
    total = rows * steps
    count = lax.axis_size("seq")
    chunk, block = 256, 16
    parts = hidden // chunk
    anywhere = pl.BlockSpec(memory_space=pl.ANY)
    vmem = pl.BlockSpec(memory_space=pltpu.VMEM)
    shape = jax.ShapeDtypeStruct
    return pl.pallas_call(
        functools.partial(front_kernel, count, rows, steps, chunk, block),
        out_shape=(
            shape((total, width), BF16), shape((total, width), BF16), shape((total, width), F32),
            shape((total, hidden), BF16), shape((total, hidden), F32), shape((total, hidden), BF16),
            shape((total, hidden), BF16), shape((total, hidden), BF16), shape((total, hidden), BF16),
        ),
        in_specs=[anywhere, anywhere, anywhere, vmem, anywhere, vmem, vmem, anywhere],
        out_specs=(anywhere,) * 9,
        scratch_shapes=[
            pltpu.VMEM(reset.shape, jnp.int32), pltpu.VMEM(tokens.shape, BF16), pltpu.VMEM(tokens.shape, BF16), pltpu.VMEM((total, width), BF16), pltpu.VMEM((total, width), BF16),
            pltpu.VMEM((parts, width, 3 * chunk), BF16), pltpu.VMEM(w_out.shape, BF16), pltpu.VMEM((total, 128), F32),
            pltpu.VMEM((total, hidden), F32), pltpu.VMEM((total, hidden), F32), pltpu.VMEM((total, hidden), F32),
            pltpu.VMEM((2, total, chunk), BF16), pltpu.VMEM((2, total, chunk), BF16), pltpu.VMEM((2, total, chunk), BF16),
            pltpu.VMEM((2, total, chunk), BF16), pltpu.VMEM((total, hidden), BF16), pltpu.VMEM((total, width), F32),
            *chain_scratch(parts, count, rows, chunk),
            pltpu.SemaphoreType.DMA((4 + 3 * parts,)), pltpu.SemaphoreType.DMA((3 + 6 * parts,)),
        ],
        compiler_params=pltpu.CompilerParams(collective_id=cid, has_side_effects=True, vmem_limit_bytes=62 * 2**20),
        cost_estimate=pl.CostEstimate(flops=2 * total * width * 4 * hidden, bytes_accessed=40 * 2**20, transcendentals=3 * total * hidden),
        name="front",
    )(tokens, cotangent, reset, gain.reshape(1, -1), w_in, forget_bias.reshape(1, -1), input_bias.reshape(1, -1), w_out)


class Summing:
    def __init__(self, plan, grads, half_in, part_in, lines_in, last_in, send, recv, local, free, result):
        self.plan, self.grads = plan, grads
        self.whole = sum(width == WIDE for slot, column, width in plan)
        self.half_in, self.part_in, self.lines_in, self.last_in = half_in, part_in, lines_in, last_in
        self.result, self.send, self.recv, self.local, self.free = result, send, recv, local, free
        x, y, z, core = place()
        self.z = z
        first = core == 0
        self.sibling = spot(x, y, z, 1 - core)
        along_x, along_y = spot(1 - x, y, z, core), spot(x, 1 - y, z, core)
        self.near = tuple(jnp.where(first, a, b) for a, b in zip(along_x, along_y))
        self.far = tuple(jnp.where(first, b, a) for a, b in zip(along_x, along_y))
        self.above = spot(x, y, z + 1, core)
        self.below = spot(x, y, z - 1, core)
        near_bit = jnp.where(first, x, y)
        far_bit = jnp.where(first, y, x)
        self.n_half, self.n_part, self.n_line, self.n_tip = SPAN // 2, SPAN // 4, SPAN // 16, SPAN // 32
        self.half = core * self.n_half
        self.other_half = (1 - core) * self.n_half
        self.part = self.half + near_bit * self.n_part
        self.other_part = self.half + (1 - near_bit) * self.n_part
        self.tip = self.part + self.n_line * z + self.n_tip * far_bit
        self.other_tip = self.part + self.n_line * z + self.n_tip * (1 - far_bit)

    def copy(self, kind, unit, source, target, device):
        return pltpu.make_async_remote_copy(
            src_ref=source, dst_ref=target, send_sem=self.send.at[kind, unit], recv_sem=self.recv.at[kind, unit],
            device_id=device, device_id_type=MESH,
        )

    def slot_of(self, u):
        return self.plan[u] if isinstance(u, int) else (u, 0, WIDE)

    def rows(self, u, start, count):
        slot, column, width = self.slot_of(u)
        return self.grads.at[slot, pl.ds(pl.multiple_of(start, 8), count), pl.ds(column, width)]

    def done(self, u, start, count):
        return self.result.at[u, pl.ds(pl.multiple_of(start, 8), count), pl.ds(0, self.slot_of(u)[2])]

    def land(self, ref, wide, u, start, count):
        if self.slot_of(u)[2] == WIDE:
            return ref.at[lax.rem(u, wide), pl.ds(start, count)]
        turn = (u - self.whole) % (2 * (ref.shape[0] - wide))
        return ref.at[wide + turn // 2, pl.ds(start, count), pl.ds(turn % 2 * UNIT, UNIT)]

    def turns(self, kind, u):
        ref, wide = ((self.half_in, 2), (self.part_in, 3), (self.lines_in, 3), (self.lines_in, 3))[kind]
        if self.slot_of(u)[2] == WIDE:
            return wide, 0, self.whole
        return 2 * (ref.shape[0] - wide), self.whole, len(self.plan)

    def claim(self, kind, u):
        apart, first, last = self.turns(kind, u)
        if isinstance(u, int):
            if u - apart >= first:
                pl.semaphore_wait(self.free.at[kind, u - apart], 1)
        else:
            @pl.when(u >= apart)
            def _():
                pl.semaphore_wait(self.free.at[kind, u - apart], 1)

    def release(self, kind, u, sender):
        apart, first, last = self.turns(kind, u)

        def signal():
            pl.semaphore_signal(self.free.at[kind, u], inc=1, device_id=sender, device_id_type=MESH)

        if isinstance(u, int):
            if u + apart < last:
                signal()
        else:
            pl.when(u + apart < last)(signal)

    def land_half(self, u):
        return self.land(self.half_in, 2, u, 0, self.n_half)

    def land_part(self, u):
        return self.land(self.part_in, 3, u, 0, self.n_part)

    def land_up(self, u, z):
        return self.land(self.lines_in, 3, u, 0, self.n_line * (4 - z))

    def land_down(self, u, z):
        return self.land(self.lines_in, 3, u, self.n_line * (4 - z) if z > 0 else 0, self.n_line * (z + 1))

    def land_last(self, u):
        return self.land(self.last_in, self.whole, u, 0, self.n_tip)

    def c_half(self, u):
        return self.copy(0, u, self.rows(u, self.other_half, self.n_half), self.land_half(u), self.sibling)

    def c_part(self, u):
        return self.copy(1, u, self.rows(u, self.other_part, self.n_part), self.land_part(u), self.near)

    def c_up(self, u, z):
        low, rest = self.n_line * (z + 1), self.n_line * (3 - z)
        return self.copy(2, u, self.rows(u, self.part + low, rest), self.land_up(u, z + 1), self.above)

    def c_down(self, u, z):
        rest = self.n_line * z
        return self.copy(3, u, self.rows(u, self.part, rest), self.land_down(u, z - 1), self.below)

    def c_last(self, u):
        return self.copy(4, u, self.rows(u, self.other_tip, self.n_tip), self.land_last(u), self.far)

    def c_own(self, u):
        return pltpu.make_async_copy(self.rows(u, self.tip, self.n_tip), self.done(u, self.tip, self.n_tip), self.local.at[u])

    def c_far(self, u, start):
        return self.copy(5, u, self.rows(u, start, self.n_tip), self.done(u, start, self.n_tip), self.far)

    def c_rise(self, u, z):
        piece = self.done(u, self.part, self.n_line * (z + 1))
        return self.copy(6, u, piece, piece, self.above)

    def c_fall(self, u, z):
        piece = self.done(u, self.part + self.n_line * z, self.n_line * (4 - z))
        return self.copy(7, u, piece, piece, self.below)

    def c_near(self, u, start):
        piece = self.done(u, start, self.n_part)
        return self.copy(8, u, piece, piece, self.near)

    def c_sibling(self, u, start):
        piece = self.done(u, start, self.n_half)
        return self.copy(9, u, piece, piece, self.sibling)

    def add(self, u, start, count, ref):
        slot, column, width = self.slot_of(u)
        step = min(count, 128)
        lanes = pl.ds(column, width)

        def one(i, carry):
            here = pl.ds(pl.multiple_of(start + i * step, 8), step)
            there = pl.ds(pl.multiple_of(i * step, 8), step)
            self.grads[slot, here, lanes] = self.grads[slot, here, lanes] + ref[there]
            return carry

        if count == step:
            one(0, 0)
        else:
            lax.fori_loop(0, count // step, one, 0)

    def settle_sums(self, units):
        def sent(k):
            for u in units:
                if k < 3:
                    self.c_up(u, k).wait_send()
                if k > 0:
                    self.c_down(u, k).wait_send()

        self.at_each(sent)

    def settle_lines(self, units):
        def sent(k):
            for u in units:
                if k < 3:
                    self.c_rise(u, k).wait_send()
                if k > 0:
                    self.c_fall(u, k).wait_send()

        self.at_each(sent)

    def at_each(self, action):
        for k in range(4):
            pl.when(self.z == k)(functools.partial(action, k))

    def stage(self, s, u):
        z = self.z
        if s == 0:
            self.claim(0, u)
            self.c_half(u).start()
        elif s == 1:
            self.c_half(u).wait()
            self.add(u, self.half, self.n_half, self.land_half(u))
            self.release(0, u, self.sibling)
            self.claim(1, u)
            self.c_part(u).start()
        elif s == 2:
            self.c_part(u).wait()
            self.add(u, self.part, self.n_part, self.land_part(u))
            self.release(1, u, self.near)
        if 2 <= s <= 5:
            up, down = s - 2, 5 - s

            @pl.when(z == up)
            def _():
                if up > 0:
                    self.c_up(u, up - 1).wait_recv()
                    low, rest = self.n_line * up, self.n_line * (4 - up)
                    self.add(u, self.part + low, rest, self.land_up(u, up))
                    self.release(2, u, self.below)
                if up < 3:
                    self.claim(2, u)
                    self.c_up(u, up).start()

            @pl.when(z == down)
            def _():
                if down < 3:
                    self.c_down(u, down + 1).wait_recv()
                    rest = self.n_line * (down + 1)
                    self.add(u, self.part, rest, self.land_down(u, down))
                    self.release(3, u, self.above)
                if down > 0:
                    self.claim(3, u)
                    self.c_down(u, down).start()
        if s == 5:
            self.c_last(u).start()
        elif s == 6:
            self.c_last(u).wait()
            self.add(u, self.tip, self.n_tip, self.land_last(u))
            self.c_far(u, self.tip).start()
            self.c_own(u).start()
        elif s == 7:
            self.c_far(u, self.tip).wait_send()
            self.c_far(u, self.other_tip).wait_recv()
            self.c_own(u).wait()
        if 7 <= s <= 10:
            up, down = s - 7, 10 - s

            @pl.when(z == up)
            def _():
                if up > 0:
                    self.c_rise(u, up - 1).wait_recv()
                if up < 3:
                    self.c_rise(u, up).start()

            @pl.when(z == down)
            def _():
                if down < 3:
                    self.c_fall(u, down + 1).wait_recv()
                if down > 0:
                    self.c_fall(u, down).start()
        if s == 10:
            self.c_near(u, self.part).start()
        elif s == 11:
            self.c_near(u, self.part).wait_send()
            self.c_near(u, self.other_part).wait_recv()
            self.c_sibling(u, self.half).start()
        elif s == 12:
            self.c_sibling(u, self.half).wait_send()
            self.c_sibling(u, self.other_half).wait_recv()


def sum_scratch(units, whole, slots):
    pairs = (units - whole + 1) // 2
    return [
        pltpu.VMEM((slots, SPAN, WIDE), F32),
        pltpu.VMEM((2 + min(pairs, 2), SPAN // 2, WIDE), F32),
        pltpu.VMEM((3 + min(pairs, 4), SPAN // 4, WIDE), F32),
        pltpu.VMEM((3 + pairs, 5 * SPAN // 16, WIDE), F32),
        pltpu.VMEM((whole + pairs, SPAN // 32, WIDE), F32),
        pltpu.SemaphoreType.DMA((KINDS, units)),
        pltpu.SemaphoreType.DMA((KINDS, units)),
        pltpu.SemaphoreType.DMA((units,)),
        pltpu.SemaphoreType.REGULAR((4, units)),
    ]


class Doubling:
    def __init__(self, own, got, send, recv):
        self.own, self.got, self.send, self.recv = own, got, send, recv
        x, y, z, core = place()
        self.partners = (
            spot(x, y, z, 1 - core), spot(1 - x, y, z, core), spot(x, 1 - y, z, core),
            spot(x, y, z + 1 - 2 * lax.rem(z, 2), core), spot(x, y, z + 2 - 4 * lax.div(z, 2), core),
        )

    def copy(self, k):
        return pltpu.make_async_remote_copy(
            src_ref=self.own.at[k], dst_ref=self.got.at[k], send_sem=self.send.at[k], recv_sem=self.recv.at[k],
            device_id=self.partners[k], device_id_type=MESH,
        )

    def step(self, k):
        if k > 0:
            self.copy(k - 1).wait()
            self.own[k] = self.own[k - 1] + self.got[k - 1]
        if k < DOUBLINGS:
            self.copy(k).start()


def greet_ring(ring):
    barrier = pltpu.get_barrier_semaphore()
    for there in (ring.sibling, ring.near, ring.far):
        pl.semaphore_signal(barrier, inc=1, device_id=there, device_id_type=MESH)

    @pl.when(ring.z > 0)
    def _():
        pl.semaphore_signal(barrier, inc=1, device_id=ring.below, device_id_type=MESH)

    @pl.when(ring.z < 3)
    def _():
        pl.semaphore_signal(barrier, inc=1, device_id=ring.above, device_id_type=MESH)

    return 3 + jnp.where(ring.z > 0, 1, 0) + jnp.where(ring.z < 3, 1, 0)


GELU_A = math.sqrt(2.0 / math.pi)
GELU_B = GELU_A * 0.044715


def back_kernel(
    ringed, count, rows, steps, plan, block,
    x_in, cot_in, middle_in, state_in, decay_in, fade_in, rise_in, weight_in, lean_in,
    gain_one, gain_two, up_bias, down_bias, w_in, w_out, w_up, w_down,
    mixed_out, tokens_out, result, small_out,
    middle_v, second_v, mixed_v, state_v, cot_v, x_v, low_v, cand_v, turned_v, w_in_v, w_out_v, w_up_v, w_down_v,
    decay_s, fade_s, rise_s, weight_s, lean_s, mixed_s, tokens_s, sums_v,
    load_sems, stream_sems, stage_sems,
    sent, got, join, send, recv,
    *ring_refs,
):
    total, width = x_v.shape
    hidden = w_out_v.shape[0]
    inner = w_down_v.shape[0]
    size = block * rows
    blocks = steps // block
    wide = UNIT
    parts = hidden // wide
    big = 512
    per = total // big
    feeds = inner // SPAN
    chain = Chain(count, -1, sent, got, join, send, recv)
    barrier, greeted = greet_chain(chain)
    grads, own_v = ring_refs[:2]
    if ringed:
        ring = Summing(plan, grads, *ring_refs[2:10], result)
        small = Doubling(own_v, *ring_refs[10:])
        greeted = greeted + greet_ring(ring)
    small_v = own_v.at[0]

    inner_columns = pl.ds(0, inner)
    rest_columns = pl.ds(inner, w_in.shape[1] - inner)
    loads = [
        pltpu.make_async_copy(source, target, load_sems.at[k])
        for k, (source, target) in enumerate((
            (middle_in, middle_v), (w_up, w_up_v), (cot_in, cot_v), (w_down, w_down_v), (state_in, state_v),
            (w_out, w_out_v), (x_in, x_v), (w_in.at[:, rest_columns], w_in_v), (w_in.at[:, inner_columns], w_up_v),
        ))
    ]
    loads[0].start()

    def at_block(b, n=size):
        return pl.ds(pl.multiple_of(b * n, n), n)

    due = {}
    clock = [0.0]

    def travel(unit, s):
        return 2.0 * (SLOW[s] - SLOW[s - 1]) if plan[unit][2] == WIDE else 1.0 * (FAST[s] - FAST[s - 1])

    def enter(unit):
        due[unit] = (0, clock[0])

    def tick(passed):
        clock[0] += passed
        for unit in sorted(due):
            s, when = due[unit]
            if s < STAGES and when <= clock[0] + 1e-6:
                if ringed:
                    ring.stage(s, unit)
                due[unit] = (s + 1, clock[0] + travel(unit, s + 1) if s + 1 < STAGES else 0.0)

    def rolling_tick(i, half):
        for s in reversed(range(STAGES)):
            behind = SLOW[s] + early - half
            if ringed and behind % 2 == 0 and behind // 2 < feeds * per // 2:
                pl.when(i >= behind // 2)(functools.partial(ring.stage, s, i - behind // 2))

    def beat(number, body, ticks, passed, *carry):
        each = number // ticks
        for k in range(ticks):
            carry = lax.fori_loop(each * k, each * k + each, lambda i, c: body(i, *c), carry)
            tick(passed / ticks)
        return carry

    def put_unit(unit):
        if not ringed:
            slot, column, length = plan[unit] if isinstance(unit, int) else (unit, 0, WIDE)
            copy = pltpu.make_async_copy(
                grads.at[slot, :, pl.ds(column, length)], result.at[unit, :, pl.ds(0, length)], load_sems.at[0]
            )
            copy.start()
            copy.wait()

    sums_v[...] = jnp.zeros_like(sums_v)
    small_v[...] = jnp.zeros_like(small_v)

    def put_small(row, value):
        for k in range(value.shape[1] // 128):
            small_v[pl.ds(row + k, 1)] = value[:, 128 * k : 128 * k + 128]

    def gather(slot, value, fresh):
        grads[slot] = jnp.where(fresh, 0.0, grads[slot]) + value

    loads[0].wait()
    for k in (1, 2, 3):
        loads[k].start()
    gains = gain_two[...]
    bias = down_bias[...]

    def norm_two(b, carry):
        at = at_block(b)
        value = middle_v[at]
        scale = lax.rsqrt(jnp.mean(value * value, axis=-1, keepdims=True) + EPS)
        normed = value * scale * gains
        low_v[at] = normed.astype(BF16)
        turned_v[:, at] = jnp.swapaxes(normed, 0, 1).astype(BF16)
        mixed_v[at] = value + bias
        second_v[at] = jnp.zeros_like(value)
        return carry

    lax.fori_loop(0, blocks, norm_two, 0)
    for k in (1, 2, 3):
        loads[k].wait()
    for k in (4, 5, 6, 7):
        loads[k].start()
    pl.semaphore_wait(barrier, greeted)

    def feed(f, tok):
        at = at_block(tok, big)
        lanes = pl.ds(pl.multiple_of(f * SPAN, SPAN), SPAN)
        cot = cot_v[at]
        pre = dot(low_v[at], w_up_v[:, lanes]) + up_bias[:, lanes]
        back_act = dot_nt(cot, w_down_v[lanes])
        square = pre * pre
        gate = 0.5 * jnp.tanh(pre * (GELU_A + GELU_B * square)) + 0.5
        act = pre * gate
        slope = gate + act * (1.0 - gate) * (2.0 * GELU_A + 6.0 * GELU_B * square)
        back_up = back_act * slope
        sums_v[0:1, lanes] = sums_v[0:1, lanes] + jnp.sum(back_up, axis=0, keepdims=True)
        act, back_up = act.astype(BF16), back_up.astype(BF16)
        mixed_v[at] = mixed_v[at] + dot(act, w_down_v[lanes])
        second_v[at] = second_v[at] + dot_nt(back_up, w_up_v[:, lanes])
        gather(2 * f, dot_tn(act, cot), tok == 0)
        gather(2 * f + 1, dot(turned_v[:, at], back_up), tok == 0)

    early = per - 1

    def feed_pair(i, carry):
        f, tok = lax.div(2 * i, per), lax.rem(2 * i, per)
        for half in range(2):
            feed(f, tok + half)
            if half == 1:
                @pl.when(tok + 2 == per)
                def _():
                    put_unit(2 * f)
                    put_unit(2 * f + 1)
            rolling_tick(i, half)
        return carry

    lax.fori_loop(0, feeds * per // 2, feed_pair, 0)
    clock[0] = 2.0 * (feeds * per - 1 - early)
    for u in range(2 * feeds):
        stages = [s for s in range(STAGES) if 4.0 * u + 2.0 * SLOW[s] > clock[0]]
        due[u] = (stages[0], 4.0 * u + 2.0 * SLOW[stages[0]])

    def decays(j):
        slot = j % 2
        return pltpu.make_async_copy(decay_in.at[:, pl.ds(j * wide, wide)], decay_s.at[slot], stream_sems.at[0, slot])

    decays(0).start()
    decays(1).start()

    streams = ((fade_s, fade_in), (rise_s, rise_in), (weight_s, weight_in), (lean_s, lean_in))
    depth = blocks // 2

    def streamed(k, half, i):
        if half == 0:
            return streams[k][0].at[i]
        each = inner // (len(streams) * wide)
        row, column = lax.div(i, each) * size, (lax.rem(i, each) * len(streams) + k) * wide
        return w_up_v.at[pl.ds(pl.multiple_of(row, size), size), pl.ds(pl.multiple_of(column, wide), wide)]

    def stream(j, half, i):
        b = blocks - 1 - half * depth - i
        return [
            pltpu.make_async_copy(source.at[at_block(b), pl.ds(j * wide, wide)], streamed(k, half, i), stream_sems.at[1 + k, half * depth + i])
            for k, (buffer, source) in enumerate(streams)
        ]

    for half in range(2):
        for i in range(depth):
            for copy in stream(0, half, i):
                copy.start()

    def stage_copy(buffer, target, b):
        slot = lax.rem(b, 2)
        return pltpu.make_async_copy(buffer.at[slot], target.at[:, pl.ds(pl.multiple_of(b * block, block), block), :], stage_sems.at[slot])

    def finish_two(b, norm_sum, cot_sum):
        at = at_block(b)

        @pl.when(b >= 2)
        def _():
            stage_copy(mixed_s, mixed_out, b - 2).wait()
        mixed = jnp.swapaxes(mixed_v[at].reshape(block, rows, width), 0, 1)
        mixed_s[lax.rem(b, 2)] = mixed.astype(BF16)
        stage_copy(mixed_s, mixed_out, b).start()
        value, grad, cot = middle_v[at], second_v[at], cot_v[at].astype(F32)
        scale = lax.rsqrt(jnp.mean(value * value, axis=-1, keepdims=True) + EPS)
        plain = value * scale
        norm_sum = norm_sum + jnp.sum((grad * plain).reshape(size // 8, 8, width), axis=0)
        cot_sum = cot_sum + jnp.sum(cot.reshape(size // 8, 8, width), axis=0)
        lean = grad * gains
        back = cot + scale * (lean - plain * jnp.mean(lean * plain, axis=-1, keepdims=True))
        second_v[at] = back
        low_v[at] = back.astype(BF16)
        return norm_sum, cot_sum

    zero = jnp.zeros((8, width), F32)
    norm_sum, cot_sum = beat(blocks, finish_two, 2, 2.4, zero, zero)
    for b in (blocks - 2, blocks - 1):
        stage_copy(mixed_s, mixed_out, b).wait()
    put_small(20, jnp.sum(norm_sum, axis=0, keepdims=True))
    put_small(24, sums_v[0:1])
    put_small(40, jnp.sum(cot_sum, axis=0, keepdims=True))

    loads[4].wait()
    loads[5].wait()

    def half_of(refs, j):
        return refs[j // 2], slice(UNIT * (j % 2), UNIT * (j % 2) + UNIT)

    def back_states():
        def one(tok, carry):
            at = at_block(tok, big)
            back = dot_nt(low_v[at], w_out_v[...])
            mixed_v[at] = back[:, :SPAN]
            middle_v[at] = back[:, SPAN:]
            return carry

        lax.fori_loop(0, per, one, 0)
        tick(2.0)

    def first_pass(j):
        flows, lanes = half_of((mixed_v, middle_v), j)
        decays(j).wait()

        def one(i, carry):
            product, flow = carry
            b = blocks - 1 - i
            for t in reversed(range(block)):
                there = pl.ds(pl.multiple_of(b * size + t * rows, rows), rows)
                decay = decay_s[j % 2, there]
                flow = decay * (flows[there, lanes] + flow)
                product = decay * product
            return product, flow

        product, flow = lax.fori_loop(0, blocks, one, (jnp.ones((rows, wide), F32), jnp.zeros((rows, wide), F32)))
        chain.start(j, product, flow)
        decays((j + 2) % parts).start()
        tick(0.6)

    def grad_out():
        for j in range(hidden // SPAN):
            def one(tok, carry):
                at = at_block(tok, big)
                gather(2 * feeds + j, dot_tn(state_v[at, pl.ds(j * SPAN, SPAN)], low_v[at]), tok == 0)
                return carry

            lax.fori_loop(0, per, one, 0)
            put_unit(2 * feeds + j)
            enter(2 * feeds + j)
            tick(2.0)

    gains_one = gain_one[...]

    def norm_one(b):
        at = at_block(b)
        value = x_v[at].astype(F32)
        scale = lax.rsqrt(jnp.mean(value * value, axis=-1, keepdims=True) + EPS)
        turned_v[:, at] = jnp.swapaxes(value * scale * gains_one, 0, 1).astype(BF16)
        return ()

    back_states()
    work = [functools.partial(first_pass, j) for j in range(parts)]
    work += [grad_out]

    def turn():
        loads[6].wait()
        beat(blocks, norm_one, 1, 1.6)

    work.append(turn)
    for step in range(max(len(work), parts + chain.rounds)):
        if step < len(work):
            work[step]()
        else:
            tick(1.0)
        for i in range(parts):
            if 0 <= step - 1 - i < chain.rounds:
                chain.advance(i, step - 1 - i)

    cand_refs = (low_v, cand_v)
    input_refs = (cot_v, w_down_v)

    def second_pass(j):
        flows, lanes = half_of((mixed_v, middle_v), j)
        to_input, to_cand = half_of(input_refs, j)[0], half_of(cand_refs, j)[0]
        decays(j).wait()

        def one(half, i, carry):
            flow, sum_f, sum_i = carry
            b = blocks - 1 - half * depth - i
            for copy in stream(j, half, i):
                copy.wait()
            fade, rise, weight, lean_part = (streamed(k, half, i) for k in range(len(streams)))
            for t in reversed(range(block)):
                here = pl.ds(t * rows, rows)
                there = pl.ds(pl.multiple_of(b * size + t * rows, rows), rows)
                reach = flows[there, lanes] + flow
                flow = decay_s[j % 2, there] * reach
                lean = reach * lean_part[here].astype(F32)
                grad_f = fade[here].astype(F32) * lean
                grad_i = -(rise[here].astype(F32) * lean)
                sum_f, sum_i = sum_f + grad_f, sum_i + grad_i
                state_v[there, wide * j : wide * j + wide] = grad_f.astype(BF16)
                to_input[there, lanes] = grad_i.astype(BF16)
                to_cand[there, lanes] = (weight[here].astype(F32) * reach).astype(BF16)
            if j + 1 < parts:
                for copy in stream(j + 1, half, i):
                    copy.start()
            return flow, sum_f, sum_i

        none = jnp.zeros((rows, wide), F32)
        carry = (join[j, 1], none, none)
        for half in range(2):
            carry = lax.fori_loop(0, depth, functools.partial(one, half), carry)
        unused, sum_f, sum_i = carry
        tick(1.2)
        if j + 2 < parts:
            decays(j + 2).start()
        put_small(4 + 2 * j, jnp.sum(sum_f, axis=0, keepdims=True))
        put_small(12 + 2 * j, jnp.sum(sum_i, axis=0, keepdims=True))

    def grad_in(j):
        unit = 2 * feeds + hidden // SPAN + 3 * j

        lanes = half_of(input_refs, j)[1]
        pieces = ((state_v, slice(wide * j, wide * j + wide)), (half_of(input_refs, j)[0], lanes), (half_of(cand_refs, j)[0], lanes))
        over = [u for u in range(2 * feeds + hidden // SPAN) if plan[u][0] in {plan[unit + k][0] for k in range(3)} and u not in settled]
        settled.update(over)
        assert all(due[u][0] > 7 for u in over)
        if ringed and over:
            ring.settle_sums(over)
        for k, (ref, columns) in enumerate(pieces):
            slot, column, length = plan[unit + k]
            grads[slot, :, pl.ds(column, length)] = dot(turned_v[...], ref[:, columns])
            put_unit(unit + k)
            enter(unit + k)
            tick(0.5)

    settled = set()
    for j in range(parts):
        second_pass(j)
        if j == parts - 1:
            loads[8].start()
        grad_in(j)

    for k in (7, 8):
        loads[k].wait()
    project_refs = [(state_v, slice(0, hidden), w_up_v, 0)]
    for k, refs in enumerate((input_refs, cand_refs)):
        for half in range(2):
            column = (k + 1) * hidden + half * SPAN
            wide_ref, column = (w_up_v, column) if column < inner else (w_in_v, column - inner)
            project_refs.append((refs[half], slice(None), wide_ref, column))

    def finish_one(tok, norm_sum):
        at = at_block(tok, big)
        grad_all = jnp.zeros((big, width), F32)
        for ref, columns, weight, column in project_refs:
            piece = ref[at, columns]
            grad_all = grad_all + dot_nt(piece, weight[:, column : column + piece.shape[1]])
        for k in range(big // size):
            b = tok * (big // size) + k

            @pl.when(b >= 2)
            def _():
                stage_copy(tokens_s, tokens_out, b - 2).wait()
            here = at_block(b)
            grad = grad_all[k * size : k * size + size]
            value = x_v[here].astype(F32)
            scale = lax.rsqrt(jnp.mean(value * value, axis=-1, keepdims=True) + EPS)
            plain = value * scale
            norm_sum = norm_sum + jnp.sum((grad * plain).reshape(size // 8, 8, width), axis=0)
            lean = grad * gains_one
            back = second_v[here] + scale * (lean - plain * jnp.mean(lean * plain, axis=-1, keepdims=True))
            tokens_s[lax.rem(b, 2)] = jnp.swapaxes(back.reshape(block, rows, width), 0, 1)
            stage_copy(tokens_s, tokens_out, b).start()
        return (norm_sum,)

    (norm_sum,) = beat(per, finish_one, 4, 9.0, jnp.zeros((8, width), F32))
    put_small(0, jnp.sum(norm_sum, axis=0, keepdims=True))
    if ringed:
        step = 0
        while step <= DOUBLINGS or any(due[unit][0] < STAGES for unit in due):
            tick(1.0)
            if step <= DOUBLINGS:
                small.step(step)
            step += 1
        ring.settle_sums([u for u in due if u not in settled])
        ring.settle_lines(list(due))
        copy = pltpu.make_async_copy(own_v.at[DOUBLINGS], small_out.at[0], load_sems.at[0])
    else:
        copy = pltpu.make_async_copy(small_v, small_out.at[0], load_sems.at[0])
    copy.start()
    copy.wait()
    for b in (blocks - 2, blocks - 1):
        stage_copy(tokens_s, tokens_out, b).wait()
    for j in range(parts):
        chain.finish(j)


def back(ringed, shape_in, x, cot, middle, state, decay, fade, rise, weight, lean, gain_one, gain_two, up_bias, down_bias, w_in, w_out, w_up, w_down, cid=2):
    rows, steps, width = shape_in
    total = rows * steps
    hidden = w_out.shape[0]
    inner = w_down.shape[0]
    count = lax.axis_size("seq")
    block = 16
    size = block * rows
    wide = UNIT
    parts = hidden // wide
    feeds = inner // SPAN
    whole = 2 * feeds + hidden // SPAN
    plan = [(u, 0, WIDE) for u in range(whole)]
    for k in range(3 * parts):
        plan.append(((whole + k // 2) % SLOTS, k % 2 * UNIT, UNIT))
    units = len(plan)
    anywhere = pl.BlockSpec(memory_space=pl.ANY)
    vmem = pl.BlockSpec(memory_space=pltpu.VMEM)
    shape = jax.ShapeDtypeStruct
    if ringed:
        first, *others = sum_scratch(units, whole, SLOTS)
        more = [first, pltpu.VMEM((DOUBLINGS + 1, SMALL_ROWS, 128), F32), *others]
        more += [pltpu.VMEM((DOUBLINGS, SMALL_ROWS, 128), F32)] + [pltpu.SemaphoreType.DMA((DOUBLINGS,))] * 2
    else:
        more = [pltpu.VMEM((SLOTS, SPAN, WIDE), F32), pltpu.VMEM((1, SMALL_ROWS, 128), F32)]
    return pl.pallas_call(
        functools.partial(back_kernel, ringed, count, rows, steps, plan, block),
        out_shape=(
            shape(shape_in, BF16), shape(shape_in, F32), shape((units, SPAN, WIDE), F32), shape((1, SMALL_ROWS, 128), F32),
        ),
        in_specs=[anywhere] * 9 + [vmem] * 4 + [anywhere] * 4,
        out_specs=(anywhere,) * 4,
        scratch_shapes=[
            pltpu.VMEM((total, width), F32), pltpu.VMEM((total, width), F32), pltpu.VMEM((total, width), F32),
            pltpu.VMEM((total, hidden), BF16), pltpu.VMEM((total, width), BF16), pltpu.VMEM((total, width), BF16), pltpu.VMEM((total, width), BF16),
            pltpu.VMEM((total, width), BF16), pltpu.VMEM((width, total), BF16),
            pltpu.VMEM((width, w_in.shape[1] - inner), BF16), pltpu.VMEM(w_out.shape, BF16), pltpu.VMEM(w_up.shape, BF16), pltpu.VMEM(w_down.shape, BF16),
            pltpu.VMEM((2, total, wide), F32), pltpu.VMEM((4, size, wide), BF16), pltpu.VMEM((4, size, wide), BF16),
            pltpu.VMEM((4, size, wide), BF16), pltpu.VMEM((4, size, wide), BF16),
            pltpu.VMEM((2, rows, block, width), BF16), pltpu.VMEM((2, rows, block, width), F32), pltpu.VMEM((8, inner), F32),
            pltpu.SemaphoreType.DMA((9,)), pltpu.SemaphoreType.DMA((5, 8)), pltpu.SemaphoreType.DMA((2,)),
            *chain_scratch(parts, count, rows, wide),
            *more,
        ],
        compiler_params=pltpu.CompilerParams(collective_id=cid, has_side_effects=True, vmem_limit_bytes=63 * 2**20 + 2**19),
        cost_estimate=pl.CostEstimate(flops=2 * total * width * (8 * hidden + 6 * inner), bytes_accessed=80 * 2**20, transcendentals=total * inner),
        name="back",
    )(x, cot, middle, state, decay, fade, rise, weight, lean, gain_one.reshape(1, -1), gain_two.reshape(1, -1), up_bias.reshape(1, -1), down_bias.reshape(1, -1), w_in, w_out, w_up, w_down)


def settle_kernel(places, mixed, tokens, units, small, *refs):
    outs, (mixed_v, tokens_v, units_v, reads, writes) = refs[:-5], refs[-5:]
    copies = []
    for k in range(mixed.shape[0] // 4):
        some = pl.ds(4 * k, 4)
        copies.append((tokens.at[some], tokens_v.at[some], outs[1].at[some]))
        copies.append((mixed.at[some], mixed_v.at[some], outs[0].at[some]))
    for u, length, array, row, column in places:
        lanes = pl.ds(0, length)
        copies.append((units.at[u, :, lanes], units_v.at[u, :, lanes], outs[2 + array].at[pl.ds(row, SPAN), pl.ds(column, length)]))
    moves = [
        (pltpu.make_async_copy(a, b, reads.at[k]), pltpu.make_async_copy(b, c, writes.at[k])) for k, (a, b, c) in enumerate(copies)
    ]
    for read, write in moves:
        read.start()
    row = 0
    for out in outs[6:]:
        out[...] = small[0, pl.ds(row, out.shape[0])]
        row += out.shape[0]
    for read, write in moves:
        read.wait()
        write.start()
    for read, write in moves:
        write.wait()


def settle(mixed, tokens, units, small, hidden, inner):
    width = tokens.shape[-1]
    parts = hidden // UNIT
    feeds = inner // SPAN
    places = []
    for f in range(feeds):
        places += [(2 * f, SPAN, 3, f * SPAN, 0), (2 * f + 1, SPAN, 2, 0, f * SPAN)]
    places += [(2 * feeds + j, SPAN, 1, j * SPAN, 0) for j in range(hidden // SPAN)]
    for j in range(parts):
        places += [(len(places) + k, UNIT, 0, 0, k * hidden + j * UNIT) for k in range(3)]
    anywhere = pl.BlockSpec(memory_space=pl.ANY)
    vmem = pl.BlockSpec(memory_space=pltpu.VMEM)
    shape = jax.ShapeDtypeStruct
    lengths = (width, hidden, hidden, width, inner, width)
    return pl.pallas_call(
        functools.partial(settle_kernel, places),
        out_shape=(
            shape(mixed.shape, mixed.dtype), shape(tokens.shape, F32), shape((width, 3 * hidden), F32), shape((hidden, width), F32),
            shape((width, inner), F32), shape((inner, width), F32), *(shape((n // 128, 128), F32) for n in lengths),
        ),
        in_specs=[anywhere] * 3 + [vmem],
        out_specs=(anywhere,) * 6 + (vmem,) * 6,
        scratch_shapes=[
            pltpu.VMEM(mixed.shape, mixed.dtype), pltpu.VMEM(tokens.shape, F32), pltpu.VMEM(units.shape, F32),
            pltpu.SemaphoreType.DMA((mixed.shape[0] // 2 + len(places),)), pltpu.SemaphoreType.DMA((mixed.shape[0] // 2 + len(places),)),
        ],
        compiler_params=pltpu.CompilerParams(vmem_limit_bytes=63 * 2**20),
        name="settle",
    )(mixed, tokens, units, small)


def on_device(tokens, cotangent, reset_pos, norm1_gain, w_in, forget_bias, input_bias, w_out, norm2_gain, w_up, up_bias, w_down, down_bias):
    ringed = lax.axis_size("seq") == 8 and lax.axis_size("rows") == 4
    hidden, inner = w_out.shape[0], w_down.shape[0]
    kept = front(tokens, cotangent, reset_pos, norm1_gain, w_in, forget_bias, input_bias, w_out)
    mixed, grad_tokens, units, small = back(
        ringed, tokens.shape, *kept, norm1_gain, norm2_gain, up_bias, down_bias, w_in, w_out, w_up, w_down
    )
    if not ringed:
        units, small = lax.psum((units, small), ("seq", "rows"))
    mixed, grad_tokens, grad_in, grad_out, grad_up, grad_down, *rest = settle(mixed, grad_tokens, units, small, hidden, inner)
    norm_one, forget, inputs, norm_two, up, down = (one.reshape(-1) for one in rest)
    return mixed, grad_tokens, norm_one, grad_in, forget, inputs, grad_out, norm_two, grad_up, up, grad_down, down


def solution(mesh):
    return jax.shard_map(
        on_device,
        mesh=mesh,
        in_specs=(
            P("rows", "seq", None),
            P("rows", "seq", None),
            P("rows", None),
            P(),
            P(),
            P(),
            P(),
            P(),
            P(),
            P(),
            P(),
            P(),
            P(),
        ),
        out_specs=(
            P("rows", "seq", None),
            P("rows", "seq", None),
            P(),
            P(),
            P(),
            P(),
            P(),
            P(),
            P(),
            P(),
            P(),
            P(),
        ),
        check_vma=False,
    )
```
